32 devices in a mesh: exp: 8 (over z, x), hid: 4 (over y, core).
Axes of the slice: x: 2, y: 2, z: 4, core: 2. Of those that a mesh axis runs over, the one named last changes fastest.
Arguments:
- tokens: bfloat16 [8192, 1024], P('exp'), may hold values from -6 to 6
- segment_ids: int32 [8, 1024], P('exp'), may hold values from 0 to 3, never falling along the last dimension, each value on 1 to 682 neighbouring positions
- routes: int32 [8192, 8], P('exp'), may hold values from 0 to 31, all different within a row
- norm1_gain: float32 [1024], P('exp'), may hold values from 0.5 to 1.5
- norm2_gain: float32 [1024], P('exp'), may hold values from 0.5 to 1.5
- query_weight: float32 [1024, 1024], P('exp', 'hid'), may hold values from -0.1875 to 0.1875
- key_matrix: float32 [1024, 512], P('exp', 'hid'), may hold values from -0.1875 to 0.1875
- value_matrix: float32 [1024, 512], P('exp', 'hid'), may hold values from -0.1875 to 0.1875
- out_weight: float32 [1024, 1024], P('exp', 'hid'), may hold values from -0.75 to 0.75
- router_weight: float32 [1024, 32], P('exp'), may hold values from -0.09375 to 0.09375
- gate_weight: float32 [32, 1024, 512], P('exp', None, 'hid'), may hold values from -0.1875 to 0.1875
- up_weight: float32 [32, 1024, 512], P('exp', None, 'hid'), may hold values from -0.1875 to 0.1875
- down_weight: float32 [32, 512, 1024], P('exp', 'hid'), may hold values from -1 to 1
- out_grad: bfloat16 [8192, 1024], P('exp', 'hid'), may hold values from -6 to 6
Outputs:
- layer_out: bfloat16 [8192, 1024], P('exp', 'hid')
- input_grad: float32 [8192, 1024], P('exp')
- norm1_gain_grad: float32 [1024], P('exp')
- norm2_gain_grad: float32 [1024], P('exp')
- query_weight_grad: float32 [1024, 1024], P('exp', 'hid')
- key_weight_grad: float32 [1024, 512], P('exp', 'hid')
- value_weight_grad: float32 [1024, 512], P('exp', 'hid')
- out_weight_grad: float32 [1024, 1024], P('exp', 'hid')
- router_weight_grad: float32 [1024, 32], P('exp')
- gate_weight_grad: float32 [32, 1024, 512], P('exp', None, 'hid')
- up_weight_grad: float32 [32, 1024, 512], P('exp', None, 'hid')
- down_weight_grad: float32 [32, 512, 1024], P('exp', 'hid')
The draws below stay inside these ranges and needn't reach their ends.
Inputs may be any that keep to these rules, and one draw needn't show every extreme that they name: `routes`: each token names 8 different experts. `segment_ids`: within a row ids never fall; a document has at most 682 tokens and one has exactly that many.
All inputs are finite; a program needn't handle non-finite values.
Results may differ from the reference program's by a relative error of at most 0.023.
Values may be sent and summed in bfloat16 or wider, within the bound.
A program may use at most 384 MiB of HBM per device.

```python
import math
import jax
import jax.numpy as jnp
import numpy as np
from jax import lax

MODEL_DIM = 1024
FF = 512
QUERY_HEADS_COUNT = 16
KEY_VALUE_HEADS = 8
HEAD_DIM = 64
EXPERTS = 32
TOPK = 8
TOK_DEV = 1024
SEGS = 4
CAP = 320
ROWS = 8
TOKENS = 8192


def shard_levels(rng, extent, shards, low, top_value):
    loudness, own = 1.0, jax.random.fold_in(rng, 6)
    for axis_at, blocks in shards:
        heights = jnp.exp(jax.random.uniform(jax.random.fold_in(own, axis_at), (blocks,), jnp.float32, low / len(shards), top_value / len(shards)))
        loudness = loudness * jnp.repeat(heights, extent[axis_at] // blocks).reshape([-1 if axis == axis_at else 1 for axis in range(len(extent))])
    return loudness


def different_ones(stream_key, rows, amount, top, lift):
    sequence = jax.random.permutation(jax.random.fold_in(stream_key, 1), amount)
    pull = sequence
    for power in range(3):
        pull = pull * pull // amount
    pull = pull * lift // amount
    lots = jax.random.randint(jax.random.fold_in(stream_key, 2), (rows, amount), 0, 4096) + pull
    sure = jax.random.permutation(jax.random.fold_in(stream_key, 3), rows)[jnp.arange(amount) % rows]
    lots = jnp.where(jnp.arange(rows)[:, None] == sure[None, :], 1 << 14, lots)
    priority = lots * amount + jnp.arange(amount)
    return lax.top_k(priority.astype(jnp.int32), top)[1].astype(jnp.int32)


def profile(amount, total, bound, lean):
    weights = [(1 << 20) // math.isqrt(standing ** lean) + 1 for standing in range(2, amount + 1)]
    rest, given = total - bound - (amount - 1), [1] * (amount - 1)
    while rest > 0:
        movable = [i for i in range(amount - 1) if given[i] < bound]
        whole, remaining = sum([weights[i] for i in movable]), rest
        for i in movable:
            extra = min(bound - given[i], max(1, remaining * weights[i] // whole), rest)
            given[i] = given[i] + extra
            rest = rest - extra
    return np.array([bound] + given)


def uneven_parts(own_key, number_of, total, limit, lean):
    if number_of == 2:
        one = jax.random.randint(own_key, (), max(1, total - limit), min(limit, total - 1) + 1)
        return jnp.stack([one, total - one])
    tallies = jnp.asarray(profile(number_of, total, limit, lean), jnp.int32)
    twos = (number_of - 1) // 2
    donor, receiver = tallies[1:1 + 2 * twos:2], tallies[2:2 + 2 * twos:2]
    room = jnp.minimum(donor - 1, limit - receiver)
    shifted = jax.random.randint(jax.random.fold_in(own_key, 1), (twos,), 0, 1 << 20) % (room + 1)
    tallies = tallies.at[1:1 + 2 * twos:2].set(donor - shifted).at[2:2 + 2 * twos:2].set(receiver + shifted)
    return tallies[jax.random.permutation(jax.random.fold_in(own_key, 2), number_of)]


def scatter_about(own_key, extent, width, bound, split=(), held_as=jnp.bfloat16):
    loudness = shard_levels(own_key, extent, split, -0.22, 0.18) if split else 1.0
    drawn = jax.random.normal(own_key, extent, jnp.float32) * width * loudness
    return jnp.minimum(jnp.maximum(drawn, -bound), bound).astype(held_as)


def setup_inputs(seed: int = 0) -> dict:
    streams_of = jax.random.split(jax.random.key(seed), 15)
    tokens = scatter_about(streams_of[0], (TOKENS, MODEL_DIM), 1.0, 6.0, ((0, 8),))
    segment_ids = jax.vmap(lambda own: jnp.searchsorted(jnp.cumsum(uneven_parts(own, SEGS, TOK_DEV, TOK_DEV * 2 // 3, 2)), jnp.arange(TOK_DEV), side="right"))(jax.random.split(streams_of[1], ROWS)).reshape((ROWS, TOK_DEV)).astype(jnp.int32)
    routes = different_ones(streams_of[2], TOKENS, EXPERTS, TOPK, 2048)
    norm1_gain = jnp.clip(1.0 + 0.1 * jax.random.normal(streams_of[3], (MODEL_DIM,), jnp.float32), 0.5, 1.5)
    norm2_gain = jnp.clip(1.0 + 0.1 * jax.random.normal(streams_of[4], (MODEL_DIM,), jnp.float32), 0.5, 1.5)
    query_weight = scatter_about(streams_of[5], (MODEL_DIM, QUERY_HEADS_COUNT * HEAD_DIM), MODEL_DIM ** -0.5, 0.1875, ((0, 8), (1, 4)), jnp.float32)
    key_matrix = scatter_about(streams_of[6], (MODEL_DIM, KEY_VALUE_HEADS * HEAD_DIM), MODEL_DIM ** -0.5, 0.1875, ((0, 8), (1, 4)), jnp.float32)
    value_matrix = scatter_about(streams_of[7], (MODEL_DIM, KEY_VALUE_HEADS * HEAD_DIM), MODEL_DIM ** -0.5, 0.1875, ((0, 8), (1, 4)), jnp.float32)
    out_weight = scatter_about(streams_of[8], (MODEL_DIM, QUERY_HEADS_COUNT * HEAD_DIM), (QUERY_HEADS_COUNT * HEAD_DIM // 16) ** -0.5, 0.75, ((0, 8), (1, 4)), jnp.float32)
    router_weight = scatter_about(streams_of[9], (MODEL_DIM, EXPERTS), (4 * MODEL_DIM) ** -0.5, 0.09375, ((0, 8),), jnp.float32)
    gate_weight = scatter_about(streams_of[10], (EXPERTS, MODEL_DIM, FF), MODEL_DIM ** -0.5, 0.1875, ((0, 8), (2, 4)), jnp.float32)
    up_weight = scatter_about(streams_of[11], (EXPERTS, MODEL_DIM, FF), MODEL_DIM ** -0.5, 0.1875, ((0, 8), (2, 4)), jnp.float32)
    down_weight = scatter_about(streams_of[12], (EXPERTS, FF, MODEL_DIM), (FF // 16) ** -0.5, 1.0, ((0, 8), (1, 4)), jnp.float32)
    out_grad = scatter_about(streams_of[13], (TOKENS, MODEL_DIM), 1.0, 6.0, ((0, 8), (1, 4)))
    return {"tokens": tokens, "segment_ids": segment_ids, "routes": routes, "norm1_gain": norm1_gain, "norm2_gain": norm2_gain, "query_weight": query_weight, "key_matrix": key_matrix, "value_matrix": value_matrix, "out_weight": out_weight, "router_weight": router_weight, "gate_weight": gate_weight, "up_weight": up_weight, "down_weight": down_weight, "out_grad": out_grad}


@jax.custom_vjp
def low(v):
    return lax.optimization_barrier(v.astype(jnp.bfloat16)).astype(jnp.float32)

@jax.custom_vjp
def low_back(v):
    return v

def low_keep(v):
    return (low(v), None)

def low_pass(kept, grad):
    return (grad,)

def back_keep(v):
    return (v, None)

def back_low(kept, grad):
    return (low(grad),)
low.defvjp(low_keep, low_pass)
low_back.defvjp(back_keep, back_low)
EPSILON = 1e-05
ROPE_BASE = 10000.0
NEG_FILL = -1e+30
FULL_PRECISION = lax.Precision.HIGHEST

def rms_scale(values_in):
    return lax.rsqrt(lax.optimization_barrier(jnp.mean(values_in * values_in, axis=-1, keepdims=True)) + EPSILON)

def positions_of(segments, seg_count):
    same = segments[:, None] == jnp.arange(seg_count, dtype=jnp.int32)[None, :]
    counts = lax.optimization_barrier(jnp.sum(same.astype(jnp.int32), axis=0))
    starts = jnp.cumsum(counts) - counts
    begin = lax.optimization_barrier(jnp.sum(jnp.where(same, starts[None, :], 0), axis=1))
    return (jnp.arange(segments.shape[0], dtype=jnp.int32) - begin).astype(jnp.int32)

def rope_tables(positions, head_size):
    half = head_size // 2
    freqs = ROPE_BASE ** (-(jnp.arange(half, dtype=jnp.float32) * 2.0 / head_size))
    angles = positions.astype(jnp.float32)[:, None] * freqs[None, :]
    return (jnp.cos(angles)[:, None, :], jnp.sin(angles)[:, None, :])

def rotate(values_in, cosine, sine):
    half = values_in.shape[-1] // 2
    first = values_in[..., :half]
    second = values_in[..., half:]
    return jnp.concatenate([first * cosine - second * sine, second * cosine + first * sine], axis=-1)

def slot_tables(row_routes, expert_count, capacity):
    token_count = row_routes.shape[0]
    chosen = row_routes[:, :, None] == jnp.arange(expert_count, dtype=jnp.int32)[None, None, :]
    chosen_int = chosen.astype(jnp.int32)
    per_token = lax.optimization_barrier(jnp.sum(chosen_int, axis=1))
    before = jnp.cumsum(per_token, axis=0) - per_token
    rank = lax.optimization_barrier(jnp.sum(chosen_int * before[:, None, :], axis=2))
    pair_slot = jnp.where(rank < capacity, row_routes * capacity + rank, expert_count * capacity).astype(jnp.int32)
    owners = jnp.broadcast_to(jnp.arange(token_count, dtype=jnp.int32)[:, None], row_routes.shape)
    source = jnp.full((expert_count * capacity + 1,), token_count, jnp.int32)
    source = source.at[pair_slot.reshape(-1)].set(owners.reshape(-1))
    return (chosen, pair_slot, source[:expert_count * capacity])

def attend(normed_input, w_query, key_projection_weight, value_projection_weight, w_out, positions, segments):
    token_count = normed_input.shape[0]
    cosine, sine = rope_tables(positions, HEAD_DIM)
    query_rows = jnp.dot(normed_input, w_query, precision=FULL_PRECISION).reshape(token_count, QUERY_HEADS_COUNT, HEAD_DIM)
    key_rows = jnp.dot(normed_input, key_projection_weight, precision=FULL_PRECISION).reshape(token_count, KEY_VALUE_HEADS, HEAD_DIM)
    value_rows = jnp.dot(normed_input, value_projection_weight, precision=FULL_PRECISION).reshape(token_count, KEY_VALUE_HEADS, HEAD_DIM)
    query_rows = low(rotate(low_back(query_rows), cosine, sine))
    key_rows = low(rotate(low_back(key_rows), cosine, sine))
    value_rows = low(low_back(value_rows))
    grouped_heads = query_rows.reshape(token_count, KEY_VALUE_HEADS, QUERY_HEADS_COUNT // KEY_VALUE_HEADS, HEAD_DIM)
    scores = low_back(jnp.einsum('qkgd,skd->kgqs', grouped_heads, key_rows, precision=FULL_PRECISION) * HEAD_DIM ** (-0.5))
    index_row = jnp.arange(token_count, dtype=jnp.int32)
    allowed = (segments[:, None] == segments[None, :]) & (index_row[:, None] >= index_row[None, :])
    scores = jnp.where(allowed[None, None], scores, NEG_FILL)
    peak = lax.optimization_barrier(jnp.max(scores, axis=-1, keepdims=True))
    powers = jnp.exp(scores - peak)
    probs = low(powers / lax.optimization_barrier(jnp.sum(powers, axis=-1, keepdims=True)))
    mixed = jnp.einsum('kgqs,skd->qkgd', probs, value_rows, precision=FULL_PRECISION).reshape(token_count, QUERY_HEADS_COUNT * HEAD_DIM)
    mixed = low(low_back(mixed))
    return low_back(jnp.dot(mixed, w_out.T, precision=FULL_PRECISION))

def row_forward(inputs, segments, row_routes, params):
    gain_one, gain_two, w_query, key_projection_weight, value_projection_weight, w_out, w_router, w_gate, w_up, w_down = params
    positions = positions_of(segments, SEGS)
    normed_one = low(inputs * rms_scale(inputs) * gain_one[None, :])
    resid = inputs + attend(normed_one, w_query, key_projection_weight, value_projection_weight, w_out, positions, segments)
    normed_two = low(resid * rms_scale(resid) * gain_two[None, :])
    chosen, pair_slot, source = slot_tables(row_routes, EXPERTS, CAP)
    chosen_f = chosen.astype(jnp.float32)
    logits = low_back(jnp.dot(normed_two, w_router, precision=FULL_PRECISION))
    picked = lax.optimization_barrier(jnp.sum(chosen_f * logits[:, None, :], axis=2))
    peak = lax.optimization_barrier(jnp.max(picked, axis=1, keepdims=True))
    powers = jnp.exp(picked - peak)
    gates = powers / lax.optimization_barrier(jnp.sum(powers, axis=1, keepdims=True))
    padded = jnp.concatenate([normed_two, jnp.zeros((1, MODEL_DIM), jnp.float32)], axis=0)
    slots = low_back(padded[source].reshape(EXPERTS, CAP, MODEL_DIM))
    gate_pre = low_back(jnp.einsum('ecd,edf->ecf', slots, w_gate, precision=FULL_PRECISION))
    up_pre = low_back(jnp.einsum('ecd,edf->ecf', slots, w_up, precision=FULL_PRECISION))
    hidden = low(jax.nn.silu(gate_pre) * up_pre)
    expert_out = low(low_back(jnp.einsum('ecf,efd->ecd', hidden, w_down, precision=FULL_PRECISION)))
    flat_out = jnp.concatenate([expert_out.reshape(EXPERTS * CAP, MODEL_DIM), jnp.zeros((1, MODEL_DIM), jnp.float32)], axis=0)
    paired = flat_out[pair_slot]
    combined = lax.optimization_barrier(jnp.sum(gates[:, :, None] * paired, axis=1))
    return resid + combined

def reference(tokens, segment_ids, routes, norm1_gain, norm2_gain, query_weight, key_matrix, value_matrix, out_weight, router_weight, gate_weight, up_weight, down_weight, out_grad):
    row_count = segment_ids.shape[0]
    x_rows = tokens.astype(jnp.float32).reshape(row_count, TOK_DEV, MODEL_DIM)
    route_rows = routes.reshape(row_count, TOK_DEV, TOPK)

    def forward(x_all, g_one, g_two, w_query, key_projection_weight, value_projection_weight, w_out, w_router, w_gate, w_up, w_down):
        params = (low(g_one), low(g_two), low(w_query), low(key_projection_weight), low(value_projection_weight), low(w_out), low(w_router), low(w_gate), low(w_up), low(w_down))

        def one_row(packed):
            return row_forward(packed[0], packed[1], packed[2], params)
        return lax.map(jax.checkpoint(one_row), (x_all, segment_ids, route_rows))
    result, pullback = jax.vjp(forward, x_rows, norm1_gain, norm2_gain, query_weight, key_matrix, value_matrix, out_weight, router_weight, gate_weight, up_weight, down_weight)
    grads = pullback(out_grad.astype(jnp.float32).reshape(row_count, TOK_DEV, MODEL_DIM))
    layer_out = result.reshape(row_count * TOK_DEV, MODEL_DIM).astype(jnp.bfloat16)
    input_grad = grads[0].reshape(row_count * TOK_DEV, MODEL_DIM)
    return (layer_out, input_grad, grads[1], grads[2], grads[3], grads[4], grads[5], grads[6], grads[7], grads[8], grads[9], grads[10])
```

```python
import functools

import jax
import jax.numpy as jnp
from jax import lax
from jax.experimental import pallas as pl
from jax.experimental.pallas import tpu as pltpu
from jax.sharding import PartitionSpec as P

HEAD_DIM = 64
SEGS = 4
EPSILON = 1e-05
ROPE_BASE = 10000.0
NEG_FILL = -1e30
LANES = 128
MESH = pl.DeviceIdType.MESH
F32 = jnp.float32
BF16 = jnp.bfloat16
VMEM_LIMIT = 60 * 2**20
SMALL_VMEM = 30 * 2**20


def nn(a, b):
    return lax.dot_general(a, b, (((1,), (0,)), ((), ())), preferred_element_type=F32)


def nt(a, b):
    return lax.dot_general(a, b, (((1,), (1,)), ((), ())), preferred_element_type=F32)


def tn(a, b):
    return lax.dot_general(a, b, (((0,), (0,)), ((), ())), preferred_element_type=F32)


def tn_exact(a, b):
    return lax.dot_general(
        a, b, (((0,), (0,)), ((), ())), preferred_element_type=F32, precision=lax.Precision.HIGHEST
    )


def iota(shape, dim):
    return lax.broadcasted_iota(jnp.int32, shape, dim)


def rows_at(index, size):
    return pl.ds(pl.multiple_of(index * size, size), size)


def pos_of(index, n):
    odd = index % 2
    return (1 - odd) * (index // 2) + odd * (n - 1 - index // 2)


def at_pos(pos, n):
    back = pos // (n // 2)
    return (1 - back) * (2 * pos) + back * (2 * (n - 1 - pos) + 1)


class Place:
    def __init__(self, n):
        self.n = n
        self.e = lax.axis_index("exp")
        self.h = lax.axis_index("hid")
        self.p = pos_of(self.e, n)
        self.right = self.ring(1)
        self.left = self.ring(-1)
        self.sib = self.h + 1 - 2 * (self.h % 2)
        self.far = (self.h + 2) % 4
        self.diag = (self.sib + 2) % 4

    def ring(self, away):
        return at_pos((self.p + self.n + away) % self.n, self.n)


def greet(exp_peers, hid_peers):
    barrier = pltpu.get_barrier_semaphore()
    for peer in exp_peers:
        pl.semaphore_signal(barrier, inc=1, device_id={"exp": peer}, device_id_type=MESH)
    for peer in hid_peers:
        pl.semaphore_signal(barrier, inc=1, device_id={"hid": peer}, device_id_type=MESH)
    pl.semaphore_wait(barrier, len(exp_peers) + len(hid_peers))


def remote(src, dst, sems, k, axis, to):
    return pltpu.make_async_remote_copy(
        src_ref=src,
        dst_ref=dst,
        send_sem=sems.at[0, k],
        recv_sem=sems.at[1, k],
        device_id={axis: to},
        device_id_type=MESH,
    )


class Sent:
    def __init__(self):
        self.copies = {}
        self.unsent = []

    def start(self, key, copy):
        copy.start()
        self.copies[key] = copy
        self.unsent.append(copy)

    def recv(self, key):
        self.copies[key].wait_recv()

    def done(self):
        for copy in self.unsent:
            copy.wait_send()
        self.unsent = []


class RingGather:
    def __init__(self, place, view, rows, sems):
        self.place, self.view, self.rows, self.sems = place, view, rows, sems
        self.steps = place.n // 2
        self.sent = Sent()

    def start(self, s):
        rows, half = self.rows, self.rows // 2
        last = s == self.steps - 1
        for side, (away, to) in enumerate(((-s, self.place.right), (s, self.place.left))):
            first, size = ((side * half, half) if last else (0, rows))
            block = self.view(self.place.ring(away), first, size)
            self.sent.start((s, side), remote(block, block, self.sems, 2 * s + side, "exp", to))

    def recv(self, s):
        self.sent.recv((s, 0))
        self.sent.recv((s, 1))

    def done(self):
        self.sent.done()


class RingSum:
    def __init__(self, place, send, recv, rows, sems):
        self.place, self.send, self.recv, self.rows, self.sems = place, send, recv, rows, sems
        self.steps = place.n // 2
        self.slots = send.shape[1]
        self.copies = {}

    def owner(self, s, side):
        away = self.steps - s
        return self.place.ring(away if side == 0 else -away)

    def room(self, s):
        for side in (0, 1):
            if s >= self.slots:
                self.copies[(s - self.slots, side)].wait_send()

    def buffer(self, s, side):
        return self.send.at[side, s % self.slots]

    def go(self, s):
        half = self.rows // 2
        for side, to in ((0, self.place.right), (1, self.place.left)):
            src, dst = self.send.at[side, s % self.slots], self.recv.at[side, s]
            if s == 0:
                src, dst = src.at[pl.ds(side * half, half)], dst.at[pl.ds(side * half, half)]
            copy = remote(src, dst, self.sems, 2 * s + side, "exp", to)
            copy.start()
            self.copies[(s, side)] = copy

    def arrived(self, s, side):
        self.copies[(s, side)].wait_recv()

    def add_into(self, s, side, get):
        half = self.rows // 2
        out = self.buffer(s, side)
        if s == 0:
            out[pl.ds(side * half, half)] = get(pl.ds(side * half, half)).astype(out.dtype)
            return
        self.arrived(s - 1, side)
        came = self.recv.at[side, s - 1]
        for k in (0, 1):
            part = pl.ds(k * half, half)
            value = get(part)
            if s > 1 or k == side:
                value = value + came[part].astype(F32)
            out[part] = value.astype(out.dtype)

    def total(self, part):
        return self.recv[0, self.steps - 1, part].astype(F32) + self.recv[1, self.steps - 1, part].astype(F32)

    def arrive_last(self):
        self.arrived(self.steps - 1, 0)
        self.arrived(self.steps - 1, 1)

    def done(self):
        for s in range(max(0, self.steps - self.slots), self.steps):
            for side in (0, 1):
                self.copies[(s, side)].wait_send()


def local_start(src, dst, sem):
    copy = pltpu.make_async_copy(src, dst, sem)
    copy.start()
    return copy


def split_parts(count):
    return (pl.ds(0, count // 2), pl.ds(count // 2, count // 2))


def rms(values):
    return lax.rsqrt(jnp.mean(values * values, axis=-1, keepdims=True) + EPSILON)


def swap_halves(values):
    half = HEAD_DIM // 2
    width = values.shape[1]
    up = pltpu.roll(values, width - half, 1)
    down = pltpu.roll(values, half, 1)
    first = iota(values.shape, 1) % HEAD_DIM < half
    return jnp.where(first, up, down)


def gain_rows(slab, expert_count):
    pick = (iota((16, LANES), 1) == iota((16, LANES), 0) + expert_count).astype(BF16)
    return nt(pick, slab)


def bias_block(begin_row, first_row, key_count):
    shape = (key_count, begin_row.shape[1])
    keys = iota(shape, 0)
    seen = (keys >= begin_row) & (keys <= first_row + iota(shape, 1))
    return jnp.where(seen, 0.0, NEG_FILL)


class Dims:
    def __init__(self, n, token_count, width, expert_count, local_experts, ff, topk, qc, kc):
        self.n, self.tokens, self.d = n, token_count, width
        self.experts, self.local, self.ff, self.topk = expert_count, local_experts, ff, topk
        self.qc, self.kc = qc, kc
        self.quarter = token_count // 4
        self.shard = width // n
        self.capacity = token_count * topk * 5 // (4 * expert_count)
        self.attn_cols = qc + 2 * kc
        self.slab_at = 2 * qc + 2 * kc
        self.ws_cols = self.slab_at + LANES
        self.heads = qc // HEAD_DIM
        self.group = qc // kc
        self.part_ff = ff // 4
        self.steps = n // 2


def front_kernel(
    dims,
    x, ws, g, cosine, sine, begin, routes, wg, wu, wd,
    ws_out, wg_all, wu_all, wd_all, g_all, normed, qkv, mixed, lse, resid, normed_two, coef, gates, kept,
    ws_all, scale, part, came, mid, came_far,
    ws_sems, g_sems, hid_sems, swap_sems, weight_sems, local_sems,
):
    at = Place(dims.n)
    t, d, ff4 = dims.quarter, dims.d, dims.part_ff
    q4 = d // 4
    greet((at.right, at.left), (at.sib, at.far, at.diag))

    own = local_start(ws, ws_all.at[rows_at(at.e, dims.shard)], local_sems.at[0])
    own.wait()
    ring = RingGather(
        at, lambda o, f, s: ws_all.at[pl.ds(pl.multiple_of(o * dims.shard + f, 16), s)], dims.shard, ws_sems
    )
    ring.start(0)

    swaps = Sent()
    for k, peer in enumerate((at.sib, at.far, at.diag)):
        swaps.start(
            k, remote(g.at[rows_at(peer, t)], g_all.at[at.e, :, rows_at(at.h, q4)], swap_sems, k, "hid", peer)
        )
    g_own = local_start(g.at[rows_at(at.h, t)], g_all.at[at.e, :, rows_at(at.h, q4)], local_sems.at[1])

    weights = ((wg, wg_all, 2), (wu, wu_all, 2), (wd, wd_all, 1))

    def piece(ref, dim, owner):
        spot = rows_at(owner, ff4)
        return ref.at[:, :, spot] if dim == 2 else ref.at[:, spot, :]

    moves = Sent()
    kept_own = []
    for k, (shard, whole, dim) in enumerate(weights):
        moves.start(("far", k), remote(shard, piece(whole, dim, at.h), weight_sems, k, "hid", at.far))
    for k, (shard, whole, dim) in enumerate(weights):
        moves.start(("sib", k), remote(shard, piece(whole, dim, at.h), weight_sems, 3 + k, "hid", at.sib))
        kept_own.append(local_start(shard, piece(whole, dim, at.h), local_sems.at[2 + k]))

    def pass_on(k):
        moves.recv(("far", k))
        whole, dim = weights[k][1:]
        block = piece(whole, dim, at.far)
        moves.start(("on", k), remote(block, block, weight_sems, 6 + k, "hid", at.sib))

    for j in range(4):
        rows = pl.ds(j * t, t)
        values = x[rows, :].astype(F32)
        scale[rows, :] = jnp.broadcast_to(rms(values), (t, LANES))

    for s in range(dims.steps):
        ring.recv(s)
        if s + 1 < dims.steps:
            ring.start(s + 1)
    out_ws = local_start(ws_all, ws_out, local_sems.at[5])

    for k in range(3):
        swaps.recv(k)
    g_own.wait()
    g_ring = RingGather(at, lambda o, f, s: g_all.at[o, pl.ds(f, s)], t, g_sems)
    g_ring.start(0)

    slab = ws_all[:, dims.slab_at :]
    gains = gain_rows(slab, dims.experts)
    kv = dims.kc
    for j in range(4):
        rows = pl.ds(j * t, t)
        block = (x[rows, :].astype(F32) * scale[rows, :1] * gains[0:1, :]).astype(BF16)
        normed[rows, :] = block
        raw = nn(block, ws_all[:, : dims.attn_cols])
        turned = raw[:, : dims.qc + kv]
        repeat = (dims.qc + kv) // LANES
        turned = turned * jnp.tile(cosine[rows, :], (1, repeat)) + swap_halves(turned) * jnp.tile(
            sine[rows, :], (1, repeat)
        )
        queries = turned[:, : dims.qc].astype(BF16) * jnp.asarray(HEAD_DIM**-0.5, BF16)
        qkv[rows, : dims.qc] = queries
        qkv[rows, dims.qc : dims.qc + kv] = turned[:, dims.qc :].astype(BF16)
        qkv[rows, dims.qc + kv :] = raw[:, dims.qc + kv :].astype(BF16)

    g_step = 0
    for j in range(4):
        rows = pl.ds(j * t, t)
        keys = (j + 1) * t
        bias = bias_block(begin[:, j * t : (j + 1) * t], j * t, keys)
        for head in range(dims.heads):
            key_at = dims.qc + head // dims.group * HEAD_DIM
            query = qkv[rows, head * HEAD_DIM : (head + 1) * HEAD_DIM]
            key = qkv[:keys, key_at : key_at + HEAD_DIM]
            value = qkv[:keys, key_at + kv : key_at + kv + HEAD_DIM]
            scores = nt(key, query) + bias
            peak = jnp.max(scores, axis=0, keepdims=True)
            powers = jnp.exp(scores - peak)
            total = jnp.sum(powers, axis=0, keepdims=True)
            probs = (powers * (1.0 / total)).astype(BF16)
            lse[head : head + 1, j * t : (j + 1) * t] = peak + jnp.log(total)
            mixed[rows, head * HEAD_DIM : (head + 1) * HEAD_DIM] = tn(value, probs).T.astype(BF16)
        part[j] = nt(mixed[rows, :], ws_all[:, dims.attn_cols : dims.slab_at]).astype(BF16)
        if j < 3 and g_step + 1 < dims.steps:
            g_ring.recv(g_step)
            g_step += 1
            g_ring.start(g_step)

    sums = Sent()
    sums.start(0, remote(part.at[at.diag], came.at[1], hid_sems, 0, "hid", at.sib))
    sums.start(1, remote(part.at[at.sib], came.at[0], hid_sems, 1, "hid", at.sib))
    sums.recv(0)
    mid[...] = (part[at.far].astype(F32) + came[1].astype(F32)).astype(BF16)
    sums.start(2, remote(mid, came_far, hid_sems, 2, "hid", at.far))
    sums.recv(1)

    chosen = jnp.zeros((dims.tokens, LANES), F32)
    lane = iota((dims.tokens, LANES), 1)
    for k in range(dims.topk):
        chosen = chosen + (routes[:, k : k + 1] == lane).astype(F32)
    earlier = (iota((t, dims.tokens), 1) < iota((t, dims.tokens), 0) + at.h * t).astype(BF16)
    rank = nn(earlier, chosen.astype(BF16))
    lane = iota((t, LANES), 1)
    mine = jnp.zeros((t, LANES), F32)
    route_rows = routes[rows_at(at.h, t), :]
    for k in range(dims.topk):
        mine = mine + (route_rows[:, k : k + 1] == lane).astype(F32)
    keep = mine * (rank < dims.capacity).astype(F32)
    kept[...] = keep

    sums.recv(2)
    for half in split_parts(t):
        first = pl.ds(pl.multiple_of(at.h * t + half.start, 16), half.size)
        values = (
            part[at.h, half].astype(F32) + came[0, half].astype(F32) + came_far[half].astype(F32)
            + x[first, :].astype(F32)
        )
        resid[half, :] = values
        normed_two[half, :] = (values * rms(values) * gains[1:2, :]).astype(BF16)
    logits = nn(normed_two[...], slab)
    picked = jnp.where(mine > 0, logits, NEG_FILL)
    powers = jnp.exp(picked - jnp.max(picked, axis=1, keepdims=True)) * mine
    gate = powers / jnp.sum(powers, axis=1, keepdims=True)
    gates[...] = gate
    coef[...] = (gate * keep).T[: dims.experts, :]

    while g_step + 1 < dims.steps:
        g_ring.recv(g_step)
        g_step += 1
        g_ring.start(g_step)
    for k in range(3):
        pass_on(k)
    g_ring.recv(g_step)
    for k in range(3):
        moves.recv(("sib", k))
        moves.recv(("on", k))
        kept_own[k].wait()
    out_ws.wait()
    for group in (ring, g_ring, swaps, moves, sums):
        group.done()


def moe_kernel(
    dims, big,
    x_own, coef_own, g_all, wg_in, wu_in, wd_in,
    dx, y_all, gate_grad, own_g, own_u, own_d, sib_g, sib_u, sib_d, x_far,
    x_near, g_near, coef, wg, wu, wd, d_gate, d_up, hid, send, recv, grads, stage, y_stage, x_stage, g_stage,
    x_sems, c_sems, sum_sems, grad_sems, job_sems, local_sems, keep_sems, y_sems,
):
    at = Place(dims.n)
    n, t, d, local, ff = dims.n, dims.quarter, dims.d, dims.local, dims.ff
    others = tuple((at.e + k) % n for k in range(1, n))
    greet(others, (at.sib,))

    xs = x_far if big else x_near
    coef[at.e] = coef_own[...]
    if big:
        local_start(x_own, xs.at[rows_at(at.e, t)], local_sems.at[0]).wait()
    else:
        xs[rows_at(at.e, t), :] = x_own[...]
    x_ring = RingGather(at, lambda o, f, s: xs.at[pl.ds(pl.multiple_of(o * t + f, 16), s)], t, x_sems)
    c_half = dims.experts // 2
    c_ring = RingGather(at, lambda o, f, s: coef.at[o, pl.ds(f, s)], dims.experts, c_sems)
    assert c_half % 8 == 0
    c_ring.start(0)
    x_ring.start(0)
    loads = [
        local_start(wg_in, wg, local_sems.at[1]),
        local_start(wu_in, wu, local_sems.at[2]),
        local_start(wd_in, wd, local_sems.at[3]),
    ]
    if not big:
        loads.append(local_start(g_all, g_near, local_sems.at[4]))
    for load in loads:
        load.wait()

    lane = iota((t, LANES), 1)
    y_flight = []

    def forward_row(owner, k):
        rows = rows_at(owner, t)
        if big:
            load = local_start(xs.at[rows], x_stage, local_sems.at[0])
            local_start(g_all.at[owner], g_stage, local_sems.at[4]).wait()
            load.wait()
            x_row, g_row = x_stage, g_stage
        else:
            x_row, g_row = xs.at[rows], g_near.at[owner]
        columns = jnp.concatenate(
            [coef[owner], jnp.zeros((LANES - dims.experts, t), F32)], axis=0
        ).T

        def expert(i, sums):
            share = jnp.sum(jnp.where(lane == at.e * local + i, columns, 0.0), axis=1, keepdims=True)
            pre_gate = nn(x_row[...], wg[i])
            pre_up = nn(x_row[...], wu[i])
            back = nt(g_row[...], wd[i])
            sig = 0.5 * jnp.tanh(0.5 * pre_gate) + 0.5
            silu = pre_gate * sig
            hidden = silu * pre_up
            own = jnp.sum(hidden * back, axis=1, keepdims=True)
            back = share * back
            d_up[i, rows, :] = (back * silu).astype(BF16)
            d_gate[i, rows, :] = (back * pre_up * (sig + silu * (1.0 - sig))).astype(BF16)
            hid[i, rows, :] = (share * hidden).astype(BF16)
            return jnp.where(lane == i, own, sums)

        sums = lax.fori_loop(0, local, expert, jnp.zeros((t, LANES), F32))
        grads[owner] = sums.T[:8, :]
        if len(y_flight) >= 2:
            y_flight[-2].wait()
        out = sum(nn(hid[i, rows, :], wd[i]) for i in range(local))
        y_stage[k % 2] = out.astype(BF16)
        y_flight.append(local_start(y_stage.at[k % 2], y_all.at[owner], y_sems.at[k % 2]))

    forward_row(at.e, 0)
    count = 1
    for s in range(dims.steps):
        x_ring.recv(s)
        c_ring.recv(s)
        if s + 1 < dims.steps:
            c_ring.start(s + 1)
            x_ring.start(s + 1)
        for away in (-(s + 1), s + 1) if s + 1 < dims.steps else (s + 1,):
            forward_row(at.ring(away), count)
            count += 1
    for copy in y_flight[-2:]:
        copy.wait()

    small = Sent()
    for k, peer in enumerate(others):
        small.start(k, remote(grads.at[peer], gate_grad.at[at.e], grad_sems, k, "exp", peer))
    own_small = local_start(grads.at[at.e], gate_grad.at[at.e], local_sems.at[5])

    jobs = [(kind, i) for kind in ("down", "gate", "up") for i in range(local)]
    flights = {}
    kept = {}

    def job(k):
        kind, i = jobs[k]
        slot = k % 2
        if k - 2 in flights:
            for copy in flights[k - 2]:
                copy.wait_send()
            for copy in kept[k - 2]:
                copy.wait()
        own_out, sib_out = {"down": (own_d, sib_d), "gate": (own_g, sib_g), "up": (own_u, sib_u)}[kind]
        if kind == "down":
            width = d // 2

            def strip(c, _):
                cols = rows_at(c, width)
                for f in range(ff // 256):
                    units = slice(f * 256, (f + 1) * 256)
                    if big:
                        def add(r, total):
                            rr = rows_at(r, t)
                            local_start(g_all.at[r], g_stage, local_sems.at[4]).wait()
                            return total + tn(hid[i, rr, units], g_stage[:, cols])
                        value = lax.fori_loop(0, n, add, jnp.zeros((256, width), F32))
                    else:
                        value = tn(hid[i, :, units], g_near.reshape(n * t, d)[:, cols])
                    stage[slot, c, units, :] = value.astype(BF16)
                return 0

            lax.fori_loop(0, 2, strip, 0)
            cuts = [
                (c, lambda b, c=c: stage.at[slot, c, rows_at(b, dims.part_ff), :]) for c in range(2)
            ]
            dest = lambda ref, which, c: ref.at[which, i, :, pl.ds(c * width, width)]
        else:
            grad = d_gate if kind == "gate" else d_up

            def strip(c, _):
                if big:
                    def add(r, total):
                        rr = rows_at(r, t)
                        local_start(xs.at[rr], x_stage, local_sems.at[0]).wait()
                        return total + tn(x_stage[:, rows_at(c, 256)], grad[i, rr, :])
                    value = lax.fori_loop(0, n, add, jnp.zeros((256, ff), F32))
                else:
                    value = tn(xs[:, rows_at(c, 256)], grad[i])
                stage[slot, c // 2, rows_at(c % 2, 256), :] = value.astype(BF16)
                return 0

            lax.fori_loop(0, d // 256, strip, 0)
            cuts = [
                (c, lambda b, c=c: stage.at[slot, c, :, rows_at(b, dims.part_ff)]) for c in range(2)
            ]
            dest = lambda ref, which, c: ref.at[which, i, pl.ds(c * (d // 2), d // 2), :]
        flights[k], kept[k] = [], []
        for c, cut in cuts:
            for which, block in ((1, at.diag), (0, at.sib)):
                copy = remote(cut(block), dest(sib_out, which, c), job_sems, 4 * k + 2 * c + which, "hid", at.sib)
                copy.start()
                flights[k].append(copy)
            for which, block in ((1, at.far), (0, at.h)):
                kept[k].append(
                    local_start(cut(block), dest(own_out, which, c), keep_sems.at[4 * slot + 2 * c + which])
                )

    def input_grad(owner, part):
        rows = pl.ds(pl.multiple_of(owner * t + part.start, 16), part.size)
        total = None
        for i in range(local):
            term = nt(d_gate[i, rows, :], wg[i]) + nt(d_up[i, rows, :], wu[i])
            total = term if total is None else total + term
        return total

    sums = RingSum(at, send, recv, t, sum_sems)
    done_jobs = 0
    for s in range(dims.steps):
        sums.room(s)
        for side in (0, 1):
            owner = sums.owner(s, side)
            sums.add_into(s, side, lambda part, o=owner: input_grad(o, part))
        sums.go(s)
        until = len(jobs) * (s + 1) // dims.steps
        while done_jobs < until:
            job(done_jobs)
            done_jobs += 1
    for part in split_parts(t):
        dx[part, :] = input_grad(at.e, part)
    sums.arrive_last()
    for part in split_parts(t):
        dx[part, :] = dx[part, :] + sums.total(part)

    for k in range(len(others)):
        small.recv(k)
    own_small.wait()
    for k in range(len(jobs)):
        for copy in flights[k]:
            copy.wait_recv()
        if k >= len(jobs) - 2:
            for copy in flights[k]:
                copy.wait_send()
            for copy in kept[k]:
                copy.wait()
    for group in (x_ring, c_ring, small, sums):
        group.done()


def back_kernel(
    dims, big,
    dx, gate_grad, gates, kept, resid, normed_two, g_all, x, ws, qkv, mixed, lse, normed, cosine, sine, begin,
    y_all, own_g, own_u, own_d, sib_g, sib_u, sib_d,
    layer, in_grad, small_one, small_two, att_grad, far_g, far_u, far_d,
    g_own, resid_grad, rows_all, mixed_grad, d_query, d_key, d_value, d_qkv, w_grad, part, came, mid, came_far,
    y_rows, y_send, y_recv, w_send, w_recv, out_rows, in_rows, sum_a, sum_b, cut_send, cut_recv, mid_g, mid_u, mid_d,
    row_sems, y_sems, w_sems, hid_sems, in_sems, layer_sems, small_sems, cut_sems, far_sems, local_sems,
):
    at = Place(dims.n)
    n, t, d, kv = dims.n, dims.quarter, dims.d, dims.kc
    q4 = d // 4
    others = tuple((at.e + k) % n for k in range(1, n))
    greet(others, (at.sib, at.far, at.diag))
    load_g = local_start(g_all.at[at.e], g_own, local_sems.at[0])
    if not big:
        load_y = local_start(y_all, y_rows, local_sems.at[1])
    mids = ((own_g, sib_g, mid_g, far_g), (own_u, sib_u, mid_u, far_u), (own_d, sib_d, mid_d, far_d))
    loads = []
    for k, (own, sib, one, _) in enumerate(mids):
        loads.append(local_start(own.at[1], one.at[0], local_sems.at[2 + 2 * k]))
        loads.append(local_start(sib.at[1], one.at[1], local_sems.at[3 + 2 * k]))

    slab = ws[:, dims.slab_at :]
    gains = gain_rows(slab, dims.experts)
    spread_shape = (n * 8, LANES)
    sub, lane = iota(spread_shape, 0), iota(spread_shape, 1)
    spread = (
        (sub // 8 == lane // dims.local) & (sub % 8 == lane % dims.local) & (lane < dims.experts)
    ).astype(F32)
    gg = tn_exact(gate_grad[...], spread) * kept[...]
    gate = gates[...]
    logit_grad = (gate * (gg - jnp.sum(gate * gg, axis=1, keepdims=True))).astype(BF16)
    load_g.wait()
    gain_two = jnp.zeros((1, d), F32)
    for half in split_parts(t):
        lg = logit_grad[half.start : half.start + half.size, :]
        normed_grad = dx[half, :] + nt(lg, slab)
        inputs = resid[half, :]
        scale = rms(inputs)
        gain_two = gain_two + jnp.sum(normed_grad * inputs * scale, axis=0, keepdims=True)
        weighted = normed_grad * gains[1:2, :]
        value = (
            g_own[half, :].astype(F32) + scale * weighted
            - inputs * (scale * scale * scale) * jnp.mean(weighted * inputs, axis=-1, keepdims=True)
        )
        resid_grad[half, :] = value
        rows_all[pl.ds(pl.multiple_of(at.h * t + half.start, 16), half.size), :] = value.astype(BF16)

    rows = Sent()
    mine = rows_all.at[rows_at(at.h, t)]
    rows.start(0, remote(mine, mine, row_sems, 0, "hid", at.far))
    rows.start(1, remote(mine, mine, row_sems, 1, "hid", at.sib))

    router_rows = dims.experts
    small_rows = router_rows + 8
    sum_a[0, :router_rows, :] = tn(logit_grad, normed_two[...])[:router_rows, :]
    sum_a[0, router_rows:, :] = jnp.broadcast_to(gain_two, (8, d))
    smalls = Sent()
    smalls.start(0, remote(sum_a.at[0], sum_a.at[1], small_sems, 0, "hid", at.sib))

    if not big:
        load_y.wait()
    y_sum = RingSum(at, y_send, y_recv, t, y_sems)

    def y_row(owner):
        if not big:
            return y_rows.at[owner]
        local_start(y_all.at[owner], y_rows.at[0], local_sems.at[1]).wait()
        return y_rows.at[0]

    def y_step(s):
        y_sum.room(s)
        for side in (0, 1):
            row = y_row(y_sum.owner(s, side))
            y_sum.add_into(s, side, lambda part, row=row: row[part].astype(F32))
        y_sum.go(s)

    y_step(0)

    smalls.recv(0)
    sum_a[2] = sum_a[0] + sum_a[1]
    smalls.start(1, remote(sum_a.at[2], sum_a.at[3], small_sems, 1, "hid", at.far))

    rows.recv(0)
    theirs = rows_all.at[rows_at(at.far, t)]
    rows.start(2, remote(theirs, theirs, row_sems, 2, "hid", at.sib))
    for load in loads:
        load.wait()
    fars = Sent()
    for k, (_, _, one, far) in enumerate(mids):
        def add(i, _, one=one):
            one[0, i] = (one[0, i].astype(F32) + one[1, i].astype(F32)).astype(BF16)
            return 0
        lax.fori_loop(0, dims.local, add, 0)
    rows.recv(1)
    rows.recv(2)

    wo = ws[:, dims.attn_cols : dims.slab_at]
    for j in range(4):
        block = pl.ds(j * t, t)
        mixed_grad[block, :] = nn(rows_all[block, :], wo).astype(BF16)
    for k, (_, _, one, far) in enumerate(mids):
        fars.start(k, remote(one.at[0], far, far_sems, k, "hid", at.far))

    shard = dims.shard
    smalls.recv(1)
    sum_a[1] = sum_a[2] + sum_a[3]
    cuts = Sent()
    for owner in range(n):
        cut_send[owner, :small_rows] = sum_a[1, :, owner * shard : (owner + 1) * shard]
    for k, peer in enumerate(others):
        cuts.start(
            k,
            remote(
                cut_send.at[peer, pl.ds(0, small_rows)], cut_recv.at[at.e, pl.ds(0, small_rows)], cut_sems, k, "exp", peer
            ),
        )
    own_cut = local_start(
        cut_send.at[at.e, pl.ds(0, small_rows)], cut_recv.at[at.e, pl.ds(0, small_rows)], local_sems.at[8]
    )

    d_key[...] = jnp.zeros_like(d_key)
    d_value[...] = jnp.zeros_like(d_value)
    y_at = 1
    for j in range(4):
        block = pl.ds(j * t, t)
        keys = (j + 1) * t
        bias = bias_block(begin[:, j * t : (j + 1) * t], j * t, keys)
        for head in range(dims.heads):
            key_at = head // dims.group * HEAD_DIM
            spot = slice(key_at, key_at + HEAD_DIM)
            query = qkv[block, head * HEAD_DIM : (head + 1) * HEAD_DIM]
            key = qkv[:keys, dims.qc + key_at : dims.qc + key_at + HEAD_DIM]
            value = qkv[:keys, dims.qc + kv + key_at : dims.qc + kv + key_at + HEAD_DIM]
            out_grad = mixed_grad[block, head * HEAD_DIM : (head + 1) * HEAD_DIM]
            probs = jnp.exp(nt(key, query) + bias - lse[head : head + 1, j * t : (j + 1) * t])
            prob_grad = nt(value, out_grad)
            inner = jnp.sum(probs * prob_grad, axis=0, keepdims=True)
            score_grad = (probs * (prob_grad - inner)).astype(BF16)
            d_query[block, head * HEAD_DIM : (head + 1) * HEAD_DIM] = tn(score_grad, key) * HEAD_DIM**-0.5
            d_key[:keys, spot] += nn(score_grad, query)
            d_value[:keys, spot] += nn(probs.astype(BF16), out_grad)
        if y_at < dims.steps:
            y_step(y_at)
            y_at += 1

    for j in range(4):
        block = pl.ds(j * t, t)
        raw = jnp.concatenate([d_query[block, :], d_key[block, :]], axis=1)
        repeat = (dims.qc + kv) // LANES
        turned = raw * jnp.tile(cosine[block, :], (1, repeat)) - swap_halves(raw) * jnp.tile(
            sine[block, :], (1, repeat)
        )
        d_qkv[block, : dims.qc + kv] = turned.astype(BF16)
        d_qkv[block, dims.qc + kv :] = d_value[block, :].astype(BF16)
        part[j] = nt(d_qkv[block, :], ws[:, : dims.attn_cols]).astype(BF16)

    sums = Sent()
    sums.start(0, remote(part.at[at.diag], came.at[1], hid_sems, 0, "hid", at.sib))
    sums.start(1, remote(part.at[at.sib], came.at[0], hid_sems, 1, "hid", at.sib))
    for c in range(d // 256):
        cols = slice(c * 256, (c + 1) * 256)
        w_grad[cols, : dims.attn_cols] = tn(normed[:, cols], d_qkv[...])
        w_grad[cols, dims.attn_cols :] = tn(rows_all[:, cols], mixed[...])
    sums.recv(0)
    mid[...] = (part[at.far].astype(F32) + came[1].astype(F32)).astype(BF16)
    sums.start(2, remote(mid, came_far, hid_sems, 2, "hid", at.far))
    sums.recv(1)

    w_sum = RingSum(at, w_send, w_recv, shard, w_sems)

    def w_step(s):
        w_sum.room(s)
        for side in (0, 1):
            owner = w_sum.owner(s, side)
            w_sum.add_into(
                s, side, lambda part, o=owner: w_grad[pl.ds(pl.multiple_of(o * shard + part.start, 16), part.size), :]
            )
        w_sum.go(s)

    w_step(0)
    while y_at < dims.steps:
        y_step(y_at)
        y_at += 1
    y_sum.arrive_last()
    y_own = y_row(at.e)
    for half in split_parts(t):
        out_rows[half, :] = (
            resid[half, :] + y_own[half].astype(F32) + y_sum.total(half)
        ).astype(BF16)
    layers = Sent()

    sums.recv(2)
    gain_one = jnp.zeros((1, d), F32)
    for half in split_parts(t):
        here = pl.ds(pl.multiple_of(at.h * t + half.start, 16), half.size)
        grad = part[at.h, half].astype(F32) + came[0, half].astype(F32) + came_far[half].astype(F32)
        inputs = x[here, :].astype(F32)
        scale = rms(inputs)
        gain_one = gain_one + jnp.sum(grad * inputs * scale, axis=0, keepdims=True)
        weighted = grad * gains[0:1, :]
        in_rows[half, :] = (
            resid_grad[half, :] + scale * weighted
            - inputs * (scale * scale * scale) * jnp.mean(weighted * inputs, axis=-1, keepdims=True)
        ).astype(BF16)
    ins = Sent()
    spot = in_grad.at[rows_at(at.h, t)]
    ins.start(0, remote(in_rows, spot, in_sems, 0, "hid", at.far))
    ins.start(1, remote(in_rows, spot, in_sems, 1, "hid", at.sib))
    own_in = local_start(in_rows, spot, local_sems.at[9])
    sum_b[0] = jnp.broadcast_to(gain_one, (8, d))
    smalls.start(2, remote(sum_b.at[0], sum_b.at[1], small_sems, 2, "hid", at.sib))
    for k, peer in enumerate((at.sib, at.far, at.diag)):
        layers.start(
            k, remote(out_rows.at[:, rows_at(peer, q4)], layer.at[rows_at(at.h, t)], layer_sems, k, "hid", peer)
        )
    own_layer = local_start(out_rows.at[:, rows_at(at.h, q4)], layer.at[rows_at(at.h, t)], local_sems.at[10])
    smalls.recv(2)
    sum_b[2] = sum_b[0] + sum_b[1]
    smalls.start(3, remote(sum_b.at[2], sum_b.at[3], small_sems, 3, "hid", at.far))
    w_at = 1
    if w_at < dims.steps:
        w_step(w_at)
        w_at += 1
    smalls.recv(3)
    sum_b[1] = sum_b[2] + sum_b[3]
    for owner in range(n):
        cut_send[owner, small_rows:] = sum_b[1, :, owner * shard : (owner + 1) * shard]
    for k, peer in enumerate(others):
        cuts.start(
            n + k,
            remote(
                cut_send.at[peer, pl.ds(small_rows, 8)], cut_recv.at[at.e, pl.ds(small_rows, 8)], cut_sems, n - 1 + k, "exp",
                peer,
            ),
        )
    own_cut_two = local_start(
        cut_send.at[at.e, pl.ds(small_rows, 8)], cut_recv.at[at.e, pl.ds(small_rows, 8)], local_sems.at[11]
    )
    ins.recv(0)
    far_rows = in_grad.at[rows_at(at.far, t)]
    ins.start(2, remote(far_rows, far_rows, in_sems, 2, "hid", at.sib))
    while w_at < dims.steps:
        w_step(w_at)
        w_at += 1
    w_sum.arrive_last()
    for part_rows in split_parts(shard):
        here = pl.ds(pl.multiple_of(at.e * shard + part_rows.start, 16), part_rows.size)
        att_grad[part_rows, :] = w_grad[here, :] + w_sum.total(part_rows)

    for k in range(n - 1):
        cuts.recv(k)
        cuts.recv(n + k)
    own_cut.wait()
    own_cut_two.wait()
    total = cut_recv[0]
    for k in range(1, n):
        total = total + cut_recv[k]
    small_one[...] = total[:small_rows]
    small_two[...] = total[small_rows:]

    for k in range(3):
        fars.recv(k)
        layers.recv(k)
    ins.recv(1)
    ins.recv(2)
    own_in.wait()
    own_layer.wait()
    for group in (rows, smalls, y_sum, fars, cuts, sums, w_sum, ins, layers):
        group.done()


def tables(segments, token_count):
    counts = [jnp.sum((segments == k).astype(jnp.int32)) for k in range(SEGS)]
    begin = jnp.zeros((token_count,), jnp.int32)
    start = jnp.zeros((), jnp.int32)
    for k in range(SEGS):
        begin = begin + jnp.where(segments == k, start, 0)
        start = start + counts[k]
    positions = jnp.arange(token_count, dtype=jnp.int32) - begin
    half = HEAD_DIM // 2
    freqs = ROPE_BASE ** (-(jnp.arange(half, dtype=F32) * 2.0 / HEAD_DIM))
    angles = positions.astype(F32)[:, None] * freqs[None, :]
    cosine, sine = jnp.cos(angles), jnp.sin(angles)
    return begin[None, :], jnp.concatenate([cosine] * 4, axis=1), jnp.concatenate([-sine, sine] * 2, axis=1)


def per_device(
    tokens,
    segment_ids,
    routes,
    norm1_gain,
    norm2_gain,
    query_weight,
    key_matrix,
    value_matrix,
    out_weight,
    router_weight,
    gate_weight,
    up_weight,
    down_weight,
    out_grad,
):
    n = lax.axis_size("exp")
    assert lax.axis_size("hid") == 4
    token_count, d = tokens.shape
    local, _, part_ff = gate_weight.shape
    experts = router_weight.shape[1]
    dims = Dims(
        n, token_count, d, experts, local, 4 * part_ff, routes.shape[1], query_weight.shape[1], key_matrix.shape[1]
    )
    t, ff, steps, shard = dims.quarter, dims.ff, dims.steps, dims.shard
    begin, cosine, sine = tables(segment_ids[0], token_count)
    pad = jnp.zeros((shard, LANES - experts - 2), F32)
    ws = jnp.concatenate(
        [query_weight, key_matrix, value_matrix, out_weight, router_weight, norm1_gain[:, None], norm2_gain[:, None], pad],
        axis=1,
    ).astype(BF16)
    wg, wu, wd = gate_weight.astype(BF16), up_weight.astype(BF16), down_weight.astype(BF16)

    vmem = pl.BlockSpec(memory_space=pltpu.VMEM)
    anywhere = pl.BlockSpec(memory_space=pl.ANY)
    shape = jax.ShapeDtypeStruct
    dma = pltpu.SemaphoreType.DMA

    (ws_all, wg_all, wu_all, wd_all, g_all, normed, qkv, mixed, lse, resid, normed_two, coef, gates, kept) = pl.pallas_call(
        functools.partial(front_kernel, dims),
        out_shape=[
            shape((d, dims.ws_cols), BF16),
            shape((local, d, ff), BF16),
            shape((local, d, ff), BF16),
            shape((local, ff, d), BF16),
            shape((n, t, d), BF16),
            shape((token_count, d), BF16),
            shape((token_count, dims.attn_cols), BF16),
            shape((token_count, dims.qc), BF16),
            shape((8, token_count), F32),
            shape((t, d), F32),
            shape((t, d), BF16),
            shape((experts, t), F32),
            shape((t, LANES), F32),
            shape((t, LANES), F32),
        ],
        in_specs=[vmem, vmem, anywhere, vmem, vmem, vmem, vmem, anywhere, anywhere, anywhere],
        out_specs=[anywhere] * 5 + [vmem] * 9,
        scratch_shapes=[
            pltpu.VMEM((d, dims.ws_cols), BF16),
            pltpu.VMEM((token_count, LANES), F32),
            pltpu.VMEM((4, t, d), BF16),
            pltpu.VMEM((2, t, d), BF16),
            pltpu.VMEM((t, d), BF16),
            pltpu.VMEM((t, d), BF16),
            dma((2, 2 * steps)),
            dma((2, 2 * steps)),
            dma((2, 3)),
            dma((2, 3)),
            dma((2, 9)),
            dma((6,)),
        ],
        compiler_params=pltpu.CompilerParams(
            collective_id=0, has_side_effects=True, vmem_limit_bytes=SMALL_VMEM
        ),
    )(tokens, ws, out_grad, cosine, sine, begin, routes, wg, wu, wd)

    big = n * t * d * 2 > 6 * 2**20
    near = 16 if big else n * t
    jobs = 3 * local
    wide = [shape((2, local, d, part_ff), BF16)] * 2 + [shape((2, local, part_ff, d), BF16)]
    (dx, y_all, gate_grad, own_g, own_u, own_d, sib_g, sib_u, sib_d, _) = pl.pallas_call(
        functools.partial(moe_kernel, dims, big),
        out_shape=[shape((t, d), F32), shape((n, t, d), BF16), shape((n, 8, t), F32)]
        + wide
        + wide
        + [shape((n * t if big else 16, d), BF16)],
        in_specs=[vmem, vmem] + [anywhere] * 4,
        out_specs=[vmem] + [anywhere] * 9,
        scratch_shapes=[
            pltpu.VMEM((near, d), BF16),
            pltpu.VMEM((1, 16, d) if big else (n, t, d), BF16),
            pltpu.VMEM((n, experts, t), F32),
            pltpu.VMEM((local, d, ff), BF16),
            pltpu.VMEM((local, d, ff), BF16),
            pltpu.VMEM((local, ff, d), BF16),
            pltpu.VMEM((local, n * t, ff), BF16),
            pltpu.VMEM((local, n * t, ff), BF16),
            pltpu.VMEM((local, n * t, ff), BF16),
            pltpu.VMEM((2, 2, t, d), BF16),
            pltpu.VMEM((2, steps, t, d), BF16),
            pltpu.VMEM((n, 8, t), F32),
            pltpu.VMEM((2, 2, d // 2, ff), BF16),
            pltpu.VMEM((2, t, d), BF16),
            pltpu.VMEM((t, d) if big else (16, LANES), BF16),
            pltpu.VMEM((t, d) if big else (16, LANES), BF16),
            dma((2, 2 * steps)),
            dma((2, 2 * steps)),
            dma((2, 2 * steps)),
            dma((2, n - 1)),
            dma((2, 4 * jobs)),
            dma((6,)),
            dma((8,)),
            dma((2,)),
        ],
        compiler_params=pltpu.CompilerParams(
            collective_id=1, has_side_effects=True, vmem_limit_bytes=VMEM_LIMIT
        ),
    )(normed_two, coef, g_all, wg_all, wu_all, wd_all)

    small_rows = experts + 8
    att = dims.attn_cols + dims.qc
    (layer, in_grad, small_one, small_two, att_grad, far_g, far_u, far_d) = pl.pallas_call(
        functools.partial(back_kernel, dims, big),
        out_shape=[
            shape((token_count, d // 4), BF16),
            shape((token_count, d), BF16),
            shape((small_rows, shard), F32),
            shape((8, shard), F32),
            shape((shard, att), F32),
            shape((local, d, part_ff), BF16),
            shape((local, d, part_ff), BF16),
            shape((local, part_ff, d), BF16),
        ],
        in_specs=[vmem] * 6 + [anywhere] + [vmem] * 9 + [anywhere] * 7,
        out_specs=[anywhere] * 2 + [vmem] * 3 + [anywhere] * 3,
        scratch_shapes=[
            pltpu.VMEM((t, d), BF16),
            pltpu.VMEM((t, d), F32),
            pltpu.VMEM((token_count, d), BF16),
            pltpu.VMEM((token_count, dims.qc), BF16),
            pltpu.VMEM((token_count, dims.qc), F32),
            pltpu.VMEM((token_count, dims.kc), F32),
            pltpu.VMEM((token_count, dims.kc), F32),
            pltpu.VMEM((token_count, dims.attn_cols), BF16),
            pltpu.VMEM((d, att), F32),
            pltpu.VMEM((4, t, d), BF16),
            pltpu.VMEM((2, t, d), BF16),
            pltpu.VMEM((t, d), BF16),
            pltpu.VMEM((t, d), BF16),
            pltpu.VMEM((1 if big else n, t, d), BF16),
            pltpu.VMEM((2, 2, t, d), BF16),
            pltpu.VMEM((2, steps, t, d), BF16),
            pltpu.VMEM((2, 2, shard, att), BF16),
            pltpu.VMEM((2, steps, shard, att), BF16),
            pltpu.VMEM((t, d), BF16),
            pltpu.VMEM((t, d), BF16),
            pltpu.VMEM((4, small_rows, d), F32),
            pltpu.VMEM((4, 8, d), F32),
            pltpu.VMEM((n, small_rows + 8, shard), F32),
            pltpu.VMEM((n, small_rows + 8, shard), F32),
            pltpu.VMEM((2, local, d, part_ff), BF16),
            pltpu.VMEM((2, local, d, part_ff), BF16),
            pltpu.VMEM((2, local, part_ff, d), BF16),
            dma((2, 3)),
            dma((2, 2 * steps)),
            dma((2, 2 * steps)),
            dma((2, 3)),
            dma((2, 3)),
            dma((2, 3)),
            dma((2, 4)),
            dma((2, 2 * (n - 1))),
            dma((2, 3)),
            dma((12,)),
        ],
        compiler_params=pltpu.CompilerParams(
            collective_id=2, has_side_effects=True, vmem_limit_bytes=VMEM_LIMIT
        ),
    )(
        dx, gate_grad.reshape(n * 8, t), gates, kept, resid, normed_two, g_all, tokens, ws_all, qkv, mixed, lse, normed,
        cosine, sine, begin, y_all, own_g, own_u, own_d, sib_g, sib_u, sib_d,
    )

    def three(own, sib, far):
        return own[0].astype(F32) + sib[0].astype(F32) + far.astype(F32)

    qc, kc = dims.qc, dims.kc
    return (
        layer,
        in_grad.astype(F32),
        small_two[0],
        small_one[experts],
        att_grad[:, :qc],
        att_grad[:, qc : qc + kc],
        att_grad[:, qc + kc : qc + 2 * kc],
        att_grad[:, dims.attn_cols :],
        small_one[:experts].T,
        three(own_g, sib_g, far_g),
        three(own_u, sib_u, far_u),
        three(own_d, sib_d, far_d),
    )


def solution(mesh):
    in_specs = (
        P("exp", None),
        P("exp", None),
        P("exp", None),
        P("exp"),
        P("exp"),
        P("exp", "hid"),
        P("exp", "hid"),
        P("exp", "hid"),
        P("exp", "hid"),
        P("exp", None),
        P("exp", None, "hid"),
        P("exp", None, "hid"),
        P("exp", "hid", None),
        P("exp", "hid"),
    )
    out_specs = (
        P("exp", "hid"),
        P("exp", None),
        P("exp"),
        P("exp"),
        P("exp", "hid"),
        P("exp", "hid"),
        P("exp", "hid"),
        P("exp", "hid"),
        P("exp", None),
        P("exp", None, "hid"),
        P("exp", None, "hid"),
        P("exp", "hid", None),
    )
    return jax.shard_map(
        per_device, mesh=mesh, in_specs=in_specs, out_specs=out_specs, check_vma=False
    )
```

```python
import functools
import math

import jax
import jax.numpy as jnp
from jax import lax
from jax.experimental import pallas as pl
from jax.experimental.pallas import tpu as pltpu
from jax.sharding import PartitionSpec as P

HEAD_DIM = 64
SEGS = 4
EPSILON = 1e-05
ROPE_BASE = 10000.0
NEG_FILL = -1e30
LANES = 128
MESH = pl.DeviceIdType.MESH
F32 = jnp.float32
BF16 = jnp.bfloat16
VMEM_LIMIT = 62 * 2**20


def nn(a, b):
    return lax.dot_general(a, b, (((1,), (0,)), ((), ())), preferred_element_type=F32)


def nt(a, b):
    return lax.dot_general(a, b, (((1,), (1,)), ((), ())), preferred_element_type=F32)


def tn(a, b):
    return lax.dot_general(a, b, (((0,), (0,)), ((), ())), preferred_element_type=F32)


def tn_exact(a, b):
    return lax.dot_general(
        a, b, (((0,), (0,)), ((), ())), preferred_element_type=F32, precision=lax.Precision.HIGHEST
    )


def iota(shape, dim):
    return lax.broadcasted_iota(jnp.int32, shape, dim)


def rows_at(index, size):
    return pl.ds(pl.multiple_of(index * size, size), size)


def pos_of(index, n):
    odd = index % 2
    return (1 - odd) * (index // 2) + odd * (n - 1 - index // 2)


def at_pos(pos, n):
    back = pos // (n // 2)
    return (1 - back) * (2 * pos) + back * (2 * (n - 1 - pos) + 1)


class Place:
    def __init__(self, n):
        self.n = n
        self.e = lax.axis_index("exp")
        self.h = lax.axis_index("hid")
        self.p = pos_of(self.e, n)
        self.right = self.ring(1)
        self.left = self.ring(-1)
        self.sib = self.h + 1 - 2 * (self.h % 2)
        self.far = (self.h + 2) % 4
        self.diag = (self.sib + 2) % 4

    def ring(self, away):
        return at_pos((self.p + self.n + away) % self.n, self.n)


def greet(exp_peers, hid_peers):
    barrier = pltpu.get_barrier_semaphore()
    for peer in exp_peers:
        pl.semaphore_signal(barrier, inc=1, device_id={"exp": peer}, device_id_type=MESH)
    for peer in hid_peers:
        pl.semaphore_signal(barrier, inc=1, device_id={"hid": peer}, device_id_type=MESH)
    pl.semaphore_wait(barrier, len(exp_peers) + len(hid_peers))


def remote(src, dst, sems, k, axis, to):
    return pltpu.make_async_remote_copy(
        src_ref=src,
        dst_ref=dst,
        send_sem=sems.at[0, k],
        recv_sem=sems.at[1, k],
        device_id={axis: to},
        device_id_type=MESH,
    )


class Sent:
    def __init__(self):
        self.copies = {}
        self.unsent = []

    def start(self, key, copy):
        copy.start()
        self.copies[key] = copy
        self.unsent.append(copy)

    def recv(self, key):
        self.copies[key].wait_recv()

    def done(self):
        for copy in self.unsent:
            copy.wait_send()
        self.unsent = []


class RingGather:
    def __init__(self, place, view, rows, sems):
        self.place, self.view, self.rows, self.sems = place, view, rows, sems
        self.steps = place.n // 2
        self.sent = Sent()

    def chunks(self, s):
        for c in (0, 1):
            for side in (0, 1):
                if s < self.steps - 1 or c == side:
                    yield c, side

    def start(self, s):
        half = self.rows // 2
        for c, side in self.chunks(s):
            if s:
                self.sent.recv((s - 1, side, c))
            away, to = ((-s, self.place.right), (s, self.place.left))[side]
            block = self.view(self.place.ring(away), c * half, half)
            self.sent.start((s, side, c), remote(block, block, self.sems, 4 * s + 2 * side + c, "exp", to))
        if 0 < s == self.steps - 1:
            self.sent.recv((s - 1, 0, 1))
            self.sent.recv((s - 1, 1, 0))

    def recv_last(self):
        for c, side in self.chunks(self.steps - 1):
            self.sent.recv((self.steps - 1, side, c))

    def done(self):
        self.sent.done()


class RingSum:
    def __init__(self, place, send, recv, rows, sems):
        self.place, self.send, self.recv, self.rows, self.sems = place, send, recv, rows, sems
        self.steps = place.n // 2
        self.copies = {}

    def owner(self, s, side):
        away = self.steps - s
        return self.place.ring(away if side == 0 else -away)

    def chunks(self, s):
        for c in (0, 1):
            for side in (0, 1):
                if s > 0 or c == side:
                    yield c, side

    def put(self, s, get):
        if s >= 2:
            for c, side in self.chunks(s - 2):
                self.copies[(s - 2, side, c)].wait_send()
        if s == 0:
            half = self.rows // 2
            terms = get(0, self.owner(0, 0)).astype(self.send.dtype)
            self.send[0, 0, pl.ds(0, half)] = terms[:half]
            self.send[1, 0, pl.ds(half, half)] = terms[half:]
            return
        for side in (0, 1):
            self.send[side, s % 2] = get(side, self.owner(s, side)).astype(self.send.dtype)

    def go(self, s):
        half = self.rows // 2
        for c, side in self.chunks(s):
            rows = pl.ds(c * half, half)
            src = self.send.at[side, s % 2, rows]
            if s > 1 or (s == 1 and c == side):
                self.copies[(s - 1, side, c)].wait_recv()
                came = self.recv[side, s - 1, rows].astype(F32)
                src[...] = (src[...].astype(F32) + came).astype(src.dtype)
            to = self.place.left if side else self.place.right
            copy = remote(src, self.recv.at[side, s, rows], self.sems, 4 * s + 2 * side + c, "exp", to)
            copy.start()
            self.copies[(s, side, c)] = copy

    def arrive_last(self):
        for c, side in self.chunks(self.steps - 1):
            self.copies[(self.steps - 1, side, c)].wait_recv()

    def total(self, part):
        return self.recv[0, self.steps - 1, part].astype(F32) + self.recv[1, self.steps - 1, part].astype(F32)

    def done(self):
        for s in range(self.steps - 2, self.steps):
            for c, side in self.chunks(s):
                self.copies[(s, side, c)].wait_send()


def local_start(src, dst, sem):
    copy = pltpu.make_async_copy(src, dst, sem)
    copy.start()
    return copy


def split_parts(count):
    return (pl.ds(0, count // 2), pl.ds(count // 2, count // 2))


def rms(values):
    return lax.rsqrt(jnp.mean(values * values, axis=-1, keepdims=True) + EPSILON)


def swap_halves(values):
    half = HEAD_DIM // 2
    width = values.shape[1]
    up = pltpu.roll(values, width - half, 1)
    down = pltpu.roll(values, half, 1)
    first = iota(values.shape, 1) % HEAD_DIM < half
    return jnp.where(first, up, down)


def gain_rows(slab, expert_count):
    pick = (iota((16, LANES), 1) == iota((16, LANES), 0) + expert_count).astype(BF16)
    return nt(pick, slab)


def bias_block(begin_row, first_row, key_count):
    shape = (key_count, begin_row.shape[1])
    keys = iota(shape, 0)
    seen = (keys >= begin_row) & (keys <= first_row + iota(shape, 1))
    return jnp.where(seen, 0.0, NEG_FILL)


class Dims:
    def __init__(self, n, token_count, width, expert_count, local_experts, ff, topk, qc, kc):
        self.n, self.tokens, self.d = n, token_count, width
        self.experts, self.local, self.ff, self.topk = expert_count, local_experts, ff, topk
        self.qc, self.kc = qc, kc
        self.quarter = token_count // 4
        self.shard = width // n
        self.capacity = token_count * topk * 5 // (4 * expert_count)
        self.attn_cols = qc + 2 * kc
        self.slab_at = 2 * qc + 2 * kc
        self.ws_cols = self.slab_at + LANES
        self.heads = qc // HEAD_DIM
        self.group = qc // kc
        self.part_ff = ff // 4
        self.steps = n // 2
        self.jobs = 3 * local_experts
        self.crossing = self.jobs // 2


def tall(row, count):
    return jnp.broadcast_to(row, (LANES, row.shape[1])).T[:, :count]


def front_kernel(
    dims,
    x, seg, routes, wq, wk, wv, wo, router, gain_one, gain_two, g, wg, wu, wd,
    ws_out, wg_all, wu_all, wd_cast, g_all, probs_out, normed, qkv, mixed, cosine, sine, resid, normed_two, coef, gates, kept,
    ws_all, wide, cast, wide_down, cast_down, begin, probs, part, came, mid, came_far,
    ws_sems, g_sems, hid_sems, swap_sems, weight_sems, local_sems, probs_sems,
):
    at = Place(dims.n)
    t, d, ff4, shard, tokens = dims.quarter, dims.d, dims.part_ff, dims.shard, dims.tokens
    q4 = d // 4
    kv = dims.kc
    loads = [local_start(ref, wide.at[k], local_sems.at[k]) for k, ref in enumerate((wg, wu))]
    load_down = local_start(wd, wide_down, local_sems.at[2])

    mine = rows_at(at.e, shard)
    at_col = 0
    for ref in (wq, wk, wv, wo):
        ws_all[mine, at_col : at_col + ref.shape[1]] = ref[...].astype(BF16)
        at_col += ref.shape[1]
    lane = iota((shard, LANES), 1)
    slab = jnp.concatenate([router[...], jnp.zeros((LANES - dims.experts, shard), F32)], axis=0).T
    slab = jnp.where(lane == dims.experts, tall(gain_one[...], LANES), slab)
    slab = jnp.where(lane == dims.experts + 1, tall(gain_two[...], LANES), slab)
    ws_all[mine, dims.slab_at :] = slab.astype(BF16)

    greet((at.right, at.left), (at.sib, at.far, at.diag))
    ring = RingGather(at, lambda o, f, s: ws_all.at[pl.ds(pl.multiple_of(o * shard + f, 16), s)], shard, ws_sems)
    ring.start(0)

    swaps = Sent()
    for k, peer in enumerate((at.sib, at.far, at.diag)):
        swaps.start(
            k, remote(g.at[rows_at(peer, t)], g_all.at[at.e, :, rows_at(at.h, q4)], swap_sems, k, "hid", peer)
        )
    g_own = local_start(g.at[rows_at(at.h, t)], g_all.at[at.e, :, rows_at(at.h, q4)], local_sems.at[3])

    moves = Sent()
    kept_own = []
    units = [(k, i) for k in (0, 1) for i in range(dims.local)]
    lot = (5 * len(units) + 7) // 8

    def piece(ref, owner):
        return ref.at[:, :, rows_at(owner, ff4)]

    def send_unit(u):
        k, i = units[u]
        spot = (wg_all, wu_all)[k].at[i, :, rows_at(at.h, ff4)]
        moves.start(("far", u), remote(cast.at[k, i], spot, weight_sems, u, "hid", at.far))

    def pass_on(u):
        k, i = units[u]
        moves.recv(("far", u))
        spot = (wg_all, wu_all)[k].at[i, :, rows_at(at.far, ff4)]
        moves.start(("on", u), remote(spot, spot, weight_sems, len(units) + u, "hid", at.sib))

    for k, whole in enumerate((wg_all, wu_all)):
        loads[k].wait()
        cast[k] = wide[k].astype(BF16)
        for u in range(len(units)):
            if units[u][0] == k and u < lot:
                send_unit(u)
    for k, whole in enumerate((wg_all, wu_all)):
        moves.start(("sib", k), remote(cast.at[k], piece(whole, at.h), weight_sems, 2 * len(units) + k, "hid", at.sib))
        kept_own.append(local_start(cast.at[k], piece(whole, at.h), local_sems.at[4 + k]))

    ring.start(1)
    for k in range(3):
        swaps.recv(k)
    g_own.wait()
    g_ring = RingGather(at, lambda o, f, s: g_all.at[o, pl.ds(f, s)], t, g_sems)
    g_ring.start(0)

    counts = [jnp.sum((seg[...] == k).astype(F32), axis=1, keepdims=True) for k in range(SEGS)]
    first = jnp.zeros((1, tokens), F32)
    total = jnp.zeros((1, 1), F32)
    for k in range(SEGS):
        first = first + jnp.where(seg[...] == k, total, 0.0)
        total = total + counts[k]
    begin[...] = jnp.broadcast_to(first, (8, tokens)).astype(jnp.int32)
    lane = iota((1, LANES), 1)
    half = HEAD_DIM // 2
    freqs = jnp.exp((lane % half).astype(F32) * (-math.log(ROPE_BASE) / half))
    positions = iota((1, tokens), 1).astype(F32) - first

    def table(j):
        rows = pl.ds(j * t, t)
        angles = tall(positions[:, j * t : (j + 1) * t], LANES) * freqs
        cosine[rows, :] = jnp.cos(angles)
        sine[rows, :] = jnp.where(lane % HEAD_DIM < half, -1.0, 1.0) * jnp.sin(angles)

    todo = [functools.partial(table, j) for j in range(4)]

    for s in range(2, dims.steps):
        if todo:
            todo.pop(0)()
            todo.pop(0)()
        ring.start(s)
    for job in todo:
        job()
    load_down.wait()
    cast_down[...] = wide_down[...].astype(BF16)
    save_down = local_start(cast_down, wd_cast, local_sems.at[7])
    ring.recv_last()
    out_ws = local_start(ws_all, ws_out, local_sems.at[6])

    g_ring.start(1)
    g_step = 2

    slab = ws_all[:, dims.slab_at :]
    gains = gain_rows(slab, dims.experts)
    repeat = (dims.qc + kv) // LANES
    for j in range(4):
        rows = pl.ds(j * t, t)
        values = x[rows, :].astype(F32)
        block = (values * rms(values) * gains[0:1, :]).astype(BF16)
        normed[rows, :] = block
        raw = nn(block, ws_all[:, : dims.attn_cols])
        turned = raw[:, : dims.qc + kv]
        turned = turned * jnp.tile(cosine[rows, :], (1, repeat)) + swap_halves(turned) * jnp.tile(
            sine[rows, :], (1, repeat)
        )
        queries = turned[:, : dims.qc].astype(BF16) * jnp.asarray(HEAD_DIM**-0.5, BF16)
        qkv[rows, : dims.qc] = queries
        qkv[rows, dims.qc : dims.qc + kv] = turned[:, dims.qc :].astype(BF16)
        qkv[rows, dims.qc + kv :] = raw[:, dims.qc + kv :].astype(BF16)

    saves = []
    for j in range(4):
        rows = pl.ds(j * t, t)
        keys = (j + 1) * t
        bias = bias_block(begin[:1, j * t : (j + 1) * t], j * t, keys)
        for head in range(dims.heads):
            key_at = dims.qc + head // dims.group * HEAD_DIM
            query = qkv[rows, head * HEAD_DIM : (head + 1) * HEAD_DIM]
            key = qkv[:keys, key_at : key_at + HEAD_DIM]
            value = qkv[:keys, key_at + kv : key_at + kv + HEAD_DIM]
            scores = nt(key, query) + bias
            powers = jnp.exp(scores - jnp.max(scores, axis=0, keepdims=True))
            share = (powers * (1.0 / jnp.sum(powers, axis=0, keepdims=True))).astype(BF16)
            probs[j, head, :keys, :] = share
            mixed[rows, head * HEAD_DIM : (head + 1) * HEAD_DIM] = tn(value, share).T.astype(BF16)
        saves.append(
            local_start(probs.at[j, :, pl.ds(0, keys)], probs_out.at[j, :, pl.ds(0, keys)], probs_sems.at[j])
        )

    wo_all = ws_all.at[:, pl.ds(dims.attn_cols, dims.qc)]
    sums = Sent()
    for k, quarter in enumerate((at.diag, at.far, at.sib, at.h)):
        part[quarter] = nt(mixed[rows_at(quarter, t), :], wo_all[...]).astype(BF16)
        if k == 0:
            sums.start(0, remote(part.at[at.diag], came.at[1], hid_sems, 0, "hid", at.sib))
        if k == 1:
            sums.recv(0)
            mid[...] = (part[at.far].astype(F32) + came[1].astype(F32)).astype(BF16)
            sums.start(2, remote(mid, came_far, hid_sems, 2, "hid", at.far))
        if k == 2:
            sums.start(1, remote(part.at[at.sib], came.at[0], hid_sems, 1, "hid", at.sib))
    for u in range(lot, len(units)):
        send_unit(u)
    if g_step < dims.steps:
        g_ring.start(g_step)
        g_step += 1
    for u in range(lot):
        pass_on(u)

    expert = iota((dims.experts, tokens), 0)
    chosen = jnp.zeros((dims.experts, tokens), F32)
    for k in range(dims.topk):
        chosen = chosen + (routes[k : k + 1, :] == expert).astype(F32)
    earlier = (iota((tokens, t), 0) < iota((tokens, t), 1) + at.h * t).astype(BF16)
    rank = nn(chosen.astype(BF16), earlier)
    expert = iota((dims.experts, t), 0)
    own_routes = routes[:, rows_at(at.h, t)]
    mine = jnp.zeros((dims.experts, t), F32)
    for k in range(dims.topk):
        mine = mine + (own_routes[k : k + 1, :] == expert).astype(F32)
    keep = mine * (rank < dims.capacity).astype(F32)
    rest = jnp.zeros((LANES - dims.experts, t), F32)
    mine = jnp.concatenate([mine, rest], axis=0).T
    keep = jnp.concatenate([keep, rest], axis=0).T
    kept[...] = keep

    sums.recv(1)
    sums.recv(2)
    for rows in split_parts(t):
        first = pl.ds(pl.multiple_of(at.h * t + rows.start, 16), rows.size)
        values = (
            part[at.h, rows].astype(F32) + came[0, rows].astype(F32) + came_far[rows].astype(F32)
            + x[first, :].astype(F32)
        )
        resid[rows, :] = values
        normed_two[rows, :] = (values * rms(values) * gains[1:2, :]).astype(BF16)
    logits = nn(normed_two[...], slab)
    picked = jnp.where(mine > 0, logits, NEG_FILL)
    powers = jnp.exp(picked - jnp.max(picked, axis=1, keepdims=True)) * mine
    gate = powers / jnp.sum(powers, axis=1, keepdims=True)
    gates[...] = gate
    coef[...] = (gate * keep).T[: dims.experts, :]

    while g_step < dims.steps:
        g_ring.start(g_step)
        g_step += 1
    for u in range(lot, len(units)):
        pass_on(u)
    g_ring.recv_last()
    for k in range(2):
        moves.recv(("sib", k))
        kept_own[k].wait()
    for u in range(len(units)):
        moves.recv(("on", u))
    for copy in saves:
        copy.wait()
    out_ws.wait()
    save_down.wait()
    for group in (ring, g_ring, swaps, moves, sums):
        group.done()


def moe_kernel(
    dims, big,
    x_own, coef_own, g_all, wg_in, wu_in, wd_in,
    dx, y_all, gate_grad, own_out, sib_out, own_far, sib_far, far_out, x_far,
    x_near, g_near, coef, wg, wu, wd, d_gate, d_up, hid, send, recv, grads, stage, x_stage, g_stage,
    x_sems, c_sems, sum_sems, grad_sems, wd_sems, job_sems, far_sems, local_sems, keep_sems, y_sems, free_sem,
):
    at = Place(dims.n)
    n, t, d, local, ff, ff4 = dims.n, dims.quarter, dims.d, dims.local, dims.ff, dims.part_ff
    others = tuple((at.e + k) % n for k in range(1, n))
    load_gate = local_start(wg_in, wg, local_sems.at[1])
    load_up = local_start(wu_in, wu, local_sems.at[2])
    if not big:
        load_g = local_start(g_all, g_near, local_sems.at[4])
    xs = x_far if big else x_near
    coef[at.e] = coef_own[...]
    if big:
        local_start(x_own, xs.at[rows_at(at.e, t)], local_sems.at[0]).wait()
    else:
        xs[rows_at(at.e, t), :] = x_own[...]
    greet(others, (at.sib, at.far))

    x_ring = RingGather(at, lambda o, f, s: xs.at[pl.ds(pl.multiple_of(o * t + f, 16), s)], t, x_sems)
    c_ring = RingGather(at, lambda o, f, s: coef.at[o, pl.ds(f, s)], dims.experts, c_sems)
    c_ring.start(0)
    x_ring.start(0)

    def piece(owner):
        return wd.at[:, rows_at(owner, ff4), :]

    downs = Sent()
    downs.start(0, remote(wd_in, piece(at.h), wd_sems, 0, "hid", at.far))
    downs.start(1, remote(wd_in, piece(at.h), wd_sems, 1, "hid", at.sib))
    own_down = local_start(wd_in, piece(at.h), local_sems.at[3])

    def x_row(owner):
        if not big:
            return xs.at[rows_at(owner, t)]
        local_start(xs.at[rows_at(owner, t)], x_stage, local_sems.at[0]).wait()
        return x_stage

    def g_row(owner):
        if not big:
            return g_near.at[owner]
        local_start(g_all.at[owner], g_stage, local_sems.at[4]).wait()
        return g_stage

    lane = iota((t, LANES), 1)

    def pass_one(owner):
        rows = rows_at(owner, t)
        inputs = x_row(owner)
        for i in range(local):
            d_gate[i, rows, :] = nn(inputs[...], wg[i]).astype(BF16)
            d_up[i, rows, :] = nn(inputs[...], wu[i]).astype(BF16)

    def pass_two(owner, slot, fresh):
        rows = rows_at(owner, t)
        inputs = x_row(owner) if fresh else None
        outs = g_row(owner)
        columns = jnp.concatenate([coef[owner], jnp.zeros((LANES - dims.experts, t), F32)], axis=0).T
        sums = jnp.zeros((t, LANES), F32)
        for i in range(local):
            share = jnp.sum(jnp.where(lane == at.e * local + i, columns, 0.0), axis=1, keepdims=True)
            if fresh:
                pre_gate = nn(inputs[...], wg[i])
                pre_up = nn(inputs[...], wu[i])
            else:
                pre_gate = d_gate[i, rows, :].astype(F32)
                pre_up = d_up[i, rows, :].astype(F32)
            back = nt(outs[...], wd[i])
            sig = 0.5 * jnp.tanh(0.5 * pre_gate) + 0.5
            silu = pre_gate * sig
            hidden = silu * pre_up
            sums = jnp.where(lane == i, jnp.sum(hidden * back, axis=1, keepdims=True), sums)
            back = share * back
            d_up[i, rows, :] = (back * silu).astype(BF16)
            d_gate[i, rows, :] = (back * pre_up * (sig + silu * (1.0 - sig))).astype(BF16)
            hid[i, rows, :] = (share * hidden).astype(BF16)
        grads[owner] = sums.T[:8, :]
        out = sum(nn(hid[i, rows, :], wd[i]) for i in range(local))
        stage[slot, :t, :] = out.astype(BF16)
        local_start(stage.at[slot, pl.ds(0, t)], y_all.at[owner], y_sems.at[slot])

    def y_wait(slot):
        pltpu.make_async_copy(stage.at[slot, pl.ds(0, t)], y_all.at[0], y_sems.at[slot]).wait()

    def side_row(away, k):
        return at_pos((at.p + n + (2 * k - 1) * away) % n, n)

    def both(away, work):
        def one(k, _):
            work(side_row(away, k), k)
            return 0

        lax.fori_loop(0, 2, one, 0)

    old = functools.partial(pass_two, fresh=False)
    new = functools.partial(pass_two, fresh=True)
    steps = dims.steps
    load_gate.wait()
    load_up.wait()
    pass_one(at.e)
    for s in range(1, steps):
        c_ring.start(s)
        x_ring.start(s)
        if s == 1:
            both(1, lambda owner, k: pass_one(owner))
            continue
        if s == 2:
            downs.recv(0)
            downs.start(2, remote(piece(at.far), piece(at.far), wd_sems, 2, "hid", at.sib))
            if not big:
                load_g.wait()
            own_down.wait()
            downs.recv(1)
            downs.recv(2)
            both(2, new)
            for slot in (0, 1):
                y_wait(slot)
            both(1, old)
            y_wait(0)
            old(at.e, 0)
            continue
        for slot in (0, 1):
            y_wait(slot)
        both(s, new)
    c_ring.recv_last()
    x_ring.recv_last()
    for slot in (0, 1):
        y_wait(slot)
    new(side_row(steps, 1), 0)
    y_wait(0)

    small = Sent()
    for k, peer in enumerate(others):
        small.start(k, remote(grads.at[peer], gate_grad.at[at.e], grad_sems, k, "exp", peer))
    own_small = local_start(grads.at[at.e], gate_grad.at[at.e], local_sems.at[5])

    sources = (hid, d_gate, d_up)
    jobs = [(kind, i) for kind in range(3) for i in range(local)]
    crossing = dims.crossing
    flights, kept = {}, {}

    def spare(k):
        return wd.at[k // 4, pl.ds(k % 4 * ff4, ff4)]

    downs.done()
    pl.semaphore_signal(free_sem, inc=1, device_id={"hid": at.sib}, device_id_type=MESH)
    pl.semaphore_wait(free_sem, 1)


    def job(k):
        kind, i = jobs[k]
        slot = k % 2
        if k >= 2:
            for copy in flights[k - 2]:
                copy.wait_send()
            for copy in kept[k - 2]:
                copy.wait()
        left = sources[kind]
        for f in range(ff // 256):
            units = slice(f * 256, (f + 1) * 256)
            if big:
                def add(r, total, units=units):
                    right = g_row(r) if kind == 0 else x_row(r)
                    return total + tn(left[i, rows_at(r, t), units], right[...])

                value = lax.fori_loop(0, n, add, jnp.zeros((256, d), F32))
            else:
                right = g_near.reshape(n * t, d) if kind == 0 else xs
                value = tn(left[i, :, units], right[...])
            stage[slot, units, :] = value.astype(BF16)
        flights[k], kept[k] = [], []
        if k < crossing:
            far_room = ((at.diag, at.far), (spare(2 * k + 1), spare(2 * k)))
        else:
            far_room = ((at.diag, at.far), (sib_far.at[k - crossing], own_far.at[k - crossing]))
        for which, ((there, here), (sib_spot, own_spot)) in enumerate(
            (((at.sib, at.h), (sib_out.at[k], own_out.at[k])), far_room)
        ):
            copy = remote(stage.at[slot, rows_at(there, ff4)], sib_spot, job_sems, 2 * k + which, "hid", at.sib)
            copy.start()
            flights[k].append(copy)
            kept[k].append(
                local_start(stage.at[slot, rows_at(here, ff4)], own_spot, keep_sems.at[2 * slot + which])
            )

    fars = Sent()

    def cross(k):
        flights[k][1].wait_recv()
        if k >= done_jobs - 2:
            kept[k].pop().wait()
        one, two = spare(2 * k), spare(2 * k + 1)
        one[...] = (one[...].astype(F32) + two[...].astype(F32)).astype(BF16)
        fars.start(k, remote(one, far_out.at[k], far_sems, k, "hid", at.far))

    def input_grad(owner):
        rows = rows_at(owner, t)
        return sum(nt(d_gate[i, rows, :], wg[i]) + nt(d_up[i, rows, :], wu[i]) for i in range(local))

    sums = RingSum(at, send, recv, t, sum_sems)
    done_jobs = 0
    crossed = 0
    for s in range(steps):
        sums.put(s, lambda side, owner: input_grad(owner))
        sums.go(s)
        while crossed < min(crossing, done_jobs):
            cross(crossed)
            crossed += 1
        until = min(len(jobs), (len(jobs) * (2 * s + 1) + 2 * steps - 2) // (2 * steps - 1))
        while done_jobs < until:
            job(done_jobs)
            done_jobs += 1
    while crossed < crossing:
        cross(crossed)
        crossed += 1
    dx[...] = input_grad(at.e)
    sums.arrive_last()
    for rows in split_parts(t):
        dx[rows, :] = dx[rows, :] + sums.total(rows)

    for k in range(len(others)):
        small.recv(k)
    own_small.wait()
    for k in range(len(jobs)):
        flights[k][0].wait_recv()
        if k >= crossing:
            flights[k][1].wait_recv()
    for k in range(len(jobs) - 2, len(jobs)):
        for copy in flights[k]:
            copy.wait_send()
        for copy in kept[k]:
            copy.wait()
    for k in range(crossing):
        fars.recv(k)
    for group in (x_ring, c_ring, downs, small, sums, fars):
        group.done()


def back_kernel(
    dims, big,
    dx, gate_grad, gates, kept, resid, normed_two, g_all, x, ws_in, qkv_in, mixed_in, normed_in, cosine_in, sine_in, probs_in,
    y_all, own_in, sib_in,
    layer, in_grad, small_one, small_two, att_grad, far_rest,
    ws, qkv, mixed, normed, cosine, sine, probs, x_own, g_own, resid_grad, rows_all, mixed_grad, d_query, d_key, d_value,
    d_qkv, w_grad, part, came, mid, came_far, y_rows, y_send, y_recv, w_send, w_recv, out_rows, in_rows, sum_a, sum_b,
    cut_send, cut_recv, rest,
    row_sems, y_sems, w_sems, hid_sems, in_sems, layer_sems, small_sems, cut_sems, far_sems, local_sems, load_sems,
):
    at = Place(dims.n)
    n, t, d, kv, shard = dims.n, dims.quarter, dims.d, dims.kc, dims.shard
    q4 = d // 4
    others = tuple((at.e + k) % n for k in range(1, n))
    pairs = [
        (ws_in, ws), (g_all.at[at.e], g_own), (own_in, rest.at[0]), (sib_in, rest.at[1]), (qkv_in, qkv),
        (mixed_in, mixed), (normed_in, normed), (cosine_in, cosine), (sine_in, sine), (x.at[rows_at(at.h, t)], x_own),
    ]
    if not big:
        pairs.append((y_all, y_rows))
    loads = [local_start(src, dst, load_sems.at[k]) for k, (src, dst) in enumerate(pairs)]
    for j in range(4):
        span = pl.ds(0, (j + 1) * t)
        loads.append(local_start(probs_in.at[j, :, span], probs.at[j, :, span], load_sems.at[11 + j]))
    greet(others, (at.sib, at.far, at.diag))
    loads[0].wait()
    loads[1].wait()

    slab = ws[:, dims.slab_at :]
    gains = gain_rows(slab, dims.experts)
    spread_shape = (n * 8, LANES)
    sub, lane = iota(spread_shape, 0), iota(spread_shape, 1)
    spread = (
        (sub // 8 == lane // dims.local) & (sub % 8 == lane % dims.local) & (lane < dims.experts)
    ).astype(F32)
    gg = tn_exact(gate_grad[...], spread) * kept[...]
    gate = gates[...]
    logit_grad = (gate * (gg - jnp.sum(gate * gg, axis=1, keepdims=True))).astype(BF16)
    gain_two = jnp.zeros((1, d), F32)
    rows = Sent()
    for c, half in enumerate(split_parts(t)):
        lg = logit_grad[half.start : half.start + half.size, :]
        normed_grad = dx[half, :] + nt(lg, slab)
        inputs = resid[half, :]
        scale = rms(inputs)
        gain_two = gain_two + jnp.sum(normed_grad * inputs * scale, axis=0, keepdims=True)
        weighted = normed_grad * gains[1:2, :]
        value = (
            g_own[half, :].astype(F32) + scale * weighted
            - inputs * (scale * scale * scale) * jnp.mean(weighted * inputs, axis=-1, keepdims=True)
        )
        resid_grad[half, :] = value
        here = pl.ds(pl.multiple_of(at.h * t + half.start, 16), half.size)
        rows_all[here, :] = value.astype(BF16)
        rows.start(("far", c), remote(rows_all.at[here], rows_all.at[here], row_sems, c, "hid", at.far))
        rows.start(("sib", c), remote(rows_all.at[here], rows_all.at[here], row_sems, 2 + c, "hid", at.sib))

    for load in loads[2:]:
        load.wait()
    router_rows = dims.experts
    small_rows = router_rows + 8
    sum_a[0, :router_rows, :] = tn(logit_grad, normed_two[...])[:router_rows, :]
    sum_a[0, router_rows:, :] = jnp.broadcast_to(gain_two, (8, d))

    def add_rest(k, _):
        rest[0, k] = (rest[0, k].astype(F32) + rest[1, k].astype(F32)).astype(BF16)
        return 0

    lax.fori_loop(0, dims.jobs - dims.crossing, add_rest, 0)

    y_sum = RingSum(at, y_send, y_recv, t, y_sems)

    def y_row(owner):
        if not big:
            return y_rows.at[owner]
        local_start(y_all.at[owner], y_rows.at[0], local_sems.at[5]).wait()
        return y_rows.at[0]

    def y_step(s):
        y_sum.put(s, lambda side, owner: y_row(owner)[...].astype(F32))
        y_sum.go(s)

    y_step(0)
    wo = ws.at[:, pl.ds(dims.attn_cols, dims.qc)]

    def project(quarter):
        block = rows_at(quarter, t)
        mixed_grad[block, :] = nn(rows_all[block, :], wo[...]).astype(BF16)

    project(at.h)
    rows.recv(("sib", 0))
    rows.recv(("sib", 1))
    project(at.sib)
    for c in (0, 1):
        rows.recv(("far", c))
        here = pl.ds(pl.multiple_of(at.far * t + c * (t // 2), 16), t // 2)
        rows.start(("on", c), remote(rows_all.at[here], rows_all.at[here], row_sems, 4 + c, "hid", at.sib))
    project(at.far)
    fars = Sent()
    fars.start(0, remote(rest.at[0], far_rest, far_sems, 0, "hid", at.far))
    smalls = Sent()
    smalls.start(0, remote(sum_a.at[0], sum_a.at[1], small_sems, 0, "hid", at.sib))
    rows.recv(("on", 0))
    rows.recv(("on", 1))
    project(at.diag)

    d_key[...] = jnp.zeros_like(d_key)
    d_value[...] = jnp.zeros_like(d_value)
    cuts = Sent()
    y_at = 1
    for j in range(4):
        block = pl.ds(j * t, t)
        keys = (j + 1) * t
        for head in range(dims.heads):
            key_at = head // dims.group * HEAD_DIM
            spot = slice(key_at, key_at + HEAD_DIM)
            query = qkv[block, head * HEAD_DIM : (head + 1) * HEAD_DIM]
            key = qkv[:keys, dims.qc + key_at : dims.qc + key_at + HEAD_DIM]
            value = qkv[:keys, dims.qc + kv + key_at : dims.qc + kv + key_at + HEAD_DIM]
            out_grad = mixed_grad[block, head * HEAD_DIM : (head + 1) * HEAD_DIM]
            share = probs[j, head, :keys, :]
            exact = share.astype(F32)
            prob_grad = nt(value, out_grad)
            inner = jnp.sum(exact * prob_grad, axis=0, keepdims=True)
            score_grad = (exact * (prob_grad - inner)).astype(BF16)
            d_query[block, head * HEAD_DIM : (head + 1) * HEAD_DIM] = tn(score_grad, key) * HEAD_DIM**-0.5
            d_key[:keys, spot] += nn(score_grad, query)
            d_value[:keys, spot] += nn(share, out_grad)
        if y_at < dims.steps:
            y_step(y_at)
            y_at += 1
        if j == 0:
            smalls.recv(0)
            sum_a[2] = sum_a[0] + sum_a[1]
            smalls.start(1, remote(sum_a.at[2], sum_a.at[3], small_sems, 1, "hid", at.far))
        if j == 2:
            smalls.recv(1)
            sum_a[1] = sum_a[2] + sum_a[3]
            for owner in range(n):
                cut_send[owner, :small_rows] = sum_a[1, :, owner * shard : (owner + 1) * shard]
            early = pl.ds(0, small_rows)
            for k, peer in enumerate(others):
                cuts.start(
                    k, remote(cut_send.at[peer, early], cut_recv.at[at.e, early], cut_sems, k, "exp", peer)
                )
            own_cut = local_start(cut_send.at[at.e, early], cut_recv.at[at.e, early], local_sems.at[0])
    while y_at < dims.steps:
        y_step(y_at)
        y_at += 1

    repeat = (dims.qc + kv) // LANES
    sums = Sent()
    for k, quarter in enumerate((at.diag, at.far, at.sib, at.h)):
        block = rows_at(quarter, t)
        raw = jnp.concatenate([d_query[block, :], d_key[block, :]], axis=1)
        turned = raw * jnp.tile(cosine[block, :], (1, repeat)) - swap_halves(raw) * jnp.tile(
            sine[block, :], (1, repeat)
        )
        d_qkv[block, : dims.qc + kv] = turned.astype(BF16)
        d_qkv[block, dims.qc + kv :] = d_value[block, :].astype(BF16)
        part[quarter] = nt(d_qkv[block, :], ws[:, : dims.attn_cols]).astype(BF16)
        if k == 0:
            sums.start(0, remote(part.at[at.diag], came.at[1], hid_sems, 0, "hid", at.sib))
        if k == 1:
            sums.recv(0)
            mid[...] = (part[at.far].astype(F32) + came[1].astype(F32)).astype(BF16)
            sums.start(2, remote(mid, came_far, hid_sems, 2, "hid", at.far))
        if k == 2:
            sums.start(1, remote(part.at[at.sib], came.at[0], hid_sems, 1, "hid", at.sib))

    def weight_cols(c, _):
        cols = rows_at(c, 256)
        w_grad[cols, : dims.attn_cols] = tn(normed[:, cols], d_qkv[...])
        w_grad[cols, dims.attn_cols :] = tn(rows_all[:, cols], mixed[...])
        return 0

    lax.fori_loop(0, d // 256, weight_cols, 0)
    w_sum = RingSum(at, w_send, w_recv, shard, w_sems)

    def w_step(s):
        w_sum.put(s, lambda side, owner: w_grad[rows_at(owner, shard), :])
        w_sum.go(s)

    w_step(0)
    y_sum.arrive_last()
    y_own = y_row(at.e)
    for half in split_parts(t):
        out_rows[half, :] = (resid[half, :] + y_own[half].astype(F32) + y_sum.total(half)).astype(BF16)
    layers = Sent()
    sums.recv(1)
    sums.recv(2)
    gain_one = jnp.zeros((1, d), F32)
    ins = Sent()
    own_rows = []
    for c, half in enumerate(split_parts(t)):
        grad = part[at.h, half].astype(F32) + came[0, half].astype(F32) + came_far[half].astype(F32)
        inputs = x_own[half, :].astype(F32)
        scale = rms(inputs)
        gain_one = gain_one + jnp.sum(grad * inputs * scale, axis=0, keepdims=True)
        weighted = grad * gains[0:1, :]
        in_rows[half, :] = (
            resid_grad[half, :] + scale * weighted
            - inputs * (scale * scale * scale) * jnp.mean(weighted * inputs, axis=-1, keepdims=True)
        ).astype(BF16)
        spot = in_grad.at[pl.ds(pl.multiple_of(at.h * t + half.start, 16), half.size)]
        ins.start(("far", c), remote(in_rows.at[half], spot, in_sems, c, "hid", at.far))
        ins.start(("sib", c), remote(in_rows.at[half], spot, in_sems, 2 + c, "hid", at.sib))
        own_rows.append(local_start(in_rows.at[half], spot, local_sems.at[1 + c]))
    sum_b[0] = jnp.broadcast_to(gain_one, (8, d))
    smalls.start(2, remote(sum_b.at[0], sum_b.at[1], small_sems, 2, "hid", at.sib))
    w_at = 1
    if w_at < dims.steps:
        w_step(w_at)
        w_at += 1
    smalls.recv(2)
    sum_b[2] = sum_b[0] + sum_b[1]
    smalls.start(3, remote(sum_b.at[2], sum_b.at[3], small_sems, 3, "hid", at.far))
    for k, peer in enumerate((at.sib, at.far, at.diag)):
        layers.start(
            k, remote(out_rows.at[:, rows_at(peer, q4)], layer.at[rows_at(at.h, t)], layer_sems, k, "hid", peer)
        )
    own_layer = local_start(out_rows.at[:, rows_at(at.h, q4)], layer.at[rows_at(at.h, t)], local_sems.at[3])
    for c in (0, 1):
        ins.recv(("far", c))
        far_rows = in_grad.at[pl.ds(pl.multiple_of(at.far * t + c * (t // 2), 16), t // 2)]
        ins.start(("on", c), remote(far_rows, far_rows, in_sems, 4 + c, "hid", at.sib))
    smalls.recv(3)
    sum_b[1] = sum_b[2] + sum_b[3]
    for owner in range(n):
        cut_send[owner, small_rows:] = sum_b[1, :, owner * shard : (owner + 1) * shard]
    late = pl.ds(small_rows, 8)
    for k, peer in enumerate(others):
        cuts.start(
            n + k, remote(cut_send.at[peer, late], cut_recv.at[at.e, late], cut_sems, n - 1 + k, "exp", peer)
        )
    own_cut_two = local_start(cut_send.at[at.e, late], cut_recv.at[at.e, late], local_sems.at[4])
    while w_at < dims.steps:
        w_step(w_at)
        w_at += 1
    w_sum.arrive_last()
    for rows_part in split_parts(shard):
        here = pl.ds(pl.multiple_of(at.e * shard + rows_part.start, 16), rows_part.size)
        att_grad[rows_part, :] = w_grad[here, :] + w_sum.total(rows_part)

    for k in range(n - 1):
        cuts.recv(k)
        cuts.recv(n + k)
    own_cut.wait()
    own_cut_two.wait()
    total = cut_recv[0]
    for k in range(1, n):
        total = total + cut_recv[k]
    small_one[...] = total[:small_rows]
    small_two[...] = total[small_rows:]

    fars.recv(0)
    for k in range(3):
        layers.recv(k)
    for c in (0, 1):
        ins.recv(("sib", c))
        ins.recv(("on", c))
        own_rows[c].wait()
    own_layer.wait()
    for group in (rows, smalls, y_sum, fars, cuts, sums, w_sum, ins, layers):
        group.done()


def out_kernel(
    dims,
    layer_in, in_rows, small_one, small_two, att, own_d, own_g, own_u, sib_d, sib_g, sib_u, far_d, far_g, far_g_rest, far_u,
    layer, in_grad, gain_one, gain_two, wq, wk, wv, wo, router, gate, up, down,
):
    layer[...] = layer_in[...]
    in_grad[...] = in_rows[...].astype(F32)

    def three(own, sib, far):
        return own[0].astype(F32) + sib[0].astype(F32) + far.astype(F32)

    first = pl.program_id(0) < dims.crossing - dims.local
    down[0] = three(own_d, sib_d, far_d[0])
    gate[0] = three(own_g, sib_g, jnp.where(first, far_g[0], far_g_rest[0])).T
    up[0] = three(own_u, sib_u, far_u[0]).T

    @pl.when(pl.program_id(0) == 0)
    def _():
        gain_one[...] = small_two[:1, :]
        gain_two[...] = small_one[dims.experts : dims.experts + 1, :]
        router[...] = small_one[: dims.experts, :]
        qc, kc = dims.qc, dims.kc
        wq[...] = att[:, :qc]
        wk[...] = att[:, qc : qc + kc]
        wv[...] = att[:, qc + kc : qc + 2 * kc]
        wo[...] = att[:, dims.attn_cols :]


def per_device(
    tokens,
    segment_ids,
    routes,
    norm1_gain,
    norm2_gain,
    query_weight,
    key_matrix,
    value_matrix,
    out_weight,
    router_weight,
    gate_weight,
    up_weight,
    down_weight,
    out_grad,
):
    n = lax.axis_size("exp")
    assert lax.axis_size("hid") == 4
    token_count, d = tokens.shape
    local, _, part_ff = gate_weight.shape
    experts = router_weight.shape[1]
    dims = Dims(
        n, token_count, d, experts, local, 4 * part_ff, routes.shape[1], query_weight.shape[1], key_matrix.shape[1]
    )
    t, ff, steps, shard = dims.quarter, dims.ff, dims.steps, dims.shard
    qc, kc = dims.qc, dims.kc

    vmem = pl.BlockSpec(memory_space=pltpu.VMEM)
    anywhere = pl.BlockSpec(memory_space=pl.ANY)
    shape = jax.ShapeDtypeStruct
    dma = pltpu.SemaphoreType.DMA

    (
        ws_all, wg_all, wu_all, wd_cast, g_all, probs, normed, qkv, mixed, cosine, sine, resid, normed_two, coef, gates, kept,
    ) = pl.pallas_call(
        functools.partial(front_kernel, dims),
        out_shape=[
            shape((d, dims.ws_cols), BF16),
            shape((local, d, ff), BF16),
            shape((local, d, ff), BF16),
            shape((local, part_ff, d), BF16),
            shape((n, t, d), BF16),
            shape((4, dims.heads, token_count, t), BF16),
            shape((token_count, d), BF16),
            shape((token_count, dims.attn_cols), BF16),
            shape((token_count, qc), BF16),
            shape((token_count, LANES), F32),
            shape((token_count, LANES), F32),
            shape((t, d), F32),
            shape((t, d), BF16),
            shape((experts, t), F32),
            shape((t, LANES), F32),
            shape((t, LANES), F32),
        ],
        in_specs=[vmem] * 10 + [anywhere] * 4,
        out_specs=[anywhere] * 6 + [vmem] * 10,
        scratch_shapes=[
            pltpu.VMEM((d, dims.ws_cols), BF16),
            pltpu.VMEM((2, local, d, part_ff), F32),
            pltpu.VMEM((2, local, d, part_ff), BF16),
            pltpu.VMEM((local, part_ff, d), F32),
            pltpu.VMEM((local, part_ff, d), BF16),
            pltpu.VMEM((8, token_count), jnp.int32),
            pltpu.VMEM((4, dims.heads, token_count, t), BF16),
            pltpu.VMEM((4, t, d), BF16),
            pltpu.VMEM((2, t, d), BF16),
            pltpu.VMEM((t, d), BF16),
            pltpu.VMEM((t, d), BF16),
            dma((2, 4 * steps)),
            dma((2, 4 * steps)),
            dma((2, 3)),
            dma((2, 3)),
            dma((2, 4 * local + 2)),
            dma((8,)),
            dma((4,)),
        ],
        compiler_params=pltpu.CompilerParams(
            collective_id=0, has_side_effects=True, vmem_limit_bytes=VMEM_LIMIT
        ),
    )(
        tokens, segment_ids, routes.T, query_weight, key_matrix, value_matrix, out_weight, router_weight.T,
        norm1_gain[None, :], norm2_gain[None, :], out_grad, gate_weight, up_weight, down_weight,
    )

    big = n * t * d * 2 > 6 * 2**20
    jobs, crossing = dims.jobs, dims.crossing
    (dx, y_all, gate_grad, own, sib, own_rest, sib_rest, far, _) = pl.pallas_call(
        functools.partial(moe_kernel, dims, big),
        out_shape=[
            shape((t, d), F32),
            shape((n, t, d), BF16),
            shape((n, 8, t), F32),
            shape((jobs, part_ff, d), BF16),
            shape((jobs, part_ff, d), BF16),
            shape((jobs - crossing, part_ff, d), BF16),
            shape((jobs - crossing, part_ff, d), BF16),
            shape((crossing, part_ff, d), BF16),
            shape((n * t if big else 16, d), BF16),
        ],
        in_specs=[vmem, vmem] + [anywhere] * 4,
        out_specs=[vmem] + [anywhere] * 8,
        scratch_shapes=[
            pltpu.VMEM((16 if big else n * t, d), BF16),
            pltpu.VMEM((1, 16, d) if big else (n, t, d), BF16),
            pltpu.VMEM((n, experts, t), F32),
            pltpu.VMEM((local, d, ff), BF16),
            pltpu.VMEM((local, d, ff), BF16),
            pltpu.VMEM((local, ff, d), BF16),
            pltpu.VMEM((local, n * t, ff), BF16),
            pltpu.VMEM((local, n * t, ff), BF16),
            pltpu.VMEM((local, n * t, ff), BF16),
            pltpu.VMEM((2, 2, t, d), BF16),
            pltpu.VMEM((2, steps, t, d), BF16),
            pltpu.VMEM((n, 8, t), F32),
            pltpu.VMEM((2, max(ff, t), d), BF16),
            pltpu.VMEM((t, d) if big else (16, LANES), BF16),
            pltpu.VMEM((t, d) if big else (16, LANES), BF16),
            dma((2, 4 * steps)),
            dma((2, 4 * steps)),
            dma((2, 4 * steps)),
            dma((2, n - 1)),
            dma((2, 3)),
            dma((2, 2 * jobs)),
            dma((2, crossing)),
            dma((6,)),
            dma((4,)),
            dma((2,)),
            pltpu.SemaphoreType.REGULAR,
        ],
        compiler_params=pltpu.CompilerParams(
            collective_id=1, has_side_effects=True, vmem_limit_bytes=VMEM_LIMIT
        ),
    )(normed_two, coef, g_all, wg_all, wu_all, wd_cast)

    small_rows = experts + 8
    att = dims.attn_cols + qc
    (layer, in_rows, small_one, small_two, att_grad, far_rest) = pl.pallas_call(
        functools.partial(back_kernel, dims, big),
        out_shape=[
            shape((token_count, d // 4), BF16),
            shape((token_count, d), BF16),
            shape((small_rows, shard), F32),
            shape((8, shard), F32),
            shape((shard, att), F32),
            shape((jobs - crossing, part_ff, d), BF16),
        ],
        in_specs=[vmem] * 6 + [anywhere] * 12,
        out_specs=[anywhere] * 2 + [vmem] * 3 + [anywhere],
        scratch_shapes=[
            pltpu.VMEM((d, dims.ws_cols), BF16),
            pltpu.VMEM((token_count, dims.attn_cols), BF16),
            pltpu.VMEM((token_count, qc), BF16),
            pltpu.VMEM((token_count, d), BF16),
            pltpu.VMEM((token_count, LANES), F32),
            pltpu.VMEM((token_count, LANES), F32),
            pltpu.VMEM((4, dims.heads, token_count, t), BF16),
            pltpu.VMEM((t, d), BF16),
            pltpu.VMEM((t, d), BF16),
            pltpu.VMEM((t, d), F32),
            pltpu.VMEM((token_count, d), BF16),
            pltpu.VMEM((token_count, qc), BF16),
            pltpu.VMEM((token_count, qc), F32),
            pltpu.VMEM((token_count, kc), F32),
            pltpu.VMEM((token_count, kc), F32),
            pltpu.VMEM((token_count, dims.attn_cols), BF16),
            pltpu.VMEM((d, att), F32),
            pltpu.VMEM((4, t, d), BF16),
            pltpu.VMEM((2, t, d), BF16),
            pltpu.VMEM((t, d), BF16),
            pltpu.VMEM((t, d), BF16),
            pltpu.VMEM((1 if big else n, t, d), BF16),
            pltpu.VMEM((2, 2, t, d), BF16),
            pltpu.VMEM((2, steps, t, d), BF16),
            pltpu.VMEM((2, 2, shard, att), BF16),
            pltpu.VMEM((2, steps, shard, att), BF16),
            pltpu.VMEM((t, d), BF16),
            pltpu.VMEM((t, d), BF16),
            pltpu.VMEM((4, small_rows, d), F32),
            pltpu.VMEM((4, 8, d), F32),
            pltpu.VMEM((n, small_rows + 8, shard), F32),
            pltpu.VMEM((n, small_rows + 8, shard), F32),
            pltpu.VMEM((2, jobs - crossing, part_ff, d), BF16),
            dma((2, 6)),
            dma((2, 4 * steps)),
            dma((2, 4 * steps)),
            dma((2, 3)),
            dma((2, 6)),
            dma((2, 3)),
            dma((2, 4)),
            dma((2, 2 * (n - 1))),
            dma((2, 1)),
            dma((6,)),
            dma((15,)),
        ],
        compiler_params=pltpu.CompilerParams(
            collective_id=2, has_side_effects=True, vmem_limit_bytes=VMEM_LIMIT
        ),
    )(
        dx, gate_grad.reshape(n * 8, t), gates, kept, resid, normed_two, g_all, tokens, ws_all, qkv, mixed, normed, cosine, sine,
        probs, y_all, own_rest, sib_rest,
    )

    rows = token_count // local

    def whole(shape_):
        return pl.BlockSpec(shape_, lambda i: (0,) * len(shape_))

    def matrix(index):
        return pl.BlockSpec((1, part_ff, d), lambda i: (index(i), 0, 0))

    (
        layer, in_grad, gain_one, gain_two, wq, wk, wv, wo, router, gate, up, down,
    ) = pl.pallas_call(
        functools.partial(out_kernel, dims),
        grid=(local,),
        out_shape=[
            shape((token_count, d // 4), BF16),
            shape((token_count, d), F32),
            shape((1, shard), F32),
            shape((1, shard), F32),
            shape((shard, qc), F32),
            shape((shard, kc), F32),
            shape((shard, kc), F32),
            shape((shard, qc), F32),
            shape((experts, shard), F32),
            shape((local, d, part_ff), F32),
            shape((local, d, part_ff), F32),
            shape((local, part_ff, d), F32),
        ],
        in_specs=[
            pl.BlockSpec((rows, d // 4), lambda i: (i, 0)),
            pl.BlockSpec((rows, d), lambda i: (i, 0)),
            whole((small_rows, shard)),
            whole((8, shard)),
            whole((shard, att)),
            matrix(lambda i: i),
            matrix(lambda i: local + i),
            matrix(lambda i: 2 * local + i),
            matrix(lambda i: i),
            matrix(lambda i: local + i),
            matrix(lambda i: 2 * local + i),
            matrix(lambda i: i),
            matrix(lambda i: jnp.minimum(local + i, crossing - 1)),
            matrix(lambda i: jnp.maximum(local + i - crossing, 0)),
            matrix(lambda i: 2 * local + i - crossing),
        ],
        out_specs=[
            pl.BlockSpec((rows, d // 4), lambda i: (i, 0)),
            pl.BlockSpec((rows, d), lambda i: (i, 0)),
            whole((1, shard)),
            whole((1, shard)),
            whole((shard, qc)),
            whole((shard, kc)),
            whole((shard, kc)),
            whole((shard, qc)),
            whole((experts, shard)),
            pl.BlockSpec((1, d, part_ff), lambda i: (i, 0, 0)),
            pl.BlockSpec((1, d, part_ff), lambda i: (i, 0, 0)),
            pl.BlockSpec((1, part_ff, d), lambda i: (i, 0, 0)),
        ],
        compiler_params=pltpu.CompilerParams(vmem_limit_bytes=VMEM_LIMIT),
    )(layer, in_rows, small_one, small_two, att_grad, own, own, own, sib, sib, sib, far, far, far_rest, far_rest)

    return (layer, in_grad, gain_one[0], gain_two[0], wq, wk, wv, wo, router.T, gate, up, down)


def solution(mesh):
    in_specs = (
        P("exp", None),
        P("exp", None),
        P("exp", None),
        P("exp"),
        P("exp"),
        P("exp", "hid"),
        P("exp", "hid"),
        P("exp", "hid"),
        P("exp", "hid"),
        P("exp", None),
        P("exp", None, "hid"),
        P("exp", None, "hid"),
        P("exp", "hid", None),
        P("exp", "hid"),
    )
    out_specs = (
        P("exp", "hid"),
        P("exp", None),
        P("exp"),
        P("exp"),
        P("exp", "hid"),
        P("exp", "hid"),
        P("exp", "hid"),
        P("exp", "hid"),
        P("exp", None),
        P("exp", None, "hid"),
        P("exp", None, "hid"),
        P("exp", "hid", None),
    )
    return jax.shard_map(
        per_device, mesh=mesh, in_specs=in_specs, out_specs=out_specs, check_vma=False
    )
```

```python
import functools
import math

import jax
import jax.numpy as jnp
from jax import lax
from jax.experimental import pallas as pl
from jax.experimental.pallas import tpu as pltpu
from jax.sharding import PartitionSpec as P

HEAD_DIM = 64
SEGS = 4
EPSILON = 1e-05
ROPE_BASE = 10000.0
NEG_FILL = -1e30
LANES = 128
MESH = pl.DeviceIdType.MESH
F32 = jnp.float32
BF16 = jnp.bfloat16
VMEM_LIMIT = 62 * 2**20


def nn(a, b):
    return lax.dot_general(a, b, (((1,), (0,)), ((), ())), preferred_element_type=F32)


def nt(a, b):
    return lax.dot_general(a, b, (((1,), (1,)), ((), ())), preferred_element_type=F32)


def tn(a, b):
    return lax.dot_general(a, b, (((0,), (0,)), ((), ())), preferred_element_type=F32)


def tn_exact(a, b):
    return lax.dot_general(
        a, b, (((0,), (0,)), ((), ())), preferred_element_type=F32, precision=lax.Precision.HIGHEST
    )


def iota(shape, dim):
    return lax.broadcasted_iota(jnp.int32, shape, dim)


def rows_at(index, size):
    return pl.ds(pl.multiple_of(index * size, size), size)


def pos_of(index, n):
    odd = index % 2
    return (1 - odd) * (index // 2) + odd * (n - 1 - index // 2)


def at_pos(pos, n):
    back = pos // (n // 2)
    return (1 - back) * (2 * pos) + back * (2 * (n - 1 - pos) + 1)


class Place:
    def __init__(self, n):
        self.n = n
        self.e = lax.axis_index("exp")
        self.h = lax.axis_index("hid")
        self.p = pos_of(self.e, n)
        self.right = self.ring(1)
        self.left = self.ring(-1)
        self.sib = self.h + 1 - 2 * (self.h % 2)
        self.far = (self.h + 2) % 4
        self.diag = (self.sib + 2) % 4

    def ring(self, away):
        return at_pos((self.p + self.n + away) % self.n, self.n)


def greet(exp_peers, hid_peers):
    barrier = pltpu.get_barrier_semaphore()
    for peer in exp_peers:
        pl.semaphore_signal(barrier, inc=1, device_id={"exp": peer}, device_id_type=MESH)
    for peer in hid_peers:
        pl.semaphore_signal(barrier, inc=1, device_id={"hid": peer}, device_id_type=MESH)
    pl.semaphore_wait(barrier, len(exp_peers) + len(hid_peers))


def remote(src, dst, sems, k, axis, to):
    return pltpu.make_async_remote_copy(
        src_ref=src,
        dst_ref=dst,
        send_sem=sems.at[0, k],
        recv_sem=sems.at[1, k],
        device_id={axis: to},
        device_id_type=MESH,
    )


class Sent:
    def __init__(self):
        self.copies = {}
        self.unsent = []

    def start(self, key, copy):
        copy.start()
        self.copies[key] = copy
        self.unsent.append(copy)

    def recv(self, key):
        self.copies[key].wait_recv()

    def done(self):
        for copy in self.unsent:
            copy.wait_send()
        self.unsent = []


class RingGather:
    def __init__(self, place, view, rows, sems):
        self.place, self.view, self.rows, self.sems = place, view, rows, sems
        self.steps = place.n // 2
        self.sent = Sent()

    def part(self, s, c):
        half = self.rows // 2
        for side in (0, 1):
            if s:
                self.sent.recv((s - 1, side, c))
            if s < self.steps - 1 or c == side:
                away, to = ((-s, self.place.right), (s, self.place.left))[side]
                block = self.view(self.place.ring(away), c * half, half)
                self.sent.start((s, side, c), remote(block, block, self.sems, 4 * s + 2 * side + c, "exp", to))

    def start(self, s):
        self.part(s, 0)
        self.part(s, 1)

    def recv_last(self):
        self.sent.recv((self.steps - 1, 0, 0))
        self.sent.recv((self.steps - 1, 1, 1))

    def done(self):
        self.sent.done()


class RingSum:
    def __init__(self, place, send, recv, rows, sems):
        self.place, self.send, self.recv, self.rows, self.sems = place, send, recv, rows, sems
        self.steps = place.n // 2
        self.copies = {}

    def owner(self, s, side):
        away = self.steps - s
        return self.place.ring(away if side == 0 else -away)

    def chunks(self, s):
        for c in (0, 1):
            for side in (0, 1):
                if s > 0 or c == side:
                    yield c, side

    def put(self, s, get):
        if s >= 2:
            for c, side in self.chunks(s - 2):
                self.copies[(s - 2, side, c)].wait_send()
        if s == 0:
            half = self.rows // 2
            terms = get(0, self.owner(0, 0)).astype(self.send.dtype)
            self.send[0, 0, pl.ds(0, half)] = terms[:half]
            self.send[1, 0, pl.ds(half, half)] = terms[half:]
            return
        for side in (0, 1):
            self.send[side, s % 2] = get(side, self.owner(s, side)).astype(self.send.dtype)

    def part(self, s, c):
        half = self.rows // 2
        rows = pl.ds(c * half, half)
        for side in (0, 1):
            if s == 0 and c != side:
                continue
            src = self.send.at[side, s % 2, rows]
            if s > 1 or (s == 1 and c == side):
                self.copies[(s - 1, side, c)].wait_recv()
                came = self.recv[side, s - 1, rows].astype(F32)
                src[...] = (src[...].astype(F32) + came).astype(src.dtype)
            to = self.place.left if side else self.place.right
            copy = remote(src, self.recv.at[side, s, rows], self.sems, 4 * s + 2 * side + c, "exp", to)
            copy.start()
            self.copies[(s, side, c)] = copy

    def go(self, s):
        self.part(s, 0)
        self.part(s, 1)

    def arrive_last(self):
        for c, side in self.chunks(self.steps - 1):
            self.copies[(self.steps - 1, side, c)].wait_recv()

    def total(self, part):
        return self.recv[0, self.steps - 1, part].astype(F32) + self.recv[1, self.steps - 1, part].astype(F32)

    def done(self):
        for s in range(self.steps - 2, self.steps):
            for c, side in self.chunks(s):
                self.copies[(s, side, c)].wait_send()


def local_start(src, dst, sem):
    copy = pltpu.make_async_copy(src, dst, sem)
    copy.start()
    return copy


def split_parts(count):
    return (pl.ds(0, count // 2), pl.ds(count // 2, count // 2))


def rms(values):
    return lax.rsqrt(jnp.mean(values * values, axis=-1, keepdims=True) + EPSILON)


def swap_halves(values):
    half = HEAD_DIM // 2
    width = values.shape[1]
    up = pltpu.roll(values, width - half, 1)
    down = pltpu.roll(values, half, 1)
    first = iota(values.shape, 1) % HEAD_DIM < half
    return jnp.where(first, up, down)


def gain_rows(slab, expert_count):
    pick = (iota((16, LANES), 1) == iota((16, LANES), 0) + expert_count).astype(BF16)
    return nt(pick, slab)


def bias_block(begin_row, first_row, key_count):
    shape = (key_count, begin_row.shape[1])
    keys = iota(shape, 0)
    seen = (keys >= begin_row) & (keys <= first_row + iota(shape, 1))
    return jnp.where(seen, 0.0, NEG_FILL)


class Dims:
    def __init__(self, n, token_count, width, expert_count, local_experts, ff, topk, qc, kc):
        self.n, self.tokens, self.d = n, token_count, width
        self.experts, self.local, self.ff, self.topk = expert_count, local_experts, ff, topk
        self.qc, self.kc = qc, kc
        self.quarter = token_count // 4
        self.shard = width // n
        self.capacity = token_count * topk * 5 // (4 * expert_count)
        self.attn_cols = qc + 2 * kc
        self.slab_at = 2 * qc + 2 * kc
        self.ws_cols = self.slab_at + LANES
        self.heads = qc // HEAD_DIM
        self.group = qc // kc
        self.part_ff = ff // 4
        self.steps = n // 2
        self.jobs = 3 * local_experts
        self.crossing = self.jobs * 7 // 12
        self.early = 2 * local_experts


def tall(row, count):
    return jnp.broadcast_to(row, (LANES, row.shape[1])).T[:, :count]


def front_kernel(
    dims,
    x, seg, routes, wq, wk, wv, wo, router, gain_one, gain_two, g, wg, wu, wd,
    ws_out, wg_all, wd_all, wu_cast, g_all, probs_out, normed, qkv, mixed, cosine, sine, resid, normed_two, coef, gates, kept,
    ws_all, wide, cast, wide_down, cast_down, begin, probs, part, came, mid, came_far,
    ws_sems, g_sems, hid_sems, swap_sems, weight_sems, local_sems, probs_sems, own_sems,
):
    at = Place(dims.n)
    t, d, ff4, shard, tokens = dims.quarter, dims.d, dims.part_ff, dims.shard, dims.tokens
    q4 = d // 4
    kv = dims.kc
    loads = [local_start(ref, wide.at[k], local_sems.at[k]) for k, ref in enumerate((wg, wu))]
    load_down = local_start(wd, wide_down, local_sems.at[2])

    mine = rows_at(at.e, shard)
    at_col = 0
    for ref in (wq, wk, wv, wo):
        ws_all[mine, at_col : at_col + ref.shape[1]] = ref[...].astype(BF16)
        at_col += ref.shape[1]
    lane = iota((shard, LANES), 1)
    slab = jnp.concatenate([router[...], jnp.zeros((LANES - dims.experts, shard), F32)], axis=0).T
    slab = jnp.where(lane == dims.experts, tall(gain_one[...], LANES), slab)
    slab = jnp.where(lane == dims.experts + 1, tall(gain_two[...], LANES), slab)
    ws_all[mine, dims.slab_at :] = slab.astype(BF16)

    greet((at.right, at.left), (at.sib, at.far, at.diag))
    ring = RingGather(at, lambda o, f, s: ws_all.at[pl.ds(pl.multiple_of(o * shard + f, 16), s)], shard, ws_sems)
    ring.start(0)

    swaps = Sent()
    for k, peer in enumerate((at.sib, at.far, at.diag)):
        swaps.start(
            k, remote(g.at[rows_at(peer, t)], g_all.at[at.e, :, rows_at(at.h, q4)], swap_sems, k, "hid", peer)
        )
    g_own = local_start(g.at[rows_at(at.h, t)], g_all.at[at.e, :, rows_at(at.h, q4)], local_sems.at[3])

    moves = Sent()
    kept_own = []
    units = [(0, i) for i in range(dims.local)] + [(1, i) for i in range(dims.local)]
    lot = (5 * len(units) + 7) // 8

    def source(u):
        k, i = units[u]
        return cast_down.at[i] if k else cast.at[0, i]

    def spot(u, owner):
        k, i = units[u]
        return wd_all.at[i, rows_at(owner, ff4), :] if k else wg_all.at[i, :, rows_at(owner, ff4)]

    def send_unit(u):
        moves.start(("far", u), remote(source(u), spot(u, at.h), weight_sems, u, "hid", at.far))

    def pass_on(u):
        moves.recv(("far", u))
        block = spot(u, at.far)
        moves.start(("on", u), remote(block, block, weight_sems, len(units) + u, "hid", at.sib))

    loads[0].wait()
    cast[0] = wide[0].astype(BF16)
    for u in range(min(lot, dims.local)):
        send_unit(u)
    load_down.wait()
    cast_down[...] = wide_down[...].astype(BF16)
    for u in range(min(lot, dims.local), lot):
        send_unit(u)
    for u in range(len(units)):
        moves.start(
            ("sib", u), remote(source(u), spot(u, at.h), weight_sems, 2 * len(units) + u, "hid", at.sib)
        )
        kept_own.append(local_start(source(u), spot(u, at.h), own_sems.at[u]))

    ring.start(1)
    for k in range(3):
        swaps.recv(k)
    g_own.wait()
    g_ring = RingGather(at, lambda o, f, s: g_all.at[o, pl.ds(f, s)], t, g_sems)

    counts = [jnp.sum((seg[...] == k).astype(F32), axis=1, keepdims=True) for k in range(SEGS)]
    first = jnp.zeros((1, tokens), F32)
    total = jnp.zeros((1, 1), F32)
    for k in range(SEGS):
        first = first + jnp.where(seg[...] == k, total, 0.0)
        total = total + counts[k]
    begin[...] = jnp.broadcast_to(first, (8, tokens)).astype(jnp.int32)
    lane = iota((1, LANES), 1)
    half = HEAD_DIM // 2
    freqs = jnp.exp((lane % half).astype(F32) * (-math.log(ROPE_BASE) / half))
    positions = iota((1, tokens), 1).astype(F32) - first

    def table(j):
        rows = pl.ds(j * t, t)
        angles = tall(positions[:, j * t : (j + 1) * t], LANES) * freqs
        cosine[rows, :] = jnp.cos(angles)
        sine[rows, :] = jnp.where(lane % HEAD_DIM < half, -1.0, 1.0) * jnp.sin(angles)

    todo = [functools.partial(table, j) for j in range(4)]

    for s in range(2, dims.steps):
        if todo:
            todo.pop(0)()
            todo.pop(0)()
        ring.start(s)
    for job in todo:
        job()
    loads[1].wait()
    cast[1] = wide[1].astype(BF16)
    saves = [local_start(cast.at[1], wu_cast, local_sems.at[4])]
    ring.recv_last()
    out_ws = local_start(ws_all, ws_out, local_sems.at[6])

    g_ring.start(0)

    slab = ws_all[:, dims.slab_at :]
    gains = gain_rows(slab, dims.experts)
    repeat = (dims.qc + kv) // LANES
    for j in range(4):
        rows = pl.ds(j * t, t)
        values = x[rows, :].astype(F32)
        block = (values * rms(values) * gains[0:1, :]).astype(BF16)
        normed[rows, :] = block
        raw = nn(block, ws_all[:, : dims.attn_cols])
        turned = raw[:, : dims.qc + kv]
        turned = turned * jnp.tile(cosine[rows, :], (1, repeat)) + swap_halves(turned) * jnp.tile(
            sine[rows, :], (1, repeat)
        )
        queries = turned[:, : dims.qc].astype(BF16) * jnp.asarray(HEAD_DIM**-0.5, BF16)
        qkv[rows, : dims.qc] = queries
        qkv[rows, dims.qc : dims.qc + kv] = turned[:, dims.qc :].astype(BF16)
        qkv[rows, dims.qc + kv :] = raw[:, dims.qc + kv :].astype(BF16)

    for j in range(4):
        rows = pl.ds(j * t, t)
        keys = (j + 1) * t
        bias = bias_block(begin[:1, j * t : (j + 1) * t], j * t, keys)
        for head in range(dims.heads):
            key_at = dims.qc + head // dims.group * HEAD_DIM
            query = qkv[rows, head * HEAD_DIM : (head + 1) * HEAD_DIM]
            key = qkv[:keys, key_at : key_at + HEAD_DIM]
            value = qkv[:keys, key_at + kv : key_at + kv + HEAD_DIM]
            scores = nt(key, query) + bias
            powers = jnp.exp(scores - jnp.max(scores, axis=0, keepdims=True))
            share = (powers * (1.0 / jnp.sum(powers, axis=0, keepdims=True))).astype(BF16)
            probs[j, head, :keys, :] = share
            mixed[rows, head * HEAD_DIM : (head + 1) * HEAD_DIM] = tn(value, share).T.astype(BF16)
        saves.append(
            local_start(probs.at[j, :, pl.ds(0, keys)], probs_out.at[j, :, pl.ds(0, keys)], probs_sems.at[j])
        )

    g_ring.start(1)
    wo_all = ws_all.at[:, pl.ds(dims.attn_cols, dims.qc)]
    sums = Sent()
    for k, quarter in enumerate((at.diag, at.far, at.sib, at.h)):
        part[quarter] = nt(mixed[rows_at(quarter, t), :], wo_all[...]).astype(BF16)
        if k == 0:
            sums.start(0, remote(part.at[at.diag], came.at[1], hid_sems, 0, "hid", at.sib))
        if k == 1:
            sums.recv(0)
            for c, rows in enumerate(split_parts(t)):
                mid[rows, :] = (part[at.far, rows].astype(F32) + came[1, rows].astype(F32)).astype(BF16)
                sums.start(2 + c, remote(mid.at[rows], came_far.at[rows], hid_sems, 2 + c, "hid", at.far))
        if k == 2:
            sums.start(1, remote(part.at[at.sib], came.at[0], hid_sems, 1, "hid", at.sib))
    g_ring.start(2)
    for u in range(lot):
        pass_on(u)

    expert = iota((dims.experts, tokens), 0)
    chosen = jnp.zeros((dims.experts, tokens), F32)
    for k in range(dims.topk):
        chosen = chosen + (routes[k : k + 1, :] == expert).astype(F32)
    earlier = (iota((tokens, t), 0) < iota((tokens, t), 1) + at.h * t).astype(BF16)
    rank = nn(chosen.astype(BF16), earlier)
    expert = iota((dims.experts, t), 0)
    own_routes = routes[:, rows_at(at.h, t)]
    mine = jnp.zeros((dims.experts, t), F32)
    for k in range(dims.topk):
        mine = mine + (own_routes[k : k + 1, :] == expert).astype(F32)
    keep = mine * (rank < dims.capacity).astype(F32)
    rest = jnp.zeros((LANES - dims.experts, t), F32)
    mine = jnp.concatenate([mine, rest], axis=0).T
    keep = jnp.concatenate([keep, rest], axis=0).T
    kept[...] = keep

    sums.recv(1)
    for c, rows in enumerate(split_parts(t)):
        sums.recv(2 + c)
        first = pl.ds(pl.multiple_of(at.h * t + rows.start, 16), rows.size)
        values = (
            part[at.h, rows].astype(F32) + came[0, rows].astype(F32) + came_far[rows].astype(F32)
            + x[first, :].astype(F32)
        )
        resid[rows, :] = values
        normed_two[rows, :] = (values * rms(values) * gains[1:2, :]).astype(BF16)
    for u in range(lot, len(units)):
        send_unit(u)
    logits = nn(normed_two[...], slab)
    for s in range(3, dims.steps):
        g_ring.start(s)
    picked = jnp.where(mine > 0, logits, NEG_FILL)
    powers = jnp.exp(picked - jnp.max(picked, axis=1, keepdims=True)) * mine
    gate = powers / jnp.sum(powers, axis=1, keepdims=True)
    gates[...] = gate
    coef[...] = (gate * keep).T[: dims.experts, :]

    for u in range(lot, len(units)):
        pass_on(u)
    for u in range(len(units)):
        moves.recv(("sib", u))
        kept_own[u].wait()
    for u in range(len(units)):
        moves.recv(("on", u))
    g_ring.recv_last()
    for copy in saves:
        copy.wait()
    out_ws.wait()
    for group in (ring, g_ring, swaps, moves, sums):
        group.done()


def moe_kernel(
    dims, big,
    x_own, coef_own, g_all, wg_in, wd_in, wu_own,
    dx, y_all, gate_grad, own_out, sib_out, own_far, sib_far, far_out, x_far,
    x_near, g_near, coef, wg, wu, wd, d_gate, d_up, hid, send, recv, grads, stage, x_stage, g_stage,
    x_sems, c_sems, sum_sems, grad_sems, wd_sems, job_sems, far_sems, local_sems, keep_sems, y_sems, own_sems, free_sem,
):
    at = Place(dims.n)
    n, t, d, local, ff, ff4 = dims.n, dims.quarter, dims.d, dims.local, dims.ff, dims.part_ff
    others = tuple((at.e + k) % n for k in range(1, n))
    load_gate = local_start(wg_in, wg, local_sems.at[1])
    load_down = local_start(wd_in, wd, local_sems.at[2])
    if not big:
        load_g = local_start(g_all, g_near, local_sems.at[4])
    xs = x_far if big else x_near
    coef[at.e] = coef_own[...]
    if big:
        local_start(x_own, xs.at[rows_at(at.e, t)], local_sems.at[0]).wait()
    else:
        xs[rows_at(at.e, t), :] = x_own[...]
    greet(others, (at.sib, at.far))

    x_ring = RingGather(at, lambda o, f, s: xs.at[pl.ds(pl.multiple_of(o * t + f, 16), s)], t, x_sems)
    c_ring = RingGather(at, lambda o, f, s: coef.at[o, pl.ds(f, s)], dims.experts, c_sems)
    c_ring.start(0)
    x_ring.start(0)

    late = local

    def source(u):
        return wu_own.at[u]

    def spot(u, owner):
        return wu.at[u, :, rows_at(owner, ff4)]

    downs = Sent()
    kept_own = []
    lot = (late + 1) // 2

    def across(u):
        downs.start(("far", u), remote(source(u), spot(u, at.h), wd_sems, u, "hid", at.far))

    for u in range(lot):
        across(u)
    for u in range(late):
        downs.start(("sib", u), remote(source(u), spot(u, at.h), wd_sems, late + u, "hid", at.sib))
        kept_own.append(local_start(source(u), spot(u, at.h), own_sems.at[u]))

    def arrive(lot_units):
        for u in lot_units:
            downs.recv(("far", u))
            block = spot(u, at.far)
            downs.start(("on", u), remote(block, block, wd_sems, 2 * late + u, "hid", at.sib))
            if lot + u < late:
                across(lot + u)
        for u in lot_units:
            downs.recv(("sib", u))
            kept_own[u].wait()
            downs.recv(("on", u))

    def x_row(owner):
        if not big:
            return xs.at[rows_at(owner, t)]
        local_start(xs.at[rows_at(owner, t)], x_stage, local_sems.at[0]).wait()
        return x_stage

    def g_row(owner):
        if not big:
            return g_near.at[owner]
        local_start(g_all.at[owner], g_stage, local_sems.at[4]).wait()
        return g_stage

    lane = iota((t, LANES), 1)

    def gate_products(owner):
        rows = rows_at(owner, t)
        inputs = x_row(owner)
        for i in range(local):
            d_gate[i, rows, :] = nn(inputs[...], wg[i]).astype(BF16)

    def back_products(i):
        def one(r, _):
            hid[i, rows_at(r, t), :] = nt(g_row(r)[...], wd[i]).astype(BF16)
            return 0

        lax.fori_loop(0, n, one, 0)

    def work(owner, which, fresh):
        rows = rows_at(owner, t)
        inputs = x_row(owner)
        columns = jnp.concatenate([coef[owner], jnp.zeros((LANES - dims.experts, t), F32)], axis=0).T
        for i in which:
            share = jnp.sum(jnp.where(lane == at.e * local + i, columns, 0.0), axis=1, keepdims=True)
            pre_gate = nn(inputs[...], wg[i]) if fresh else d_gate[i, rows, :].astype(F32)
            pre_up = nn(inputs[...], wu[i])
            back = hid[i, rows, :].astype(F32)
            sig = 0.5 * jnp.tanh(0.5 * pre_gate) + 0.5
            silu = pre_gate * sig
            hidden = silu * pre_up
            own = jnp.sum(hidden * back, axis=1, keepdims=True)
            grads[owner, i : i + 1, :] = jnp.broadcast_to(own, (t, LANES)).T[:1, :]
            back = share * back
            d_up[i, rows, :] = (back * silu).astype(BF16)
            d_gate[i, rows, :] = (back * pre_up * (sig + silu * (1.0 - sig))).astype(BF16)
            hid[i, rows, :] = (share * hidden).astype(BF16)

    def layer_row(owner, slot):
        rows = rows_at(owner, t)
        stage[slot, :t, :] = sum(nn(hid[i, rows, :], wd[i]) for i in range(local)).astype(BF16)
        local_start(stage.at[slot, pl.ds(0, t)], y_all.at[owner], y_sems.at[slot])

    def y_wait(slot):
        pltpu.make_async_copy(stage.at[slot, pl.ds(0, t)], y_all.at[0], y_sems.at[slot]).wait()

    def side_row(away, k):
        return at_pos((at.p + n + (2 * k - 1) * away) % n, n)

    def both(away, do):
        def one(k, _):
            do(side_row(away, k), k)
            return 0

        lax.fori_loop(0, 2, one, 0)

    def near(which):
        def one(k, _):
            work(at_pos((at.p + n + k - 1) % n, n), which, False)
            return 0

        lax.fori_loop(0, 3, one, 0)

    steps = dims.steps
    load_gate.wait()
    gate_products(at.e)
    if not big:
        load_g.wait()
    load_down.wait()
    for i in range(local - 1):
        back_products(i)
    x_ring.part(1, 0)
    back_products(local - 1)
    x_ring.part(1, 1)
    c_ring.start(1)
    both(1, lambda owner, k: gate_products(owner))
    one, two = tuple(range(lot)), tuple(range(lot, local))
    arrive(one)
    for s in range(2, steps):
        x_ring.part(s, 0)
        if s == 2:
            near(one[:1])
        x_ring.part(s, 1)
        c_ring.start(s)
        if s == 2 and one[1:]:
            near(one[1:])
        both(s, lambda owner, k: gate_products(owner))
        both(s, lambda owner, k: work(owner, one, False))
    if two:
        arrive(two)
        near(two)
        for away in range(2, steps):
            both(away, lambda owner, k: work(owner, two, False))
    layer_row(at.e, 0)
    y_wait(0)
    for away in range(1, steps):
        both(away, layer_row)
        for slot in (0, 1):
            y_wait(slot)
    c_ring.recv_last()
    x_ring.recv_last()
    last = side_row(steps, 1)
    work(last, range(local), True)
    layer_row(last, 0)
    y_wait(0)

    small = Sent()
    for k, peer in enumerate(others):
        small.start(k, remote(grads.at[peer], gate_grad.at[at.e], grad_sems, k, "exp", peer))
    own_small = local_start(grads.at[at.e], gate_grad.at[at.e], local_sems.at[5])

    sources = (hid, d_gate, d_up)
    jobs = [(kind, i) for kind in range(3) for i in range(local)]
    crossing = dims.crossing
    flights, kept = {}, {}

    def spare(k):
        return wd.at[k // 4, pl.ds(k % 4 * ff4, ff4)]

    downs.done()
    pl.semaphore_signal(free_sem, inc=1, device_id={"hid": at.sib}, device_id_type=MESH)
    pl.semaphore_wait(free_sem, 1)


    def job(k):
        kind, i = jobs[k]
        slot = k % 2
        if k >= 2:
            for copy in flights[k - 2]:
                copy.wait_send()
            for copy in kept[k - 2]:
                copy.wait()
        left = sources[kind]
        for f in range(ff // 256):
            units = slice(f * 256, (f + 1) * 256)
            if big:
                def add(r, total, units=units):
                    right = g_row(r) if kind == 0 else x_row(r)
                    return total + tn(left[i, rows_at(r, t), units], right[...])

                value = lax.fori_loop(0, n, add, jnp.zeros((256, d), F32))
            else:
                right = g_near.reshape(n * t, d) if kind == 0 else xs
                value = tn(left[i, :, units], right[...])
            stage[slot, units, :] = value.astype(BF16)
        flights[k], kept[k] = [], []
        if k < crossing:
            far_room = ((at.diag, at.far), (spare(2 * k + 1), spare(2 * k)))
        else:
            far_room = ((at.diag, at.far), (sib_far.at[k - crossing], own_far.at[k - crossing]))
        for which, ((there, here), (sib_spot, own_spot)) in enumerate(
            (((at.sib, at.h), (sib_out.at[k], own_out.at[k])), far_room)
        ):
            copy = remote(stage.at[slot, rows_at(there, ff4)], sib_spot, job_sems, 2 * k + which, "hid", at.sib)
            copy.start()
            flights[k].append(copy)
            kept[k].append(
                local_start(stage.at[slot, rows_at(here, ff4)], own_spot, keep_sems.at[2 * slot + which])
            )

    fars = Sent()

    def cross(k):
        flights[k][1].wait_recv()
        if k >= done_jobs - 2:
            kept[k].pop().wait()
        one, two = spare(2 * k), spare(2 * k + 1)
        one[...] = (one[...].astype(F32) + two[...].astype(F32)).astype(BF16)
        fars.start(k, remote(one, far_out.at[k], far_sems, k, "hid", at.far))

    def input_grad(owner):
        rows = rows_at(owner, t)
        return sum(nt(d_gate[i, rows, :], wg[i]) + nt(d_up[i, rows, :], wu[i]) for i in range(local))

    sums = RingSum(at, send, recv, t, sum_sems)
    done_jobs = 0

    def jobs_until(count):
        nonlocal done_jobs
        while done_jobs < count:
            job(done_jobs)
            done_jobs += 1
            if 2 <= done_jobs <= crossing + 1:
                cross(done_jobs - 2)

    sums.put(0, lambda side, owner: input_grad(owner))
    sums.go(0)
    for s in range(1, steps):
        jobs_until(len(jobs) * (2 * s - 1) // (2 * steps - 1))
        sums.put(s, lambda side, owner: input_grad(owner))
        sums.part(s, 0)
        jobs_until(min(len(jobs), done_jobs + 1))
        sums.part(s, 1)
    jobs_until(len(jobs))
    if crossing >= len(jobs):
        cross(len(jobs) - 1)
    dx[...] = input_grad(at.e)
    sums.arrive_last()
    for rows in split_parts(t):
        dx[rows, :] = dx[rows, :] + sums.total(rows)

    for k in range(len(others)):
        small.recv(k)
    own_small.wait()
    for k in range(len(jobs)):
        flights[k][0].wait_recv()
        if k >= crossing:
            flights[k][1].wait_recv()
    for k in range(len(jobs) - 2, len(jobs)):
        for copy in flights[k]:
            copy.wait_send()
        for copy in kept[k]:
            copy.wait()
    for k in range(crossing):
        fars.recv(k)
    for group in (x_ring, c_ring, downs, small, sums, fars):
        group.done()


def back_kernel(
    dims, big,
    dx, gate_grad, gates, kept, resid, normed_two, g_all, x, ws_in, qkv_in, mixed_in, normed_in, cosine_in, sine_in, probs_in,
    y_all, own_in, sib_in,
    layer, in_grad, small_one, small_two, att_grad, far_rest,
    ws, qkv, mixed, normed, cosine, sine, probs, x_own, g_own, resid_grad, rows_all, mixed_grad, d_query, d_key, d_value,
    d_qkv, w_grad, part, came, mid, came_far, y_rows, y_send, y_recv, w_send, w_recv, out_rows, in_rows, sum_a,
    cut_send, cut_recv, rest,
    row_sems, y_sems, w_sems, hid_sems, in_sems, layer_sems, small_sems, cut_sems, far_sems, local_sems, load_sems,
):
    at = Place(dims.n)
    n, t, d, kv, shard = dims.n, dims.quarter, dims.d, dims.kc, dims.shard
    q4 = d // 4
    others = tuple((at.e + k) % n for k in range(1, n))
    pairs = [
        (ws_in, ws), (g_all.at[at.e], g_own), (own_in, rest.at[0]), (sib_in, rest.at[1]), (qkv_in, qkv),
        (mixed_in, mixed), (normed_in, normed), (cosine_in, cosine), (sine_in, sine), (x.at[rows_at(at.h, t)], x_own),
    ]
    if not big:
        pairs.append((y_all, y_rows))
    loads = [local_start(src, dst, load_sems.at[k]) for k, (src, dst) in enumerate(pairs)]
    for j in range(4):
        span = pl.ds(0, (j + 1) * t)
        loads.append(local_start(probs_in.at[j, :, span], probs.at[j, :, span], load_sems.at[11 + j]))
    greet(others, (at.sib, at.far, at.diag))
    loads[0].wait()
    loads[1].wait()

    slab = ws[:, dims.slab_at :]
    gains = gain_rows(slab, dims.experts)
    spread_shape = (n * 8, LANES)
    sub, lane = iota(spread_shape, 0), iota(spread_shape, 1)
    spread = (
        (sub // 8 == lane // dims.local) & (sub % 8 == lane % dims.local) & (lane < dims.experts)
    ).astype(F32)
    gg = tn_exact(gate_grad[...], spread) * kept[...]
    gate = gates[...]
    logit_grad = (gate * (gg - jnp.sum(gate * gg, axis=1, keepdims=True))).astype(BF16)
    gain_two = jnp.zeros((1, d), F32)
    rows = Sent()
    for c, half in enumerate(split_parts(t)):
        lg = logit_grad[half.start : half.start + half.size, :]
        normed_grad = dx[half, :] + nt(lg, slab)
        inputs = resid[half, :]
        scale = rms(inputs)
        gain_two = gain_two + jnp.sum(normed_grad * inputs * scale, axis=0, keepdims=True)
        weighted = normed_grad * gains[1:2, :]
        value = (
            g_own[half, :].astype(F32) + scale * weighted
            - inputs * (scale * scale * scale) * jnp.mean(weighted * inputs, axis=-1, keepdims=True)
        )
        resid_grad[half, :] = value
        here = pl.ds(pl.multiple_of(at.h * t + half.start, 16), half.size)
        rows_all[here, :] = value.astype(BF16)
        rows.start(("far", c), remote(rows_all.at[here], rows_all.at[here], row_sems, c, "hid", at.far))
        rows.start(("sib", c), remote(rows_all.at[here], rows_all.at[here], row_sems, 2 + c, "hid", at.sib))

    for load in loads[2:]:
        load.wait()
    router_rows = dims.experts
    small_rows = router_rows + 8
    router_part = tn(logit_grad, normed_two[...])
    for owner in range(n):
        cols = slice(owner * shard, (owner + 1) * shard)
        cut_send[owner, :router_rows] = router_part[:router_rows, cols]
        cut_send[owner, router_rows:small_rows] = jnp.broadcast_to(gain_two[:, cols], (8, shard))

    def add_rest(k, _):
        rest[0, k] = (rest[0, k].astype(F32) + rest[1, k].astype(F32)).astype(BF16)
        return 0

    lax.fori_loop(0, dims.jobs - dims.crossing, add_rest, 0)

    y_sum = RingSum(at, y_send, y_recv, t, y_sems)

    def y_row(owner):
        if not big:
            return y_rows.at[owner]
        local_start(y_all.at[owner], y_rows.at[0], local_sems.at[5]).wait()
        return y_rows.at[0]

    def y_step(s):
        y_sum.put(s, lambda side, owner: y_row(owner)[...].astype(F32))
        y_sum.go(s)

    y_step(0)
    wo = ws.at[:, pl.ds(dims.attn_cols, dims.qc)]

    def project(quarter):
        block = rows_at(quarter, t)
        mixed_grad[block, :] = nn(rows_all[block, :], wo[...]).astype(BF16)

    project(at.h)
    rows.recv(("sib", 0))
    rows.recv(("sib", 1))
    project(at.sib)
    for c in (0, 1):
        rows.recv(("far", c))
        here = pl.ds(pl.multiple_of(at.far * t + c * (t // 2), 16), t // 2)
        rows.start(("on", c), remote(rows_all.at[here], rows_all.at[here], row_sems, 4 + c, "hid", at.sib))
    project(at.far)
    fars = Sent()
    count = dims.jobs - dims.crossing

    def send_rest(k):
        fars.start(k, remote(rest.at[0, k], far_rest.at[k], far_sems, k, "hid", at.far))

    for k in range(count // 2):
        send_rest(k)
    rows.recv(("on", 0))
    rows.recv(("on", 1))
    project(at.diag)
    y_step(1)

    d_key[...] = jnp.zeros_like(d_key)
    d_value[...] = jnp.zeros_like(d_value)
    cuts = Sent()
    y_at = 2
    for j in range(4):
        block = pl.ds(j * t, t)
        keys = (j + 1) * t
        for head in range(dims.heads):
            key_at = head // dims.group * HEAD_DIM
            spot = slice(key_at, key_at + HEAD_DIM)
            query = qkv[block, head * HEAD_DIM : (head + 1) * HEAD_DIM]
            key = qkv[:keys, dims.qc + key_at : dims.qc + key_at + HEAD_DIM]
            value = qkv[:keys, dims.qc + kv + key_at : dims.qc + kv + key_at + HEAD_DIM]
            out_grad = mixed_grad[block, head * HEAD_DIM : (head + 1) * HEAD_DIM]
            share = probs[j, head, :keys, :]
            exact = share.astype(F32)
            prob_grad = nt(value, out_grad)
            inner = jnp.sum(exact * prob_grad, axis=0, keepdims=True)
            score_grad = (exact * (prob_grad - inner)).astype(BF16)
            d_query[block, head * HEAD_DIM : (head + 1) * HEAD_DIM] = tn(score_grad, key) * HEAD_DIM**-0.5
            d_key[:keys, spot] += nn(score_grad, query)
            d_value[:keys, spot] += nn(share, out_grad)
    early = pl.ds(0, small_rows)
    for k, peer in enumerate(others):
        cuts.start(k, remote(cut_send.at[peer, early], cut_recv.at[at.e, early], cut_sems, k, "exp", peer))
    own_cut = local_start(cut_send.at[at.e, early], cut_recv.at[at.e, early], local_sems.at[0])

    repeat = (dims.qc + kv) // LANES
    sums = Sent()
    for k, quarter in enumerate((at.diag, at.far, at.sib, at.h)):
        block = rows_at(quarter, t)
        raw = jnp.concatenate([d_query[block, :], d_key[block, :]], axis=1)
        turned = raw * jnp.tile(cosine[block, :], (1, repeat)) - swap_halves(raw) * jnp.tile(
            sine[block, :], (1, repeat)
        )
        d_qkv[block, : dims.qc + kv] = turned.astype(BF16)
        d_qkv[block, dims.qc + kv :] = d_value[block, :].astype(BF16)
        part[quarter] = nt(d_qkv[block, :], ws[:, : dims.attn_cols]).astype(BF16)
        if k == 0:
            sums.start(0, remote(part.at[at.diag], came.at[1], hid_sems, 0, "hid", at.sib))
        if k == 1:
            sums.recv(0)
            for c, half in enumerate(split_parts(t)):
                mid[half, :] = (part[at.far, half].astype(F32) + came[1, half].astype(F32)).astype(BF16)
                sums.start(2 + c, remote(mid.at[half], came_far.at[half], hid_sems, 2 + c, "hid", at.far))
        if k == 2:
            sums.start(1, remote(part.at[at.sib], came.at[0], hid_sems, 1, "hid", at.sib))

    def weight_cols(c, _):
        cols = rows_at(c, 256)
        w_grad[cols, : dims.attn_cols] = tn(normed[:, cols], d_qkv[...])
        w_grad[cols, dims.attn_cols :] = tn(rows_all[:, cols], mixed[...])
        return 0

    lax.fori_loop(0, d // 256, weight_cols, 0)
    w_sum = RingSum(at, w_send, w_recv, shard, w_sems)

    def w_step(s):
        w_sum.put(s, lambda side, owner: w_grad[rows_at(owner, shard), :])
        w_sum.go(s)

    w_step(0)
    if y_at < dims.steps:
        y_step(y_at)
        y_at += 1
    sums.recv(1)
    gain_one = jnp.zeros((1, d), F32)
    ins = Sent()
    own_rows = []
    for c, half in enumerate(split_parts(t)):
        sums.recv(2 + c)
        grad = part[at.h, half].astype(F32) + came[0, half].astype(F32) + came_far[half].astype(F32)
        inputs = x_own[half, :].astype(F32)
        scale = rms(inputs)
        gain_one = gain_one + jnp.sum(grad * inputs * scale, axis=0, keepdims=True)
        weighted = grad * gains[0:1, :]
        in_rows[half, :] = (
            resid_grad[half, :] + scale * weighted
            - inputs * (scale * scale * scale) * jnp.mean(weighted * inputs, axis=-1, keepdims=True)
        ).astype(BF16)
        spot = in_grad.at[pl.ds(pl.multiple_of(at.h * t + half.start, 16), half.size)]
        ins.start(("far", c), remote(in_rows.at[half], spot, in_sems, c, "hid", at.far))
        ins.start(("sib", c), remote(in_rows.at[half], spot, in_sems, 2 + c, "hid", at.sib))
        own_rows.append(local_start(in_rows.at[half], spot, local_sems.at[1 + c]))
    for owner in range(n):
        cols = slice(owner * shard, (owner + 1) * shard)
        cut_send[owner, small_rows:] = jnp.broadcast_to(gain_one[:, cols], (8, shard))
    late = pl.ds(small_rows, 8)
    for k, peer in enumerate(others):
        cuts.start(
            n + k, remote(cut_send.at[peer, late], cut_recv.at[at.e, late], cut_sems, n - 1 + k, "exp", peer)
        )
    own_cut_two = local_start(cut_send.at[at.e, late], cut_recv.at[at.e, late], local_sems.at[4])
    for k in range(count // 2, count):
        send_rest(k)
    w_at = 1
    if w_at < dims.steps:
        w_step(w_at)
        w_at += 1
    for k in range(n - 1):
        cuts.recv(k)
        cuts.recv(n + k)
    own_cut.wait()
    own_cut_two.wait()
    total = cut_recv[0]
    for k in range(1, n):
        total = total + cut_recv[k]
    sum_a[0] = total
    smalls = Sent()
    smalls.start(0, remote(sum_a.at[0], sum_a.at[1], small_sems, 0, "hid", at.sib))
    for c in (0, 1):
        ins.recv(("far", c))
        far_rows = in_grad.at[pl.ds(pl.multiple_of(at.far * t + c * (t // 2), 16), t // 2)]
        ins.start(("on", c), remote(far_rows, far_rows, in_sems, 4 + c, "hid", at.sib))
    smalls.recv(0)
    sum_a[2] = sum_a[0] + sum_a[1]
    smalls.start(1, remote(sum_a.at[2], sum_a.at[3], small_sems, 1, "hid", at.far))
    while y_at < dims.steps:
        y_step(y_at)
        y_at += 1
    while w_at < dims.steps:
        w_step(w_at)
        w_at += 1
    y_sum.arrive_last()
    y_own = y_row(at.e)
    for half in split_parts(t):
        out_rows[half, :] = (resid[half, :] + y_own[half].astype(F32) + y_sum.total(half)).astype(BF16)
    layers = Sent()
    for k, peer in enumerate((at.far, at.diag, at.sib)):
        layers.start(
            k, remote(out_rows.at[:, rows_at(peer, q4)], layer.at[rows_at(at.h, t)], layer_sems, k, "hid", peer)
        )
    own_layer = local_start(out_rows.at[:, rows_at(at.h, q4)], layer.at[rows_at(at.h, t)], local_sems.at[3])
    w_sum.arrive_last()
    for rows_part in split_parts(shard):
        here = pl.ds(pl.multiple_of(at.e * shard + rows_part.start, 16), rows_part.size)
        att_grad[rows_part, :] = w_grad[here, :] + w_sum.total(rows_part)
    smalls.recv(1)
    total = sum_a[2] + sum_a[3]
    small_one[...] = total[:small_rows]
    small_two[...] = total[small_rows:]

    for k in range(count):
        fars.recv(k)
    for k in range(3):
        layers.recv(k)
    for c in (0, 1):
        ins.recv(("sib", c))
        ins.recv(("on", c))
        own_rows[c].wait()
    own_layer.wait()
    for group in (rows, smalls, y_sum, fars, cuts, sums, w_sum, ins, layers):
        group.done()


def out_kernel(
    dims,
    layer_in, in_rows, small_one, small_two, att, own_d, own_g, own_u, sib_d, sib_g, sib_u, far_d, far_g, far_g_rest, far_u,
    layer, in_grad, gain_one, gain_two, wq, wk, wv, wo, router, gate, up, down,
):
    layer[...] = layer_in[...]
    in_grad[...] = in_rows[...].astype(F32)

    def three(own, sib, far):
        return own[0].astype(F32) + sib[0].astype(F32) + far.astype(F32)

    first = pl.program_id(0) < dims.crossing - dims.local
    down[0] = three(own_d, sib_d, far_d[0])
    gate[0] = three(own_g, sib_g, jnp.where(first, far_g[0], far_g_rest[0])).T
    up[0] = three(own_u, sib_u, far_u[0]).T

    @pl.when(pl.program_id(0) == 0)
    def _():
        gain_one[...] = small_two[:1, :]
        gain_two[...] = small_one[dims.experts : dims.experts + 1, :]
        router[...] = small_one[: dims.experts, :]
        qc, kc = dims.qc, dims.kc
        wq[...] = att[:, :qc]
        wk[...] = att[:, qc : qc + kc]
        wv[...] = att[:, qc + kc : qc + 2 * kc]
        wo[...] = att[:, dims.attn_cols :]


def per_device(
    tokens,
    segment_ids,
    routes,
    norm1_gain,
    norm2_gain,
    query_weight,
    key_matrix,
    value_matrix,
    out_weight,
    router_weight,
    gate_weight,
    up_weight,
    down_weight,
    out_grad,
):
    n = lax.axis_size("exp")
    assert lax.axis_size("hid") == 4
    token_count, d = tokens.shape
    local, _, part_ff = gate_weight.shape
    experts = router_weight.shape[1]
    dims = Dims(
        n, token_count, d, experts, local, 4 * part_ff, routes.shape[1], query_weight.shape[1], key_matrix.shape[1]
    )
    t, ff, steps, shard = dims.quarter, dims.ff, dims.steps, dims.shard
    qc, kc = dims.qc, dims.kc

    vmem = pl.BlockSpec(memory_space=pltpu.VMEM)
    anywhere = pl.BlockSpec(memory_space=pl.ANY)
    shape = jax.ShapeDtypeStruct
    dma = pltpu.SemaphoreType.DMA

    (
        ws_all, wg_all, wd_all, wu_cast, g_all, probs, normed, qkv, mixed, cosine, sine, resid, normed_two, coef, gates, kept,
    ) = pl.pallas_call(
        functools.partial(front_kernel, dims),
        out_shape=[
            shape((d, dims.ws_cols), BF16),
            shape((local, d, ff), BF16),
            shape((local, ff, d), BF16),
            shape((local, d, part_ff), BF16),
            shape((n, t, d), BF16),
            shape((4, dims.heads, token_count, t), BF16),
            shape((token_count, d), BF16),
            shape((token_count, dims.attn_cols), BF16),
            shape((token_count, qc), BF16),
            shape((token_count, LANES), F32),
            shape((token_count, LANES), F32),
            shape((t, d), F32),
            shape((t, d), BF16),
            shape((experts, t), F32),
            shape((t, LANES), F32),
            shape((t, LANES), F32),
        ],
        in_specs=[vmem] * 10 + [anywhere] * 4,
        out_specs=[anywhere] * 6 + [vmem] * 10,
        scratch_shapes=[
            pltpu.VMEM((d, dims.ws_cols), BF16),
            pltpu.VMEM((2, local, d, part_ff), F32),
            pltpu.VMEM((2, local, d, part_ff), BF16),
            pltpu.VMEM((local, part_ff, d), F32),
            pltpu.VMEM((local, part_ff, d), BF16),
            pltpu.VMEM((8, token_count), jnp.int32),
            pltpu.VMEM((4, dims.heads, token_count, t), BF16),
            pltpu.VMEM((4, t, d), BF16),
            pltpu.VMEM((2, t, d), BF16),
            pltpu.VMEM((t, d), BF16),
            pltpu.VMEM((t, d), BF16),
            dma((2, 4 * steps)),
            dma((2, 4 * steps)),
            dma((2, 4)),
            dma((2, 3)),
            dma((2, 3 * dims.early)),
            dma((8,)),
            dma((4,)),
            dma((dims.early,)),
        ],
        compiler_params=pltpu.CompilerParams(
            collective_id=0, has_side_effects=True, vmem_limit_bytes=VMEM_LIMIT
        ),
    )(
        tokens, segment_ids, routes.T, query_weight, key_matrix, value_matrix, out_weight, router_weight.T,
        norm1_gain[None, :], norm2_gain[None, :], out_grad, gate_weight, up_weight, down_weight,
    )

    big = n * t * d * 2 > 6 * 2**20
    jobs, crossing = dims.jobs, dims.crossing
    (dx, y_all, gate_grad, own, sib, own_rest, sib_rest, far, _) = pl.pallas_call(
        functools.partial(moe_kernel, dims, big),
        out_shape=[
            shape((t, d), F32),
            shape((n, t, d), BF16),
            shape((n, 8, t), F32),
            shape((jobs, part_ff, d), BF16),
            shape((jobs, part_ff, d), BF16),
            shape((jobs - crossing, part_ff, d), BF16),
            shape((jobs - crossing, part_ff, d), BF16),
            shape((crossing, part_ff, d), BF16),
            shape((n * t if big else 16, d), BF16),
        ],
        in_specs=[vmem, vmem] + [anywhere] * 4,
        out_specs=[vmem] + [anywhere] * 8,
        scratch_shapes=[
            pltpu.VMEM((16 if big else n * t, d), BF16),
            pltpu.VMEM((1, 16, d) if big else (n, t, d), BF16),
            pltpu.VMEM((n, experts, t), F32),
            pltpu.VMEM((local, d, ff), BF16),
            pltpu.VMEM((local, d, ff), BF16),
            pltpu.VMEM((local, ff, d), BF16),
            pltpu.VMEM((local, n * t, ff), BF16),
            pltpu.VMEM((local, n * t, ff), BF16),
            pltpu.VMEM((local, n * t, ff), BF16),
            pltpu.VMEM((2, 2, t, d), BF16),
            pltpu.VMEM((2, steps, t, d), BF16),
            pltpu.VMEM((n, 8, t), F32),
            pltpu.VMEM((2, max(ff, t), d), BF16),
            pltpu.VMEM((t, d) if big else (16, LANES), BF16),
            pltpu.VMEM((t, d) if big else (16, LANES), BF16),
            dma((2, 4 * steps)),
            dma((2, 4 * steps)),
            dma((2, 4 * steps)),
            dma((2, n - 1)),
            dma((2, 3 * local)),
            dma((2, 2 * jobs)),
            dma((2, crossing)),
            dma((6,)),
            dma((4,)),
            dma((2,)),
            dma((local,)),
            pltpu.SemaphoreType.REGULAR,
        ],
        compiler_params=pltpu.CompilerParams(
            collective_id=1, has_side_effects=True, vmem_limit_bytes=VMEM_LIMIT
        ),
    )(normed_two, coef, g_all, wg_all, wd_all, wu_cast)

    small_rows = experts + 8
    att = dims.attn_cols + qc
    (layer, in_rows, small_one, small_two, att_grad, far_rest) = pl.pallas_call(
        functools.partial(back_kernel, dims, big),
        out_shape=[
            shape((token_count, d // 4), BF16),
            shape((token_count, d), BF16),
            shape((small_rows, shard), F32),
            shape((8, shard), F32),
            shape((shard, att), F32),
            shape((jobs - crossing, part_ff, d), BF16),
        ],
        in_specs=[vmem] * 6 + [anywhere] * 12,
        out_specs=[anywhere] * 2 + [vmem] * 3 + [anywhere],
        scratch_shapes=[
            pltpu.VMEM((d, dims.ws_cols), BF16),
            pltpu.VMEM((token_count, dims.attn_cols), BF16),
            pltpu.VMEM((token_count, qc), BF16),
            pltpu.VMEM((token_count, d), BF16),
            pltpu.VMEM((token_count, LANES), F32),
            pltpu.VMEM((token_count, LANES), F32),
            pltpu.VMEM((4, dims.heads, token_count, t), BF16),
            pltpu.VMEM((t, d), BF16),
            pltpu.VMEM((t, d), BF16),
            pltpu.VMEM((t, d), F32),
            pltpu.VMEM((token_count, d), BF16),
            pltpu.VMEM((token_count, qc), BF16),
            pltpu.VMEM((token_count, qc), F32),
            pltpu.VMEM((token_count, kc), F32),
            pltpu.VMEM((token_count, kc), F32),
            pltpu.VMEM((token_count, dims.attn_cols), BF16),
            pltpu.VMEM((d, att), F32),
            pltpu.VMEM((4, t, d), BF16),
            pltpu.VMEM((2, t, d), BF16),
            pltpu.VMEM((t, d), BF16),
            pltpu.VMEM((t, d), BF16),
            pltpu.VMEM((1 if big else n, t, d), BF16),
            pltpu.VMEM((2, 2, t, d), BF16),
            pltpu.VMEM((2, steps, t, d), BF16),
            pltpu.VMEM((2, 2, shard, att), BF16),
            pltpu.VMEM((2, steps, shard, att), BF16),
            pltpu.VMEM((t, d), BF16),
            pltpu.VMEM((t, d), BF16),
            pltpu.VMEM((4, small_rows + 8, shard), F32),
            pltpu.VMEM((n, small_rows + 8, shard), F32),
            pltpu.VMEM((n, small_rows + 8, shard), F32),
            pltpu.VMEM((2, jobs - crossing, part_ff, d), BF16),
            dma((2, 6)),
            dma((2, 4 * steps)),
            dma((2, 4 * steps)),
            dma((2, 4)),
            dma((2, 6)),
            dma((2, 3)),
            dma((2, 2)),
            dma((2, 2 * (n - 1))),
            dma((2, jobs - crossing)),
            dma((6,)),
            dma((15,)),
        ],
        compiler_params=pltpu.CompilerParams(
            collective_id=2, has_side_effects=True, vmem_limit_bytes=VMEM_LIMIT
        ),
    )(
        dx, gate_grad.reshape(n * 8, t), gates, kept, resid, normed_two, g_all, tokens, ws_all, qkv, mixed, normed, cosine, sine,
        probs, y_all, own_rest, sib_rest,
    )

    rows = token_count // local

    def whole(shape_):
        return pl.BlockSpec(shape_, lambda i: (0,) * len(shape_))

    def matrix(index):
        return pl.BlockSpec((1, part_ff, d), lambda i: (index(i), 0, 0))

    (
        layer, in_grad, gain_one, gain_two, wq, wk, wv, wo, router, gate, up, down,
    ) = pl.pallas_call(
        functools.partial(out_kernel, dims),
        grid=(local,),
        out_shape=[
            shape((token_count, d // 4), BF16),
            shape((token_count, d), F32),
            shape((1, shard), F32),
            shape((1, shard), F32),
            shape((shard, qc), F32),
            shape((shard, kc), F32),
            shape((shard, kc), F32),
            shape((shard, qc), F32),
            shape((experts, shard), F32),
            shape((local, d, part_ff), F32),
            shape((local, d, part_ff), F32),
            shape((local, part_ff, d), F32),
        ],
        in_specs=[
            pl.BlockSpec((rows, d // 4), lambda i: (i, 0)),
            pl.BlockSpec((rows, d), lambda i: (i, 0)),
            whole((small_rows, shard)),
            whole((8, shard)),
            whole((shard, att)),
            matrix(lambda i: i),
            matrix(lambda i: local + i),
            matrix(lambda i: 2 * local + i),
            matrix(lambda i: i),
            matrix(lambda i: local + i),
            matrix(lambda i: 2 * local + i),
            matrix(lambda i: i),
            matrix(lambda i: jnp.minimum(local + i, crossing - 1)),
            matrix(lambda i: jnp.maximum(local + i - crossing, 0)),
            matrix(lambda i: 2 * local + i - crossing),
        ],
        out_specs=[
            pl.BlockSpec((rows, d // 4), lambda i: (i, 0)),
            pl.BlockSpec((rows, d), lambda i: (i, 0)),
            whole((1, shard)),
            whole((1, shard)),
            whole((shard, qc)),
            whole((shard, kc)),
            whole((shard, kc)),
            whole((shard, qc)),
            whole((experts, shard)),
            pl.BlockSpec((1, d, part_ff), lambda i: (i, 0, 0)),
            pl.BlockSpec((1, d, part_ff), lambda i: (i, 0, 0)),
            pl.BlockSpec((1, part_ff, d), lambda i: (i, 0, 0)),
        ],
        compiler_params=pltpu.CompilerParams(vmem_limit_bytes=VMEM_LIMIT),
    )(layer, in_rows, small_one, small_two, att_grad, own, own, own, sib, sib, sib, far, far, far_rest, far_rest)

    return (layer, in_grad, gain_one[0], gain_two[0], wq, wk, wv, wo, router.T, gate, up, down)


def solution(mesh):
    in_specs = (
        P("exp", None),
        P("exp", None),
        P("exp", None),
        P("exp"),
        P("exp"),
        P("exp", "hid"),
        P("exp", "hid"),
        P("exp", "hid"),
        P("exp", "hid"),
        P("exp", None),
        P("exp", None, "hid"),
        P("exp", None, "hid"),
        P("exp", "hid", None),
        P("exp", "hid"),
    )
    out_specs = (
        P("exp", "hid"),
        P("exp", None),
        P("exp"),
        P("exp"),
        P("exp", "hid"),
        P("exp", "hid"),
        P("exp", "hid"),
        P("exp", "hid"),
        P("exp", None),
        P("exp", None, "hid"),
        P("exp", None, "hid"),
        P("exp", "hid", None),
    )
    return jax.shard_map(
        per_device, mesh=mesh, in_specs=in_specs, out_specs=out_specs, check_vma=False
    )
```

```python
import functools
import math

import jax
import jax.numpy as jnp
from jax import lax
from jax.experimental import pallas as pl
from jax.experimental.pallas import tpu as pltpu
from jax.sharding import PartitionSpec as P

HEAD_DIM = 64
SEGS = 4
EPSILON = 1e-05
ROPE_BASE = 10000.0
NEG_FILL = -1e30
LANES = 128
MESH = pl.DeviceIdType.MESH
F32 = jnp.float32
BF16 = jnp.bfloat16
VMEM_LIMIT = 62 * 2**20


def nn(a, b):
    return lax.dot_general(a, b, (((1,), (0,)), ((), ())), preferred_element_type=F32)


def nt(a, b):
    return lax.dot_general(a, b, (((1,), (1,)), ((), ())), preferred_element_type=F32)


def tn(a, b):
    return lax.dot_general(a, b, (((0,), (0,)), ((), ())), preferred_element_type=F32)


def tn_exact(a, b):
    return lax.dot_general(
        a, b, (((0,), (0,)), ((), ())), preferred_element_type=F32, precision=lax.Precision.HIGHEST
    )


def iota(shape, dim):
    return lax.broadcasted_iota(jnp.int32, shape, dim)


def rows_at(index, size):
    return pl.ds(pl.multiple_of(index * size, size), size)


def pos_of(index, n):
    odd = index % 2
    return (1 - odd) * (index // 2) + odd * (n - 1 - index // 2)


def at_pos(pos, n):
    back = pos // (n // 2)
    return (1 - back) * (2 * pos) + back * (2 * (n - 1 - pos) + 1)


class Place:
    def __init__(self, n):
        self.n = n
        self.e = lax.axis_index("exp")
        self.h = lax.axis_index("hid")
        self.p = pos_of(self.e, n)
        self.right = self.ring(1)
        self.left = self.ring(-1)
        self.sib = self.h + 1 - 2 * (self.h % 2)
        self.far = (self.h + 2) % 4
        self.diag = (self.sib + 2) % 4

    def ring(self, away):
        return at_pos((self.p + self.n + away) % self.n, self.n)


def greet(exp_peers, hid_peers):
    barrier = pltpu.get_barrier_semaphore()
    for peer in exp_peers:
        pl.semaphore_signal(barrier, inc=1, device_id={"exp": peer}, device_id_type=MESH)
    for peer in hid_peers:
        pl.semaphore_signal(barrier, inc=1, device_id={"hid": peer}, device_id_type=MESH)
    pl.semaphore_wait(barrier, len(exp_peers) + len(hid_peers))


def remote(src, dst, sems, k, axis, to):
    return pltpu.make_async_remote_copy(
        src_ref=src,
        dst_ref=dst,
        send_sem=sems.at[0, k],
        recv_sem=sems.at[1, k],
        device_id={axis: to},
        device_id_type=MESH,
    )


class Sent:
    def __init__(self):
        self.copies = {}
        self.unsent = []

    def start(self, key, copy):
        copy.start()
        self.copies[key] = copy
        self.unsent.append(copy)

    def recv(self, key):
        self.copies[key].wait_recv()

    def done(self):
        for copy in self.unsent:
            copy.wait_send()
        self.unsent = []


class RingGather:
    def __init__(self, place, view, rows, sems):
        self.place, self.view, self.rows, self.sems = place, view, rows, sems
        self.steps = place.n // 2
        self.sent = Sent()

    def part(self, s, c):
        half = self.rows // 2
        for side in (0, 1):
            if s:
                self.sent.recv((s - 1, side, c))
            if s < self.steps - 1 or c == side:
                away, to = ((-s, self.place.right), (s, self.place.left))[side]
                block = self.view(self.place.ring(away), c * half, half)
                self.sent.start((s, side, c), remote(block, block, self.sems, 4 * s + 2 * side + c, "exp", to))

    def start(self, s):
        self.part(s, 0)
        self.part(s, 1)

    def recv_last(self):
        self.sent.recv((self.steps - 1, 0, 0))
        self.sent.recv((self.steps - 1, 1, 1))

    def done(self):
        self.sent.done()


class RingSum:
    def __init__(self, place, send, recv, rows, sems):
        self.place, self.send, self.recv, self.rows, self.sems = place, send, recv, rows, sems
        self.steps = place.n // 2
        self.copies = {}

    def owner(self, s, side):
        away = self.steps - s
        return self.place.ring(away if side == 0 else -away)

    def chunks(self, s):
        for c in (0, 1):
            for side in (0, 1):
                if s > 0 or c == side:
                    yield c, side

    def put(self, s, get):
        if s >= 2:
            for c, side in self.chunks(s - 2):
                self.copies[(s - 2, side, c)].wait_send()
        if s == 0:
            half = self.rows // 2
            terms = get(0, self.owner(0, 0)).astype(self.send.dtype)
            self.send[0, 0, pl.ds(0, half)] = terms[:half]
            self.send[1, 0, pl.ds(half, half)] = terms[half:]
            return
        for side in (0, 1):
            self.send[side, s % 2] = get(side, self.owner(s, side)).astype(self.send.dtype)

    def part(self, s, c):
        half = self.rows // 2
        rows = pl.ds(c * half, half)
        for side in (0, 1):
            if s == 0 and c != side:
                continue
            src = self.send.at[side, s % 2, rows]
            if s > 1 or (s == 1 and c == side):
                self.copies[(s - 1, side, c)].wait_recv()
                came = self.recv[side, s - 1, rows].astype(F32)
                src[...] = (src[...].astype(F32) + came).astype(src.dtype)
            to = self.place.left if side else self.place.right
            copy = remote(src, self.recv.at[side, s, rows], self.sems, 4 * s + 2 * side + c, "exp", to)
            copy.start()
            self.copies[(s, side, c)] = copy

    def go(self, s):
        self.part(s, 0)
        self.part(s, 1)

    def arrive_last(self):
        for c, side in self.chunks(self.steps - 1):
            self.copies[(self.steps - 1, side, c)].wait_recv()

    def total(self, part):
        return self.recv[0, self.steps - 1, part].astype(F32) + self.recv[1, self.steps - 1, part].astype(F32)

    def done(self):
        for s in range(self.steps - 2, self.steps):
            for c, side in self.chunks(s):
                self.copies[(s, side, c)].wait_send()


def local_start(src, dst, sem):
    copy = pltpu.make_async_copy(src, dst, sem)
    copy.start()
    return copy


def split_parts(count):
    return (pl.ds(0, count // 2), pl.ds(count // 2, count // 2))


def rms(values):
    return lax.rsqrt(jnp.mean(values * values, axis=-1, keepdims=True) + EPSILON)


def swap_halves(values):
    half = HEAD_DIM // 2
    width = values.shape[1]
    up = pltpu.roll(values, width - half, 1)
    down = pltpu.roll(values, half, 1)
    first = iota(values.shape, 1) % HEAD_DIM < half
    return jnp.where(first, up, down)


def gain_rows(slab, expert_count):
    pick = (iota((16, LANES), 1) == iota((16, LANES), 0) + expert_count).astype(BF16)
    return nt(pick, slab)


def bias_block(begin_row, first_row, key_count):
    shape = (key_count, begin_row.shape[1])
    keys = iota(shape, 0)
    seen = (keys >= begin_row) & (keys <= first_row + iota(shape, 1))
    return jnp.where(seen, 0.0, NEG_FILL)


class Dims:
    def __init__(self, n, token_count, width, expert_count, local_experts, ff, topk, qc, kc):
        self.n, self.tokens, self.d = n, token_count, width
        self.experts, self.local, self.ff, self.topk = expert_count, local_experts, ff, topk
        self.qc, self.kc = qc, kc
        self.quarter = token_count // 4
        self.shard = width // n
        self.capacity = token_count * topk * 5 // (4 * expert_count)
        self.attn_cols = qc + 2 * kc
        self.slab_at = 2 * qc + 2 * kc
        self.ws_cols = self.slab_at + LANES
        self.heads = qc // HEAD_DIM
        self.group = qc // kc
        self.part_ff = ff // 4
        self.steps = n // 2
        self.jobs = 3 * local_experts
        self.crossing = self.jobs * 7 // 12
        self.early = 2 * local_experts


def tall(row, count):
    return jnp.broadcast_to(row, (LANES, row.shape[1])).T[:, :count]


def front_kernel(
    dims,
    x, seg, routes, wq, wk, wv, wo, router, gain_one, gain_two, g, wg, wu, wd,
    ws_out, wg_all, wd_all, wu_cast, g_all, probs_out, normed, qkv, mixed, cosine, sine, resid, normed_two, coef, gates, kept,
    ws_all, wide, cast, wide_down, cast_down, begin, probs, part, came, mid, came_far,
    ws_sems, g_sems, hid_sems, swap_sems, weight_sems, local_sems, probs_sems, own_sems,
):
    at = Place(dims.n)
    t, d, ff4, shard, tokens = dims.quarter, dims.d, dims.part_ff, dims.shard, dims.tokens
    q4 = d // 4
    kv = dims.kc
    loads = [local_start(ref, wide.at[k], local_sems.at[k]) for k, ref in enumerate((wg, wu))]
    load_down = local_start(wd, wide_down, local_sems.at[2])

    mine = rows_at(at.e, shard)
    at_col = 0
    for ref in (wq, wk, wv, wo):
        ws_all[mine, at_col : at_col + ref.shape[1]] = ref[...].astype(BF16)
        at_col += ref.shape[1]
    lane = iota((shard, LANES), 1)
    slab = jnp.concatenate([router[...], jnp.zeros((LANES - dims.experts, shard), F32)], axis=0).T
    slab = jnp.where(lane == dims.experts, tall(gain_one[...], LANES), slab)
    slab = jnp.where(lane == dims.experts + 1, tall(gain_two[...], LANES), slab)
    ws_all[mine, dims.slab_at :] = slab.astype(BF16)

    greet((at.right, at.left), (at.sib, at.far, at.diag))
    ring = RingGather(at, lambda o, f, s: ws_all.at[pl.ds(pl.multiple_of(o * shard + f, 16), s)], shard, ws_sems)
    ring.start(0)

    swaps = Sent()
    for k, peer in enumerate((at.sib, at.far, at.diag)):
        swaps.start(
            k, remote(g.at[rows_at(peer, t)], g_all.at[at.e, :, rows_at(at.h, q4)], swap_sems, k, "hid", peer)
        )
    g_own = local_start(g.at[rows_at(at.h, t)], g_all.at[at.e, :, rows_at(at.h, q4)], local_sems.at[3])

    moves = Sent()
    kept_own = []
    units = [(0, i) for i in range(dims.local)] + [(1, i) for i in range(dims.local)]
    lot = (5 * len(units) + 7) // 8

    def source(u):
        k, i = units[u]
        return cast_down.at[i] if k else cast.at[0, i]

    def spot(u, owner):
        k, i = units[u]
        return wd_all.at[i, rows_at(owner, ff4), :] if k else wg_all.at[i, :, rows_at(owner, ff4)]

    def send_unit(u):
        moves.start(("far", u), remote(source(u), spot(u, at.h), weight_sems, u, "hid", at.far))

    def pass_on(u):
        moves.recv(("far", u))
        block = spot(u, at.far)
        moves.start(("on", u), remote(block, block, weight_sems, len(units) + u, "hid", at.sib))

    loads[0].wait()
    cast[0] = wide[0].astype(BF16)
    for u in range(min(lot, dims.local)):
        send_unit(u)
    load_down.wait()
    cast_down[...] = wide_down[...].astype(BF16)
    for u in range(min(lot, dims.local), lot):
        send_unit(u)
    for u in range(len(units)):
        moves.start(
            ("sib", u), remote(source(u), spot(u, at.h), weight_sems, 2 * len(units) + u, "hid", at.sib)
        )
        kept_own.append(local_start(source(u), spot(u, at.h), own_sems.at[u]))

    ring.start(1)
    for k in range(3):
        swaps.recv(k)
    g_own.wait()
    g_ring = RingGather(at, lambda o, f, s: g_all.at[o, pl.ds(f, s)], t, g_sems)

    counts = [jnp.sum((seg[...] == k).astype(F32), axis=1, keepdims=True) for k in range(SEGS)]
    first = jnp.zeros((1, tokens), F32)
    total = jnp.zeros((1, 1), F32)
    for k in range(SEGS):
        first = first + jnp.where(seg[...] == k, total, 0.0)
        total = total + counts[k]
    begin[...] = jnp.broadcast_to(first, (8, tokens)).astype(jnp.int32)
    lane = iota((1, LANES), 1)
    half = HEAD_DIM // 2
    freqs = jnp.exp((lane % half).astype(F32) * (-math.log(ROPE_BASE) / half))
    positions = iota((1, tokens), 1).astype(F32) - first

    def table(j):
        rows = pl.ds(j * t, t)
        angles = tall(positions[:, j * t : (j + 1) * t], LANES) * freqs
        cosine[rows, :] = jnp.cos(angles)
        sine[rows, :] = jnp.where(lane % HEAD_DIM < half, -1.0, 1.0) * jnp.sin(angles)

    todo = [functools.partial(table, j) for j in range(4)]

    for s in range(2, dims.steps):
        if todo:
            todo.pop(0)()
            todo.pop(0)()
        ring.start(s)
    for job in todo:
        job()
    loads[1].wait()
    cast[1] = wide[1].astype(BF16)
    saves = [local_start(cast.at[1], wu_cast, local_sems.at[4])]
    ring.recv_last()
    out_ws = local_start(ws_all, ws_out, local_sems.at[6])

    g_ring.start(0)

    slab = ws_all[:, dims.slab_at :]
    gains = gain_rows(slab, dims.experts)
    repeat = (dims.qc + kv) // LANES
    for j in range(4):
        rows = pl.ds(j * t, t)
        values = x[rows, :].astype(F32)
        block = (values * rms(values) * gains[0:1, :]).astype(BF16)
        normed[rows, :] = block
        raw = nn(block, ws_all[:, : dims.attn_cols])
        turned = raw[:, : dims.qc + kv]
        turned = turned * jnp.tile(cosine[rows, :], (1, repeat)) + swap_halves(turned) * jnp.tile(
            sine[rows, :], (1, repeat)
        )
        queries = turned[:, : dims.qc].astype(BF16) * jnp.asarray(HEAD_DIM**-0.5, BF16)
        qkv[rows, : dims.qc] = queries
        qkv[rows, dims.qc : dims.qc + kv] = turned[:, dims.qc :].astype(BF16)
        qkv[rows, dims.qc + kv :] = raw[:, dims.qc + kv :].astype(BF16)

    for j in range(4):
        rows = pl.ds(j * t, t)
        keys = (j + 1) * t
        bias = bias_block(begin[:1, j * t : (j + 1) * t], j * t, keys)
        for head in range(dims.heads):
            key_at = dims.qc + head // dims.group * HEAD_DIM
            query = qkv[rows, head * HEAD_DIM : (head + 1) * HEAD_DIM]
            key = qkv[:keys, key_at : key_at + HEAD_DIM]
            value = qkv[:keys, key_at + kv : key_at + kv + HEAD_DIM]
            scores = nt(key, query) + bias
            powers = jnp.exp(scores - jnp.max(scores, axis=0, keepdims=True))
            share = (powers * (1.0 / jnp.sum(powers, axis=0, keepdims=True))).astype(BF16)
            probs[j, head, :keys, :] = share
            mixed[rows, head * HEAD_DIM : (head + 1) * HEAD_DIM] = tn(value, share).T.astype(BF16)
        saves.append(
            local_start(probs.at[j, :, pl.ds(0, keys)], probs_out.at[j, :, pl.ds(0, keys)], probs_sems.at[j])
        )

    g_ring.start(1)
    wo_all = ws_all.at[:, pl.ds(dims.attn_cols, dims.qc)]
    sums = Sent()
    for k, quarter in enumerate((at.diag, at.far, at.sib, at.h)):
        part[quarter] = nt(mixed[rows_at(quarter, t), :], wo_all[...]).astype(BF16)
        if k == 0:
            sums.start(0, remote(part.at[at.diag], came.at[1], hid_sems, 0, "hid", at.sib))
        if k == 1:
            sums.recv(0)
            for c, rows in enumerate(split_parts(t)):
                mid[rows, :] = (part[at.far, rows].astype(F32) + came[1, rows].astype(F32)).astype(BF16)
                sums.start(2 + c, remote(mid.at[rows], came_far.at[rows], hid_sems, 2 + c, "hid", at.far))
        if k == 2:
            sums.start(1, remote(part.at[at.sib], came.at[0], hid_sems, 1, "hid", at.sib))
    g_ring.start(2)
    for u in range(lot):
        pass_on(u)

    expert = iota((dims.experts, tokens), 0)
    chosen = jnp.zeros((dims.experts, tokens), F32)
    for k in range(dims.topk):
        chosen = chosen + (routes[k : k + 1, :] == expert).astype(F32)
    earlier = (iota((tokens, t), 0) < iota((tokens, t), 1) + at.h * t).astype(BF16)
    rank = nn(chosen.astype(BF16), earlier)
    expert = iota((dims.experts, t), 0)
    own_routes = routes[:, rows_at(at.h, t)]
    mine = jnp.zeros((dims.experts, t), F32)
    for k in range(dims.topk):
        mine = mine + (own_routes[k : k + 1, :] == expert).astype(F32)
    keep = mine * (rank < dims.capacity).astype(F32)
    rest = jnp.zeros((LANES - dims.experts, t), F32)
    mine = jnp.concatenate([mine, rest], axis=0).T
    keep = jnp.concatenate([keep, rest], axis=0).T
    kept[...] = keep

    sums.recv(1)
    for c, rows in enumerate(split_parts(t)):
        sums.recv(2 + c)
        first = pl.ds(pl.multiple_of(at.h * t + rows.start, 16), rows.size)
        values = (
            part[at.h, rows].astype(F32) + came[0, rows].astype(F32) + came_far[rows].astype(F32)
            + x[first, :].astype(F32)
        )
        resid[rows, :] = values
        normed_two[rows, :] = (values * rms(values) * gains[1:2, :]).astype(BF16)
    for u in range(lot, len(units)):
        send_unit(u)
    logits = nn(normed_two[...], slab)
    for s in range(3, dims.steps):
        g_ring.start(s)
    picked = jnp.where(mine > 0, logits, NEG_FILL)
    powers = jnp.exp(picked - jnp.max(picked, axis=1, keepdims=True)) * mine
    gate = powers / jnp.sum(powers, axis=1, keepdims=True)
    gates[...] = gate
    coef[...] = (gate * keep).T[: dims.experts, :]

    for u in range(lot, len(units)):
        pass_on(u)
    for u in range(len(units)):
        moves.recv(("sib", u))
        kept_own[u].wait()
    for u in range(len(units)):
        moves.recv(("on", u))
    g_ring.recv_last()
    for copy in saves:
        copy.wait()
    out_ws.wait()
    for group in (ring, g_ring, swaps, moves, sums):
        group.done()


def moe_kernel(
    dims, big,
    x_own, coef_own, g_all, wg_in, wd_in, wu_own,
    dx, y_all, gate_grad, own_out, sib_out, own_far, sib_far, far_out, x_far,
    x_near, g_near, coef, wg, wu, wd, d_gate, d_up, hid, send, recv, grads, stage, x_stage, g_stage,
    x_sems, c_sems, sum_sems, grad_sems, wd_sems, job_sems, far_sems, local_sems, keep_sems, y_sems, own_sems, free_sem,
):
    at = Place(dims.n)
    n, t, d, local, ff, ff4 = dims.n, dims.quarter, dims.d, dims.local, dims.ff, dims.part_ff
    others = tuple((at.e + k) % n for k in range(1, n))
    load_gate = local_start(wg_in, wg, local_sems.at[1])
    load_down = local_start(wd_in, wd, local_sems.at[2])
    if not big:
        load_g = local_start(g_all, g_near, local_sems.at[4])
    xs = x_far if big else x_near
    coef[at.e] = coef_own[...]
    if big:
        local_start(x_own, xs.at[rows_at(at.e, t)], local_sems.at[0]).wait()
    else:
        xs[rows_at(at.e, t), :] = x_own[...]
    greet(others, (at.sib, at.far))

    x_ring = RingGather(at, lambda o, f, s: xs.at[pl.ds(pl.multiple_of(o * t + f, 16), s)], t, x_sems)
    c_ring = RingGather(at, lambda o, f, s: coef.at[o, pl.ds(f, s)], dims.experts, c_sems)
    c_ring.start(0)
    x_ring.start(0)

    late = local

    def source(u):
        return wu_own.at[u]

    def spot(u, owner):
        return wu.at[u, :, rows_at(owner, ff4)]

    downs = Sent()
    kept_own = []
    for u in range(late):
        downs.start(("far", u), remote(source(u), spot(u, at.h), wd_sems, u, "hid", at.far))
    for u in range(late):
        downs.start(("sib", u), remote(source(u), spot(u, at.h), wd_sems, late + u, "hid", at.sib))
        kept_own.append(local_start(source(u), spot(u, at.h), own_sems.at[u]))

    def arrive():
        for u in range(late):
            downs.recv(("far", u))
            block = spot(u, at.far)
            downs.start(("on", u), remote(block, block, wd_sems, 2 * late + u, "hid", at.sib))
        for u in range(late):
            downs.recv(("sib", u))
            kept_own[u].wait()
            downs.recv(("on", u))

    def x_row(owner):
        if not big:
            return xs.at[rows_at(owner, t)]
        local_start(xs.at[rows_at(owner, t)], x_stage, local_sems.at[0]).wait()
        return x_stage

    def g_row(owner):
        if not big:
            return g_near.at[owner]
        local_start(g_all.at[owner], g_stage, local_sems.at[4]).wait()
        return g_stage

    lane = iota((t, LANES), 1)

    def gate_products(owner):
        rows = rows_at(owner, t)
        inputs = x_row(owner)
        for i in range(local):
            d_gate[i, rows, :] = nn(inputs[...], wg[i]).astype(BF16)

    def back_products(i):
        def one(r, _):
            hid[i, rows_at(r, t), :] = nt(g_row(r)[...], wd[i]).astype(BF16)
            return 0

        lax.fori_loop(0, n, one, 0)

    def work(owner, which, fresh):
        rows = rows_at(owner, t)
        inputs = x_row(owner)
        columns = jnp.concatenate([coef[owner], jnp.zeros((LANES - dims.experts, t), F32)], axis=0).T
        for i in which:
            share = jnp.sum(jnp.where(lane == at.e * local + i, columns, 0.0), axis=1, keepdims=True)
            pre_gate = nn(inputs[...], wg[i]) if fresh else d_gate[i, rows, :].astype(F32)
            pre_up = nn(inputs[...], wu[i])
            back = hid[i, rows, :].astype(F32)
            sig = 0.5 * jnp.tanh(0.5 * pre_gate) + 0.5
            silu = pre_gate * sig
            hidden = silu * pre_up
            own = jnp.sum(hidden * back, axis=1, keepdims=True)
            grads[owner, i : i + 1, :] = jnp.broadcast_to(own, (t, LANES)).T[:1, :]
            back = share * back
            d_up[i, rows, :] = (back * silu).astype(BF16)
            d_gate[i, rows, :] = (back * pre_up * (sig + silu * (1.0 - sig))).astype(BF16)
            hid[i, rows, :] = (share * hidden).astype(BF16)

    def layer_row(owner, slot):
        rows = rows_at(owner, t)
        stage[slot, :t, :] = sum(nn(hid[i, rows, :], wd[i]) for i in range(local)).astype(BF16)
        local_start(stage.at[slot, pl.ds(0, t)], y_all.at[owner], y_sems.at[slot])

    def y_wait(slot):
        pltpu.make_async_copy(stage.at[slot, pl.ds(0, t)], y_all.at[0], y_sems.at[slot]).wait()

    def side_row(away, k):
        return at_pos((at.p + n + (2 * k - 1) * away) % n, n)

    def both(away, do):
        def one(k, _):
            do(side_row(away, k), k)
            return 0

        lax.fori_loop(0, 2, one, 0)

    def near(which):
        def one(k, _):
            work(at_pos((at.p + n + k - 1) % n, n), which, False)
            return 0

        lax.fori_loop(0, 3, one, 0)

    steps = dims.steps
    load_gate.wait()
    gate_products(at.e)
    if not big:
        load_g.wait()
    load_down.wait()
    for i in range(local - 1):
        back_products(i)
    x_ring.part(1, 0)
    back_products(local - 1)
    x_ring.part(1, 1)
    c_ring.start(1)
    both(1, lambda owner, k: gate_products(owner))
    arrive()
    for s in range(2, steps):
        x_ring.part(s, 0)
        if s == 2:
            near((0,))
        x_ring.part(s, 1)
        c_ring.start(s)
        if s == 2 and local > 1:
            near(range(1, local))
        both(s, lambda owner, k: work(owner, range(local), True))
    layer_row(at.e, 0)
    y_wait(0)
    for away in range(1, steps):
        both(away, layer_row)
        for slot in (0, 1):
            y_wait(slot)
    c_ring.recv_last()
    x_ring.recv_last()
    last = side_row(steps, 1)
    work(last, range(local), True)
    layer_row(last, 0)
    y_wait(0)

    small = Sent()
    for k, peer in enumerate(others):
        small.start(k, remote(grads.at[peer], gate_grad.at[at.e], grad_sems, k, "exp", peer))
    own_small = local_start(grads.at[at.e], gate_grad.at[at.e], local_sems.at[5])

    sources = (hid, d_gate, d_up)
    jobs = [(kind, i) for kind in range(3) for i in range(local)]
    crossing = dims.crossing
    flights, kept = {}, {}

    def spare(k):
        return wd.at[k // 4, pl.ds(k % 4 * ff4, ff4)]

    downs.done()
    pl.semaphore_signal(free_sem, inc=1, device_id={"hid": at.sib}, device_id_type=MESH)
    pl.semaphore_wait(free_sem, 1)


    def job(k):
        kind, i = jobs[k]
        slot = k % 2
        if k >= 2:
            for copy in flights[k - 2]:
                copy.wait_send()
            for copy in kept[k - 2]:
                copy.wait()
        left = sources[kind]
        for f in range(ff // 256):
            units = slice(f * 256, (f + 1) * 256)
            if big:
                def add(r, total, units=units):
                    right = g_row(r) if kind == 0 else x_row(r)
                    return total + tn(left[i, rows_at(r, t), units], right[...])

                value = lax.fori_loop(0, n, add, jnp.zeros((256, d), F32))
            else:
                right = g_near.reshape(n * t, d) if kind == 0 else xs
                value = tn(left[i, :, units], right[...])
            stage[slot, units, :] = value.astype(BF16)
        flights[k], kept[k] = [], []
        if k < crossing:
            far_room = ((at.diag, at.far), (spare(2 * k + 1), spare(2 * k)))
        else:
            far_room = ((at.diag, at.far), (sib_far.at[k - crossing], own_far.at[k - crossing]))
        for which, ((there, here), (sib_spot, own_spot)) in enumerate(
            (((at.sib, at.h), (sib_out.at[k], own_out.at[k])), far_room)
        ):
            copy = remote(stage.at[slot, rows_at(there, ff4)], sib_spot, job_sems, 2 * k + which, "hid", at.sib)
            copy.start()
            flights[k].append(copy)
            kept[k].append(
                local_start(stage.at[slot, rows_at(here, ff4)], own_spot, keep_sems.at[2 * slot + which])
            )

    fars = Sent()

    def cross(k):
        flights[k][1].wait_recv()
        if k >= done_jobs - 2:
            kept[k].pop().wait()
        one, two = spare(2 * k), spare(2 * k + 1)
        one[...] = (one[...].astype(F32) + two[...].astype(F32)).astype(BF16)
        fars.start(k, remote(one, far_out.at[k], far_sems, k, "hid", at.far))

    def input_grad(owner):
        rows = rows_at(owner, t)
        return sum(nt(d_gate[i, rows, :], wg[i]) + nt(d_up[i, rows, :], wu[i]) for i in range(local))

    sums = RingSum(at, send, recv, t, sum_sems)
    done_jobs = 0

    def jobs_until(count):
        nonlocal done_jobs
        while done_jobs < count:
            job(done_jobs)
            done_jobs += 1
            if 2 <= done_jobs <= crossing + 1:
                cross(done_jobs - 2)

    sums.put(0, lambda side, owner: input_grad(owner))
    sums.go(0)
    for s in range(1, steps):
        jobs_until(len(jobs) * (2 * s - 1) // (2 * steps - 1))
        sums.put(s, lambda side, owner: input_grad(owner))
        sums.part(s, 0)
        jobs_until(min(len(jobs), done_jobs + 1))
        sums.part(s, 1)
    jobs_until(len(jobs))
    if crossing >= len(jobs):
        cross(len(jobs) - 1)
    dx[...] = input_grad(at.e)
    sums.arrive_last()
    for rows in split_parts(t):
        dx[rows, :] = dx[rows, :] + sums.total(rows)

    for k in range(len(others)):
        small.recv(k)
    own_small.wait()
    for k in range(len(jobs)):
        flights[k][0].wait_recv()
        if k >= crossing:
            flights[k][1].wait_recv()
    for k in range(len(jobs) - 2, len(jobs)):
        for copy in flights[k]:
            copy.wait_send()
        for copy in kept[k]:
            copy.wait()
    for k in range(crossing):
        fars.recv(k)
    for group in (x_ring, c_ring, downs, small, sums, fars):
        group.done()


def back_kernel(
    dims, big,
    dx, gate_grad, gates, kept, resid, normed_two, g_all, x, ws_in, qkv_in, mixed_in, normed_in, cosine_in, sine_in, probs_in,
    y_all, own_in, sib_in,
    layer, in_grad, small_one, small_two, att_grad, far_rest,
    ws, qkv, mixed, normed, cosine, sine, probs, x_own, g_own, resid_grad, rows_all, mixed_grad, d_query, d_key, d_value,
    d_qkv, w_grad, part, came, mid, came_far, y_rows, y_send, y_recv, w_send, w_recv, out_rows, in_rows, sum_a,
    cut_send, cut_recv, rest,
    row_sems, y_sems, w_sems, hid_sems, in_sems, layer_sems, small_sems, cut_sems, far_sems, local_sems, load_sems,
):
    at = Place(dims.n)
    n, t, d, kv, shard = dims.n, dims.quarter, dims.d, dims.kc, dims.shard
    q4 = d // 4
    others = tuple((at.e + k) % n for k in range(1, n))
    pairs = [
        (ws_in, ws), (g_all.at[at.e], g_own), (own_in, rest.at[0]), (sib_in, rest.at[1]), (qkv_in, qkv),
        (mixed_in, mixed), (normed_in, normed), (cosine_in, cosine), (sine_in, sine), (x.at[rows_at(at.h, t)], x_own),
    ]
    if not big:
        pairs.append((y_all, y_rows))
    loads = [local_start(src, dst, load_sems.at[k]) for k, (src, dst) in enumerate(pairs)]
    for j in range(4):
        span = pl.ds(0, (j + 1) * t)
        loads.append(local_start(probs_in.at[j, :, span], probs.at[j, :, span], load_sems.at[11 + j]))
    greet(others, (at.sib, at.far, at.diag))
    loads[0].wait()
    loads[1].wait()

    slab = ws[:, dims.slab_at :]
    gains = gain_rows(slab, dims.experts)
    spread_shape = (n * 8, LANES)
    sub, lane = iota(spread_shape, 0), iota(spread_shape, 1)
    spread = (
        (sub // 8 == lane // dims.local) & (sub % 8 == lane % dims.local) & (lane < dims.experts)
    ).astype(F32)
    gg = tn_exact(gate_grad[...], spread) * kept[...]
    gate = gates[...]
    logit_grad = (gate * (gg - jnp.sum(gate * gg, axis=1, keepdims=True))).astype(BF16)
    gain_two = jnp.zeros((1, d), F32)
    rows = Sent()
    for c, half in enumerate(split_parts(t)):
        lg = logit_grad[half.start : half.start + half.size, :]
        normed_grad = dx[half, :] + nt(lg, slab)
        inputs = resid[half, :]
        scale = rms(inputs)
        gain_two = gain_two + jnp.sum(normed_grad * inputs * scale, axis=0, keepdims=True)
        weighted = normed_grad * gains[1:2, :]
        value = (
            g_own[half, :].astype(F32) + scale * weighted
            - inputs * (scale * scale * scale) * jnp.mean(weighted * inputs, axis=-1, keepdims=True)
        )
        resid_grad[half, :] = value
        here = pl.ds(pl.multiple_of(at.h * t + half.start, 16), half.size)
        rows_all[here, :] = value.astype(BF16)
        rows.start(("far", c), remote(rows_all.at[here], rows_all.at[here], row_sems, c, "hid", at.far))
        rows.start(("sib", c), remote(rows_all.at[here], rows_all.at[here], row_sems, 2 + c, "hid", at.sib))

    for load in loads[2:]:
        load.wait()
    router_rows = dims.experts
    small_rows = router_rows + 8
    router_part = tn(logit_grad, normed_two[...])
    for owner in range(n):
        cols = slice(owner * shard, (owner + 1) * shard)
        cut_send[owner, :router_rows] = router_part[:router_rows, cols]
        cut_send[owner, router_rows:small_rows] = jnp.broadcast_to(gain_two[:, cols], (8, shard))

    def add_rest(k, _):
        rest[0, k] = (rest[0, k].astype(F32) + rest[1, k].astype(F32)).astype(BF16)
        return 0

    lax.fori_loop(0, dims.jobs - dims.crossing, add_rest, 0)

    y_sum = RingSum(at, y_send, y_recv, t, y_sems)

    def y_row(owner):
        if not big:
            return y_rows.at[owner]
        local_start(y_all.at[owner], y_rows.at[0], local_sems.at[5]).wait()
        return y_rows.at[0]

    def y_step(s):
        y_sum.put(s, lambda side, owner: y_row(owner)[...].astype(F32))
        y_sum.go(s)

    y_step(0)
    wo = ws.at[:, pl.ds(dims.attn_cols, dims.qc)]

    def project(quarter):
        block = rows_at(quarter, t)
        mixed_grad[block, :] = nn(rows_all[block, :], wo[...]).astype(BF16)

    project(at.h)
    rows.recv(("sib", 0))
    rows.recv(("sib", 1))
    project(at.sib)
    for c in (0, 1):
        rows.recv(("far", c))
        here = pl.ds(pl.multiple_of(at.far * t + c * (t // 2), 16), t // 2)
        rows.start(("on", c), remote(rows_all.at[here], rows_all.at[here], row_sems, 4 + c, "hid", at.sib))
    project(at.far)
    fars = Sent()
    count = dims.jobs - dims.crossing

    def send_rest(k):
        fars.start(k, remote(rest.at[0, k], far_rest.at[k], far_sems, k, "hid", at.far))

    for k in range(count // 2):
        send_rest(k)
    rows.recv(("on", 0))
    rows.recv(("on", 1))
    project(at.diag)
    y_step(1)

    d_key[...] = jnp.zeros_like(d_key)
    d_value[...] = jnp.zeros_like(d_value)
    cuts = Sent()
    y_at = 2
    for j in range(4):
        block = pl.ds(j * t, t)
        keys = (j + 1) * t
        for head in range(dims.heads):
            key_at = head // dims.group * HEAD_DIM
            spot = slice(key_at, key_at + HEAD_DIM)
            query = qkv[block, head * HEAD_DIM : (head + 1) * HEAD_DIM]
            key = qkv[:keys, dims.qc + key_at : dims.qc + key_at + HEAD_DIM]
            value = qkv[:keys, dims.qc + kv + key_at : dims.qc + kv + key_at + HEAD_DIM]
            out_grad = mixed_grad[block, head * HEAD_DIM : (head + 1) * HEAD_DIM]
            share = probs[j, head, :keys, :]
            exact = share.astype(F32)
            prob_grad = nt(value, out_grad)
            inner = jnp.sum(exact * prob_grad, axis=0, keepdims=True)
            score_grad = (exact * (prob_grad - inner)).astype(BF16)
            d_query[block, head * HEAD_DIM : (head + 1) * HEAD_DIM] = tn(score_grad, key) * HEAD_DIM**-0.5
            d_key[:keys, spot] += nn(score_grad, query)
            d_value[:keys, spot] += nn(share, out_grad)
    early = pl.ds(0, small_rows)
    for k, peer in enumerate(others):
        cuts.start(k, remote(cut_send.at[peer, early], cut_recv.at[at.e, early], cut_sems, k, "exp", peer))
    own_cut = local_start(cut_send.at[at.e, early], cut_recv.at[at.e, early], local_sems.at[0])

    repeat = (dims.qc + kv) // LANES
    sums = Sent()
    for k, quarter in enumerate((at.diag, at.far, at.sib, at.h)):
        block = rows_at(quarter, t)
        raw = jnp.concatenate([d_query[block, :], d_key[block, :]], axis=1)
        turned = raw * jnp.tile(cosine[block, :], (1, repeat)) - swap_halves(raw) * jnp.tile(
            sine[block, :], (1, repeat)
        )
        d_qkv[block, : dims.qc + kv] = turned.astype(BF16)
        d_qkv[block, dims.qc + kv :] = d_value[block, :].astype(BF16)
        part[quarter] = nt(d_qkv[block, :], ws[:, : dims.attn_cols]).astype(BF16)
        if k == 0:
            sums.start(0, remote(part.at[at.diag], came.at[1], hid_sems, 0, "hid", at.sib))
        if k == 1:
            sums.recv(0)
            for c, half in enumerate(split_parts(t)):
                mid[half, :] = (part[at.far, half].astype(F32) + came[1, half].astype(F32)).astype(BF16)
                sums.start(2 + c, remote(mid.at[half], came_far.at[half], hid_sems, 2 + c, "hid", at.far))
        if k == 2:
            sums.start(1, remote(part.at[at.sib], came.at[0], hid_sems, 1, "hid", at.sib))

    def weight_cols(c, _):
        cols = rows_at(c, 256)
        w_grad[cols, : dims.attn_cols] = tn(normed[:, cols], d_qkv[...])
        w_grad[cols, dims.attn_cols :] = tn(rows_all[:, cols], mixed[...])
        return 0

    lax.fori_loop(0, d // 256, weight_cols, 0)
    w_sum = RingSum(at, w_send, w_recv, shard, w_sems)

    def w_step(s):
        w_sum.put(s, lambda side, owner: w_grad[rows_at(owner, shard), :])
        w_sum.go(s)

    w_step(0)
    if y_at < dims.steps:
        y_step(y_at)
        y_at += 1
    sums.recv(1)
    gain_one = jnp.zeros((1, d), F32)
    ins = Sent()
    own_rows = []
    for c, half in enumerate(split_parts(t)):
        sums.recv(2 + c)
        grad = part[at.h, half].astype(F32) + came[0, half].astype(F32) + came_far[half].astype(F32)
        inputs = x_own[half, :].astype(F32)
        scale = rms(inputs)
        gain_one = gain_one + jnp.sum(grad * inputs * scale, axis=0, keepdims=True)
        weighted = grad * gains[0:1, :]
        in_rows[half, :] = (
            resid_grad[half, :] + scale * weighted
            - inputs * (scale * scale * scale) * jnp.mean(weighted * inputs, axis=-1, keepdims=True)
        ).astype(BF16)
        spot = in_grad.at[pl.ds(pl.multiple_of(at.h * t + half.start, 16), half.size)]
        ins.start(("far", c), remote(in_rows.at[half], spot, in_sems, c, "hid", at.far))
        ins.start(("sib", c), remote(in_rows.at[half], spot, in_sems, 2 + c, "hid", at.sib))
        own_rows.append(local_start(in_rows.at[half], spot, local_sems.at[1 + c]))
    for owner in range(n):
        cols = slice(owner * shard, (owner + 1) * shard)
        cut_send[owner, small_rows:] = jnp.broadcast_to(gain_one[:, cols], (8, shard))
    late = pl.ds(small_rows, 8)
    for k, peer in enumerate(others):
        cuts.start(
            n + k, remote(cut_send.at[peer, late], cut_recv.at[at.e, late], cut_sems, n - 1 + k, "exp", peer)
        )
    own_cut_two = local_start(cut_send.at[at.e, late], cut_recv.at[at.e, late], local_sems.at[4])
    for k in range(count // 2, count):
        send_rest(k)
    w_at = 1
    if w_at < dims.steps:
        w_step(w_at)
        w_at += 1
    for k in range(n - 1):
        cuts.recv(k)
        cuts.recv(n + k)
    own_cut.wait()
    own_cut_two.wait()
    total = cut_recv[0]
    for k in range(1, n):
        total = total + cut_recv[k]
    sum_a[0] = total
    smalls = Sent()
    smalls.start(0, remote(sum_a.at[0], sum_a.at[1], small_sems, 0, "hid", at.sib))
    for c in (0, 1):
        ins.recv(("far", c))
        far_rows = in_grad.at[pl.ds(pl.multiple_of(at.far * t + c * (t // 2), 16), t // 2)]
        ins.start(("on", c), remote(far_rows, far_rows, in_sems, 4 + c, "hid", at.sib))
    smalls.recv(0)
    sum_a[2] = sum_a[0] + sum_a[1]
    smalls.start(1, remote(sum_a.at[2], sum_a.at[3], small_sems, 1, "hid", at.far))
    while y_at < dims.steps:
        y_step(y_at)
        y_at += 1
    while w_at < dims.steps:
        w_step(w_at)
        w_at += 1
    y_sum.arrive_last()
    y_own = y_row(at.e)
    for half in split_parts(t):
        out_rows[half, :] = (resid[half, :] + y_own[half].astype(F32) + y_sum.total(half)).astype(BF16)
    layers = Sent()
    for k, peer in enumerate((at.far, at.diag, at.sib)):
        layers.start(
            k, remote(out_rows.at[:, rows_at(peer, q4)], layer.at[rows_at(at.h, t)], layer_sems, k, "hid", peer)
        )
    own_layer = local_start(out_rows.at[:, rows_at(at.h, q4)], layer.at[rows_at(at.h, t)], local_sems.at[3])
    w_sum.arrive_last()
    for rows_part in split_parts(shard):
        here = pl.ds(pl.multiple_of(at.e * shard + rows_part.start, 16), rows_part.size)
        att_grad[rows_part, :] = w_grad[here, :] + w_sum.total(rows_part)
    smalls.recv(1)
    total = sum_a[2] + sum_a[3]
    small_one[...] = total[:small_rows]
    small_two[...] = total[small_rows:]

    for k in range(count):
        fars.recv(k)
    for k in range(3):
        layers.recv(k)
    for c in (0, 1):
        ins.recv(("sib", c))
        ins.recv(("on", c))
        own_rows[c].wait()
    own_layer.wait()
    for group in (rows, smalls, y_sum, fars, cuts, sums, w_sum, ins, layers):
        group.done()


def out_kernel(
    dims,
    layer_in, in_rows, small_one, small_two, att, own_d, own_g, own_u, sib_d, sib_g, sib_u, far_d, far_g, far_g_rest, far_u,
    layer, in_grad, gain_one, gain_two, wq, wk, wv, wo, router, gate, up, down,
):
    layer[...] = layer_in[...]
    in_grad[...] = in_rows[...].astype(F32)

    def three(own, sib, far):
        return own[0].astype(F32) + sib[0].astype(F32) + far.astype(F32)

    first = pl.program_id(0) < dims.crossing - dims.local
    down[0] = three(own_d, sib_d, far_d[0])
    gate[0] = three(own_g, sib_g, jnp.where(first, far_g[0], far_g_rest[0])).T
    up[0] = three(own_u, sib_u, far_u[0]).T

    @pl.when(pl.program_id(0) == 0)
    def _():
        gain_one[...] = small_two[:1, :]
        gain_two[...] = small_one[dims.experts : dims.experts + 1, :]
        router[...] = small_one[: dims.experts, :]
        qc, kc = dims.qc, dims.kc
        wq[...] = att[:, :qc]
        wk[...] = att[:, qc : qc + kc]
        wv[...] = att[:, qc + kc : qc + 2 * kc]
        wo[...] = att[:, dims.attn_cols :]


def per_device(
    tokens,
    segment_ids,
    routes,
    norm1_gain,
    norm2_gain,
    query_weight,
    key_matrix,
    value_matrix,
    out_weight,
    router_weight,
    gate_weight,
    up_weight,
    down_weight,
    out_grad,
):
    n = lax.axis_size("exp")
    assert lax.axis_size("hid") == 4
    token_count, d = tokens.shape
    local, _, part_ff = gate_weight.shape
    experts = router_weight.shape[1]
    dims = Dims(
        n, token_count, d, experts, local, 4 * part_ff, routes.shape[1], query_weight.shape[1], key_matrix.shape[1]
    )
    t, ff, steps, shard = dims.quarter, dims.ff, dims.steps, dims.shard
    qc, kc = dims.qc, dims.kc

    vmem = pl.BlockSpec(memory_space=pltpu.VMEM)
    anywhere = pl.BlockSpec(memory_space=pl.ANY)
    shape = jax.ShapeDtypeStruct
    dma = pltpu.SemaphoreType.DMA

    (
        ws_all, wg_all, wd_all, wu_cast, g_all, probs, normed, qkv, mixed, cosine, sine, resid, normed_two, coef, gates, kept,
    ) = pl.pallas_call(
        functools.partial(front_kernel, dims),
        out_shape=[
            shape((d, dims.ws_cols), BF16),
            shape((local, d, ff), BF16),
            shape((local, ff, d), BF16),
            shape((local, d, part_ff), BF16),
            shape((n, t, d), BF16),
            shape((4, dims.heads, token_count, t), BF16),
            shape((token_count, d), BF16),
            shape((token_count, dims.attn_cols), BF16),
            shape((token_count, qc), BF16),
            shape((token_count, LANES), F32),
            shape((token_count, LANES), F32),
            shape((t, d), F32),
            shape((t, d), BF16),
            shape((experts, t), F32),
            shape((t, LANES), F32),
            shape((t, LANES), F32),
        ],
        in_specs=[vmem] * 10 + [anywhere] * 4,
        out_specs=[anywhere] * 6 + [vmem] * 10,
        scratch_shapes=[
            pltpu.VMEM((d, dims.ws_cols), BF16),
            pltpu.VMEM((2, local, d, part_ff), F32),
            pltpu.VMEM((2, local, d, part_ff), BF16),
            pltpu.VMEM((local, part_ff, d), F32),
            pltpu.VMEM((local, part_ff, d), BF16),
            pltpu.VMEM((8, token_count), jnp.int32),
            pltpu.VMEM((4, dims.heads, token_count, t), BF16),
            pltpu.VMEM((4, t, d), BF16),
            pltpu.VMEM((2, t, d), BF16),
            pltpu.VMEM((t, d), BF16),
            pltpu.VMEM((t, d), BF16),
            dma((2, 4 * steps)),
            dma((2, 4 * steps)),
            dma((2, 4)),
            dma((2, 3)),
            dma((2, 3 * dims.early)),
            dma((8,)),
            dma((4,)),
            dma((dims.early,)),
        ],
        compiler_params=pltpu.CompilerParams(
            collective_id=0, has_side_effects=True, vmem_limit_bytes=VMEM_LIMIT
        ),
    )(
        tokens, segment_ids, routes.T, query_weight, key_matrix, value_matrix, out_weight, router_weight.T,
        norm1_gain[None, :], norm2_gain[None, :], out_grad, gate_weight, up_weight, down_weight,
    )

    big = n * t * d * 2 > 6 * 2**20
    jobs, crossing = dims.jobs, dims.crossing
    (dx, y_all, gate_grad, own, sib, own_rest, sib_rest, far, _) = pl.pallas_call(
        functools.partial(moe_kernel, dims, big),
        out_shape=[
            shape((t, d), F32),
            shape((n, t, d), BF16),
            shape((n, 8, t), F32),
            shape((jobs, part_ff, d), BF16),
            shape((jobs, part_ff, d), BF16),
            shape((jobs - crossing, part_ff, d), BF16),
            shape((jobs - crossing, part_ff, d), BF16),
            shape((crossing, part_ff, d), BF16),
            shape((n * t if big else 16, d), BF16),
        ],
        in_specs=[vmem, vmem] + [anywhere] * 4,
        out_specs=[vmem] + [anywhere] * 8,
        scratch_shapes=[
            pltpu.VMEM((16 if big else n * t, d), BF16),
            pltpu.VMEM((1, 16, d) if big else (n, t, d), BF16),
            pltpu.VMEM((n, experts, t), F32),
            pltpu.VMEM((local, d, ff), BF16),
            pltpu.VMEM((local, d, ff), BF16),
            pltpu.VMEM((local, ff, d), BF16),
            pltpu.VMEM((local, n * t, ff), BF16),
            pltpu.VMEM((local, n * t, ff), BF16),
            pltpu.VMEM((local, n * t, ff), BF16),
            pltpu.VMEM((2, 2, t, d), BF16),
            pltpu.VMEM((2, steps, t, d), BF16),
            pltpu.VMEM((n, 8, t), F32),
            pltpu.VMEM((2, max(ff, t), d), BF16),
            pltpu.VMEM((t, d) if big else (16, LANES), BF16),
            pltpu.VMEM((t, d) if big else (16, LANES), BF16),
            dma((2, 4 * steps)),
            dma((2, 4 * steps)),
            dma((2, 4 * steps)),
            dma((2, n - 1)),
            dma((2, 3 * local)),
            dma((2, 2 * jobs)),
            dma((2, crossing)),
            dma((6,)),
            dma((4,)),
            dma((2,)),
            dma((local,)),
            pltpu.SemaphoreType.REGULAR,
        ],
        compiler_params=pltpu.CompilerParams(
            collective_id=1, has_side_effects=True, vmem_limit_bytes=VMEM_LIMIT
        ),
    )(normed_two, coef, g_all, wg_all, wd_all, wu_cast)

    small_rows = experts + 8
    att = dims.attn_cols + qc
    (layer, in_rows, small_one, small_two, att_grad, far_rest) = pl.pallas_call(
        functools.partial(back_kernel, dims, big),
        out_shape=[
            shape((token_count, d // 4), BF16),
            shape((token_count, d), BF16),
            shape((small_rows, shard), F32),
            shape((8, shard), F32),
            shape((shard, att), F32),
            shape((jobs - crossing, part_ff, d), BF16),
        ],
        in_specs=[vmem] * 6 + [anywhere] * 12,
        out_specs=[anywhere] * 2 + [vmem] * 3 + [anywhere],
        scratch_shapes=[
            pltpu.VMEM((d, dims.ws_cols), BF16),
            pltpu.VMEM((token_count, dims.attn_cols), BF16),
            pltpu.VMEM((token_count, qc), BF16),
            pltpu.VMEM((token_count, d), BF16),
            pltpu.VMEM((token_count, LANES), F32),
            pltpu.VMEM((token_count, LANES), F32),
            pltpu.VMEM((4, dims.heads, token_count, t), BF16),
            pltpu.VMEM((t, d), BF16),
            pltpu.VMEM((t, d), BF16),
            pltpu.VMEM((t, d), F32),
            pltpu.VMEM((token_count, d), BF16),
            pltpu.VMEM((token_count, qc), BF16),
            pltpu.VMEM((token_count, qc), F32),
            pltpu.VMEM((token_count, kc), F32),
            pltpu.VMEM((token_count, kc), F32),
            pltpu.VMEM((token_count, dims.attn_cols), BF16),
            pltpu.VMEM((d, att), F32),
            pltpu.VMEM((4, t, d), BF16),
            pltpu.VMEM((2, t, d), BF16),
            pltpu.VMEM((t, d), BF16),
            pltpu.VMEM((t, d), BF16),
            pltpu.VMEM((1 if big else n, t, d), BF16),
            pltpu.VMEM((2, 2, t, d), BF16),
            pltpu.VMEM((2, steps, t, d), BF16),
            pltpu.VMEM((2, 2, shard, att), BF16),
            pltpu.VMEM((2, steps, shard, att), BF16),
            pltpu.VMEM((t, d), BF16),
            pltpu.VMEM((t, d), BF16),
            pltpu.VMEM((4, small_rows + 8, shard), F32),
            pltpu.VMEM((n, small_rows + 8, shard), F32),
            pltpu.VMEM((n, small_rows + 8, shard), F32),
            pltpu.VMEM((2, jobs - crossing, part_ff, d), BF16),
            dma((2, 6)),
            dma((2, 4 * steps)),
            dma((2, 4 * steps)),
            dma((2, 4)),
            dma((2, 6)),
            dma((2, 3)),
            dma((2, 2)),
            dma((2, 2 * (n - 1))),
            dma((2, jobs - crossing)),
            dma((6,)),
            dma((15,)),
        ],
        compiler_params=pltpu.CompilerParams(
            collective_id=2, has_side_effects=True, vmem_limit_bytes=VMEM_LIMIT
        ),
    )(
        dx, gate_grad.reshape(n * 8, t), gates, kept, resid, normed_two, g_all, tokens, ws_all, qkv, mixed, normed, cosine, sine,
        probs, y_all, own_rest, sib_rest,
    )

    rows = token_count // local

    def whole(shape_):
        return pl.BlockSpec(shape_, lambda i: (0,) * len(shape_))

    def matrix(index):
        return pl.BlockSpec((1, part_ff, d), lambda i: (index(i), 0, 0))

    (
        layer, in_grad, gain_one, gain_two, wq, wk, wv, wo, router, gate, up, down,
    ) = pl.pallas_call(
        functools.partial(out_kernel, dims),
        grid=(local,),
        out_shape=[
            shape((token_count, d // 4), BF16),
            shape((token_count, d), F32),
            shape((1, shard), F32),
            shape((1, shard), F32),
            shape((shard, qc), F32),
            shape((shard, kc), F32),
            shape((shard, kc), F32),
            shape((shard, qc), F32),
            shape((experts, shard), F32),
            shape((local, d, part_ff), F32),
            shape((local, d, part_ff), F32),
            shape((local, part_ff, d), F32),
        ],
        in_specs=[
            pl.BlockSpec((rows, d // 4), lambda i: (i, 0)),
            pl.BlockSpec((rows, d), lambda i: (i, 0)),
            whole((small_rows, shard)),
            whole((8, shard)),
            whole((shard, att)),
            matrix(lambda i: i),
            matrix(lambda i: local + i),
            matrix(lambda i: 2 * local + i),
            matrix(lambda i: i),
            matrix(lambda i: local + i),
            matrix(lambda i: 2 * local + i),
            matrix(lambda i: i),
            matrix(lambda i: jnp.minimum(local + i, crossing - 1)),
            matrix(lambda i: jnp.maximum(local + i - crossing, 0)),
            matrix(lambda i: 2 * local + i - crossing),
        ],
        out_specs=[
            pl.BlockSpec((rows, d // 4), lambda i: (i, 0)),
            pl.BlockSpec((rows, d), lambda i: (i, 0)),
            whole((1, shard)),
            whole((1, shard)),
            whole((shard, qc)),
            whole((shard, kc)),
            whole((shard, kc)),
            whole((shard, qc)),
            whole((experts, shard)),
            pl.BlockSpec((1, d, part_ff), lambda i: (i, 0, 0)),
            pl.BlockSpec((1, d, part_ff), lambda i: (i, 0, 0)),
            pl.BlockSpec((1, part_ff, d), lambda i: (i, 0, 0)),
        ],
        compiler_params=pltpu.CompilerParams(vmem_limit_bytes=VMEM_LIMIT),
    )(layer, in_rows, small_one, small_two, att_grad, own, own, own, sib, sib, sib, far, far, far_rest, far_rest)

    return (layer, in_grad, gain_one[0], gain_two[0], wq, wk, wv, wo, router.T, gate, up, down)


def solution(mesh):
    in_specs = (
        P("exp", None),
        P("exp", None),
        P("exp", None),
        P("exp"),
        P("exp"),
        P("exp", "hid"),
        P("exp", "hid"),
        P("exp", "hid"),
        P("exp", "hid"),
        P("exp", None),
        P("exp", None, "hid"),
        P("exp", None, "hid"),
        P("exp", "hid", None),
        P("exp", "hid"),
    )
    out_specs = (
        P("exp", "hid"),
        P("exp", None),
        P("exp"),
        P("exp"),
        P("exp", "hid"),
        P("exp", "hid"),
        P("exp", "hid"),
        P("exp", "hid"),
        P("exp", None),
        P("exp", None, "hid"),
        P("exp", None, "hid"),
        P("exp", "hid", None),
    )
    return jax.shard_map(
        per_device, mesh=mesh, in_specs=in_specs, out_specs=out_specs, check_vma=False
    )
```

```python
import functools
import math

import jax
import jax.numpy as jnp
from jax import lax
from jax.experimental import pallas as pl
from jax.experimental.pallas import tpu as pltpu
from jax.sharding import PartitionSpec as P

HEAD_DIM = 64
SEGS = 4
EPSILON = 1e-05
ROPE_BASE = 10000.0
NEG_FILL = -1e30
LANES = 128
MESH = pl.DeviceIdType.MESH
F32 = jnp.float32
BF16 = jnp.bfloat16
VMEM_LIMIT = 62 * 2**20


def nn(a, b):
    return lax.dot_general(a, b, (((1,), (0,)), ((), ())), preferred_element_type=F32)


def nt(a, b):
    return lax.dot_general(a, b, (((1,), (1,)), ((), ())), preferred_element_type=F32)


def tn(a, b):
    return lax.dot_general(a, b, (((0,), (0,)), ((), ())), preferred_element_type=F32)


def tn_exact(a, b):
    return lax.dot_general(
        a, b, (((0,), (0,)), ((), ())), preferred_element_type=F32, precision=lax.Precision.HIGHEST
    )


def iota(shape, dim):
    return lax.broadcasted_iota(jnp.int32, shape, dim)


def rows_at(index, size):
    return pl.ds(pl.multiple_of(index * size, size), size)


def pos_of(index, n):
    odd = index % 2
    return (1 - odd) * (index // 2) + odd * (n - 1 - index // 2)


def at_pos(pos, n):
    back = pos // (n // 2)
    return (1 - back) * (2 * pos) + back * (2 * (n - 1 - pos) + 1)


class Place:
    def __init__(self, n):
        self.n = n
        self.e = lax.axis_index("exp")
        self.h = lax.axis_index("hid")
        self.p = pos_of(self.e, n)
        self.right = self.ring(1)
        self.left = self.ring(-1)
        self.sib = self.h + 1 - 2 * (self.h % 2)
        self.far = (self.h + 2) % 4
        self.diag = (self.sib + 2) % 4

    def ring(self, away):
        return at_pos((self.p + self.n + away) % self.n, self.n)


def greet(exp_peers, hid_peers):
    barrier = pltpu.get_barrier_semaphore()
    for peer in exp_peers:
        pl.semaphore_signal(barrier, inc=1, device_id={"exp": peer}, device_id_type=MESH)
    for peer in hid_peers:
        pl.semaphore_signal(barrier, inc=1, device_id={"hid": peer}, device_id_type=MESH)
    pl.semaphore_wait(barrier, len(exp_peers) + len(hid_peers))


def remote(src, dst, sems, k, axis, to):
    return pltpu.make_async_remote_copy(
        src_ref=src,
        dst_ref=dst,
        send_sem=sems.at[0, k],
        recv_sem=sems.at[1, k],
        device_id={axis: to},
        device_id_type=MESH,
    )


class Sent:
    def __init__(self):
        self.copies = {}
        self.unsent = []

    def start(self, key, copy):
        copy.start()
        self.copies[key] = copy
        self.unsent.append(copy)

    def recv(self, key):
        self.copies[key].wait_recv()

    def done(self):
        for copy in self.unsent:
            copy.wait_send()
        self.unsent = []


class RingGather:
    def __init__(self, place, view, rows, sems):
        self.place, self.view, self.rows, self.sems = place, view, rows, sems
        self.steps = place.n // 2
        self.sent = Sent()

    def part(self, s, c):
        half = self.rows // 2
        for side in (0, 1):
            if s:
                self.sent.recv((s - 1, side, c))
            if s < self.steps - 1 or c == side:
                away, to = ((-s, self.place.right), (s, self.place.left))[side]
                block = self.view(self.place.ring(away), c * half, half)
                self.sent.start((s, side, c), remote(block, block, self.sems, 4 * s + 2 * side + c, "exp", to))

    def start(self, s):
        self.part(s, 0)
        self.part(s, 1)

    def recv_last(self):
        self.sent.recv((self.steps - 1, 0, 0))
        self.sent.recv((self.steps - 1, 1, 1))

    def done(self):
        self.sent.done()


class RingSum:
    def __init__(self, place, send, recv, rows, sems):
        self.place, self.send, self.recv, self.rows, self.sems = place, send, recv, rows, sems
        self.steps = place.n // 2
        self.copies = {}

    def owner(self, s, side):
        away = self.steps - s
        return self.place.ring(away if side == 0 else -away)

    def chunks(self, s):
        for c in (0, 1):
            for side in (0, 1):
                if s > 0 or c == side:
                    yield c, side

    def put(self, s, get):
        if s >= 2:
            for c, side in self.chunks(s - 2):
                self.copies[(s - 2, side, c)].wait_send()
        if s == 0:
            half = self.rows // 2
            terms = get(0, self.owner(0, 0)).astype(self.send.dtype)
            self.send[0, 0, pl.ds(0, half)] = terms[:half]
            self.send[1, 0, pl.ds(half, half)] = terms[half:]
            return
        for side in (0, 1):
            self.send[side, s % 2] = get(side, self.owner(s, side)).astype(self.send.dtype)

    def part(self, s, c):
        half = self.rows // 2
        rows = pl.ds(c * half, half)
        for side in (0, 1):
            if s == 0 and c != side:
                continue
            src = self.send.at[side, s % 2, rows]
            if s > 1 or (s == 1 and c == side):
                self.copies[(s - 1, side, c)].wait_recv()
                came = self.recv[side, s - 1, rows].astype(F32)
                src[...] = (src[...].astype(F32) + came).astype(src.dtype)
            to = self.place.left if side else self.place.right
            copy = remote(src, self.recv.at[side, s, rows], self.sems, 4 * s + 2 * side + c, "exp", to)
            copy.start()
            self.copies[(s, side, c)] = copy

    def go(self, s):
        self.part(s, 0)
        self.part(s, 1)

    def arrive_last(self):
        for c, side in self.chunks(self.steps - 1):
            self.copies[(self.steps - 1, side, c)].wait_recv()

    def total(self, part):
        return self.recv[0, self.steps - 1, part].astype(F32) + self.recv[1, self.steps - 1, part].astype(F32)

    def done(self):
        for s in range(self.steps - 2, self.steps):
            for c, side in self.chunks(s):
                self.copies[(s, side, c)].wait_send()


def local_start(src, dst, sem):
    copy = pltpu.make_async_copy(src, dst, sem)
    copy.start()
    return copy


def split_parts(count):
    return (pl.ds(0, count // 2), pl.ds(count // 2, count // 2))


def rms(values):
    return lax.rsqrt(jnp.mean(values * values, axis=-1, keepdims=True) + EPSILON)


def swap_halves(values):
    half = HEAD_DIM // 2
    width = values.shape[1]
    up = pltpu.roll(values, width - half, 1)
    down = pltpu.roll(values, half, 1)
    first = iota(values.shape, 1) % HEAD_DIM < half
    return jnp.where(first, up, down)


def gain_rows(slab, expert_count):
    pick = (iota((16, LANES), 1) == iota((16, LANES), 0) + expert_count).astype(BF16)
    return nt(pick, slab)


def bias_block(begin_row, first_row, key_count):
    shape = (key_count, begin_row.shape[1])
    keys = iota(shape, 0)
    seen = (keys >= begin_row) & (keys <= first_row + iota(shape, 1))
    return jnp.where(seen, 0.0, NEG_FILL)


class Dims:
    def __init__(self, n, token_count, width, expert_count, local_experts, ff, topk, qc, kc):
        self.n, self.tokens, self.d = n, token_count, width
        self.experts, self.local, self.ff, self.topk = expert_count, local_experts, ff, topk
        self.qc, self.kc = qc, kc
        self.quarter = token_count // 4
        self.shard = width // n
        self.capacity = token_count * topk * 5 // (4 * expert_count)
        self.attn_cols = qc + 2 * kc
        self.slab_at = 2 * qc + 2 * kc
        self.ws_cols = self.slab_at + LANES
        self.heads = qc // HEAD_DIM
        self.group = qc // kc
        self.part_ff = ff // 4
        self.steps = n // 2
        self.jobs = 3 * local_experts
        self.crossing = self.jobs * 7 // 12
        self.early = 2 * local_experts


def tall(row, count):
    return jnp.broadcast_to(row, (LANES, row.shape[1])).T[:, :count]


def front_kernel(
    dims,
    x, seg, routes, wq, wk, wv, wo, router, gain_one, gain_two, g, wg, wu, wd,
    ws_out, wg_all, wd_all, wu_cast, g_all, probs_out, normed, qkv, mixed, cosine, sine, resid, normed_two, coef, gates, kept,
    ws_all, wide, cast, wide_down, cast_down, begin, probs, part, came, mid, came_far,
    ws_sems, g_sems, hid_sems, swap_sems, weight_sems, local_sems, probs_sems, own_sems,
):
    at = Place(dims.n)
    t, d, ff4, shard, tokens = dims.quarter, dims.d, dims.part_ff, dims.shard, dims.tokens
    q4 = d // 4
    kv = dims.kc
    loads = [local_start(ref, wide.at[k], local_sems.at[k]) for k, ref in enumerate((wg, wu))]
    load_down = local_start(wd, wide_down, local_sems.at[2])

    mine = rows_at(at.e, shard)
    at_col = 0
    for ref in (wq, wk, wv, wo):
        ws_all[mine, at_col : at_col + ref.shape[1]] = ref[...].astype(BF16)
        at_col += ref.shape[1]
    lane = iota((shard, LANES), 1)
    slab = jnp.concatenate([router[...], jnp.zeros((LANES - dims.experts, shard), F32)], axis=0).T
    slab = jnp.where(lane == dims.experts, tall(gain_one[...], LANES), slab)
    slab = jnp.where(lane == dims.experts + 1, tall(gain_two[...], LANES), slab)
    ws_all[mine, dims.slab_at :] = slab.astype(BF16)

    greet((at.right, at.left), (at.sib, at.far, at.diag))
    ring = RingGather(at, lambda o, f, s: ws_all.at[pl.ds(pl.multiple_of(o * shard + f, 16), s)], shard, ws_sems)
    ring.start(0)

    swaps = Sent()
    for k, peer in enumerate((at.sib, at.far, at.diag)):
        swaps.start(
            k, remote(g.at[rows_at(peer, t)], g_all.at[at.e, :, rows_at(at.h, q4)], swap_sems, k, "hid", peer)
        )
    g_own = local_start(g.at[rows_at(at.h, t)], g_all.at[at.e, :, rows_at(at.h, q4)], local_sems.at[3])

    moves = Sent()
    kept_own = []
    units = [(0, i) for i in range(dims.local)] + [(1, i) for i in range(dims.local)]
    lot = (6 * len(units) + 7) // 8

    def source(u):
        k, i = units[u]
        return cast_down.at[i] if k else cast.at[0, i]

    def spot(u, owner):
        k, i = units[u]
        return wd_all.at[i, rows_at(owner, ff4), :] if k else wg_all.at[i, :, rows_at(owner, ff4)]

    def send_unit(u):
        moves.start(("far", u), remote(source(u), spot(u, at.h), weight_sems, u, "hid", at.far))

    def pass_on(u):
        moves.recv(("far", u))
        block = spot(u, at.far)
        moves.start(("on", u), remote(block, block, weight_sems, len(units) + u, "hid", at.sib))

    loads[0].wait()
    cast[0] = wide[0].astype(BF16)
    for u in range(min(lot, dims.local)):
        send_unit(u)
    load_down.wait()
    cast_down[...] = wide_down[...].astype(BF16)
    for u in range(min(lot, dims.local), lot):
        send_unit(u)
    for u in range(len(units)):
        moves.start(
            ("sib", u), remote(source(u), spot(u, at.h), weight_sems, 2 * len(units) + u, "hid", at.sib)
        )
        kept_own.append(local_start(source(u), spot(u, at.h), own_sems.at[u]))

    ring.start(1)
    for k in range(3):
        swaps.recv(k)
    g_own.wait()
    g_ring = RingGather(at, lambda o, f, s: g_all.at[o, pl.ds(f, s)], t, g_sems)

    counts = [jnp.sum((seg[...] == k).astype(F32), axis=1, keepdims=True) for k in range(SEGS)]
    first = jnp.zeros((1, tokens), F32)
    total = jnp.zeros((1, 1), F32)
    for k in range(SEGS):
        first = first + jnp.where(seg[...] == k, total, 0.0)
        total = total + counts[k]
    begin[...] = jnp.broadcast_to(first, (8, tokens)).astype(jnp.int32)
    lane = iota((1, LANES), 1)
    half = HEAD_DIM // 2
    freqs = jnp.exp((lane % half).astype(F32) * (-math.log(ROPE_BASE) / half))
    positions = iota((1, tokens), 1).astype(F32) - first

    def table(j):
        rows = pl.ds(j * t, t)
        angles = tall(positions[:, j * t : (j + 1) * t], LANES) * freqs
        cosine[rows, :] = jnp.cos(angles)
        sine[rows, :] = jnp.where(lane % HEAD_DIM < half, -1.0, 1.0) * jnp.sin(angles)

    todo = [functools.partial(table, j) for j in range(4)]

    for s in range(2, dims.steps):
        if todo:
            todo.pop(0)()
            todo.pop(0)()
        ring.start(s)
    for job in todo:
        job()
    loads[1].wait()
    cast[1] = wide[1].astype(BF16)
    saves = [local_start(cast.at[1], wu_cast, local_sems.at[4])]
    ring.recv_last()
    out_ws = local_start(ws_all, ws_out, local_sems.at[6])

    g_ring.start(0)

    slab = ws_all[:, dims.slab_at :]
    gains = gain_rows(slab, dims.experts)
    repeat = (dims.qc + kv) // LANES
    for j in range(4):
        rows = pl.ds(j * t, t)
        values = x[rows, :].astype(F32)
        block = (values * rms(values) * gains[0:1, :]).astype(BF16)
        normed[rows, :] = block
        raw = nn(block, ws_all[:, : dims.attn_cols])
        turned = raw[:, : dims.qc + kv]
        turned = turned * jnp.tile(cosine[rows, :], (1, repeat)) + swap_halves(turned) * jnp.tile(
            sine[rows, :], (1, repeat)
        )
        queries = turned[:, : dims.qc].astype(BF16) * jnp.asarray(HEAD_DIM**-0.5, BF16)
        qkv[rows, : dims.qc] = queries
        qkv[rows, dims.qc : dims.qc + kv] = turned[:, dims.qc :].astype(BF16)
        qkv[rows, dims.qc + kv :] = raw[:, dims.qc + kv :].astype(BF16)

    for j in range(4):
        rows = pl.ds(j * t, t)
        keys = (j + 1) * t
        bias = bias_block(begin[:1, j * t : (j + 1) * t], j * t, keys)
        for head in range(dims.heads):
            key_at = dims.qc + head // dims.group * HEAD_DIM
            query = qkv[rows, head * HEAD_DIM : (head + 1) * HEAD_DIM]
            key = qkv[:keys, key_at : key_at + HEAD_DIM]
            value = qkv[:keys, key_at + kv : key_at + kv + HEAD_DIM]
            scores = nt(key, query) + bias
            powers = jnp.exp(scores - jnp.max(scores, axis=0, keepdims=True))
            share = (powers * (1.0 / jnp.sum(powers, axis=0, keepdims=True))).astype(BF16)
            probs[j, head, :keys, :] = share
            mixed[rows, head * HEAD_DIM : (head + 1) * HEAD_DIM] = tn(value, share).T.astype(BF16)
        saves.append(
            local_start(probs.at[j, :, pl.ds(0, keys)], probs_out.at[j, :, pl.ds(0, keys)], probs_sems.at[j])
        )

    g_ring.start(1)
    wo_all = ws_all.at[:, pl.ds(dims.attn_cols, dims.qc)]
    sums = Sent()
    for k, quarter in enumerate((at.diag, at.far, at.sib, at.h)):
        part[quarter] = nt(mixed[rows_at(quarter, t), :], wo_all[...]).astype(BF16)
        if k == 0:
            sums.start(0, remote(part.at[at.diag], came.at[1], hid_sems, 0, "hid", at.sib))
        if k == 1:
            sums.recv(0)
            for c, rows in enumerate(split_parts(t)):
                mid[rows, :] = (part[at.far, rows].astype(F32) + came[1, rows].astype(F32)).astype(BF16)
                sums.start(2 + c, remote(mid.at[rows], came_far.at[rows], hid_sems, 2 + c, "hid", at.far))
        if k == 2:
            sums.start(1, remote(part.at[at.sib], came.at[0], hid_sems, 1, "hid", at.sib))
    g_ring.start(2)
    for u in range(lot):
        pass_on(u)

    expert = iota((dims.experts, tokens), 0)
    chosen = jnp.zeros((dims.experts, tokens), F32)
    for k in range(dims.topk):
        chosen = chosen + (routes[k : k + 1, :] == expert).astype(F32)
    earlier = (iota((tokens, t), 0) < iota((tokens, t), 1) + at.h * t).astype(BF16)
    rank = nn(chosen.astype(BF16), earlier)
    expert = iota((dims.experts, t), 0)
    own_routes = routes[:, rows_at(at.h, t)]
    mine = jnp.zeros((dims.experts, t), F32)
    for k in range(dims.topk):
        mine = mine + (own_routes[k : k + 1, :] == expert).astype(F32)
    keep = mine * (rank < dims.capacity).astype(F32)
    rest = jnp.zeros((LANES - dims.experts, t), F32)
    mine = jnp.concatenate([mine, rest], axis=0).T
    keep = jnp.concatenate([keep, rest], axis=0).T
    kept[...] = keep

    sums.recv(1)
    for c, rows in enumerate(split_parts(t)):
        sums.recv(2 + c)
        first = pl.ds(pl.multiple_of(at.h * t + rows.start, 16), rows.size)
        values = (
            part[at.h, rows].astype(F32) + came[0, rows].astype(F32) + came_far[rows].astype(F32)
            + x[first, :].astype(F32)
        )
        resid[rows, :] = values
        normed_two[rows, :] = (values * rms(values) * gains[1:2, :]).astype(BF16)
    for u in range(lot, len(units)):
        send_unit(u)
    logits = nn(normed_two[...], slab)
    for s in range(3, dims.steps):
        g_ring.start(s)
    picked = jnp.where(mine > 0, logits, NEG_FILL)
    powers = jnp.exp(picked - jnp.max(picked, axis=1, keepdims=True)) * mine
    gate = powers / jnp.sum(powers, axis=1, keepdims=True)
    gates[...] = gate
    coef[...] = (gate * keep).T[: dims.experts, :]

    for u in range(lot, len(units)):
        pass_on(u)
    for u in range(len(units)):
        moves.recv(("sib", u))
        kept_own[u].wait()
    for u in range(len(units)):
        moves.recv(("on", u))
    g_ring.recv_last()
    for copy in saves:
        copy.wait()
    out_ws.wait()
    for group in (ring, g_ring, swaps, moves, sums):
        group.done()


def moe_kernel(
    dims, big,
    x_own, coef_own, g_all, wg_in, wd_in, wu_own,
    dx, y_all, gate_grad, own_out, sib_out, own_far, sib_far, far_out, x_far,
    x_near, g_near, coef, wg, wu, wd, d_gate, d_up, hid, send, recv, grads, stage, x_stage, g_stage,
    x_sems, c_sems, sum_sems, grad_sems, wd_sems, job_sems, far_sems, local_sems, keep_sems, y_sems, own_sems, free_sem,
):
    at = Place(dims.n)
    n, t, d, local, ff, ff4 = dims.n, dims.quarter, dims.d, dims.local, dims.ff, dims.part_ff
    others = tuple((at.e + k) % n for k in range(1, n))
    load_gate = local_start(wg_in, wg, local_sems.at[1])
    load_down = local_start(wd_in, wd, local_sems.at[2])
    if not big:
        load_g = local_start(g_all, g_near, local_sems.at[4])
    xs = x_far if big else x_near
    coef[at.e] = coef_own[...]
    if big:
        local_start(x_own, xs.at[rows_at(at.e, t)], local_sems.at[0]).wait()
    else:
        xs[rows_at(at.e, t), :] = x_own[...]
    greet(others, (at.sib, at.far))

    x_ring = RingGather(at, lambda o, f, s: xs.at[pl.ds(pl.multiple_of(o * t + f, 16), s)], t, x_sems)
    c_ring = RingGather(at, lambda o, f, s: coef.at[o, pl.ds(f, s)], dims.experts, c_sems)
    c_ring.start(0)
    x_ring.start(0)

    late = local

    def source(u):
        return wu_own.at[u]

    def spot(u, owner):
        return wu.at[u, :, rows_at(owner, ff4)]

    downs = Sent()
    kept_own = []
    for u in range(late):
        downs.start(("far", u), remote(source(u), spot(u, at.h), wd_sems, u, "hid", at.far))
    for u in range(late):
        downs.start(("sib", u), remote(source(u), spot(u, at.h), wd_sems, late + u, "hid", at.sib))
        kept_own.append(local_start(source(u), spot(u, at.h), own_sems.at[u]))

    def arrive():
        for u in range(late):
            downs.recv(("far", u))
            block = spot(u, at.far)
            downs.start(("on", u), remote(block, block, wd_sems, 2 * late + u, "hid", at.sib))
        for u in range(late):
            downs.recv(("sib", u))
            kept_own[u].wait()
            downs.recv(("on", u))

    def x_row(owner):
        if not big:
            return xs.at[rows_at(owner, t)]
        local_start(xs.at[rows_at(owner, t)], x_stage, local_sems.at[0]).wait()
        return x_stage

    def g_row(owner):
        if not big:
            return g_near.at[owner]
        local_start(g_all.at[owner], g_stage, local_sems.at[4]).wait()
        return g_stage

    lane = iota((t, LANES), 1)

    def gate_products(owner):
        rows = rows_at(owner, t)
        inputs = x_row(owner)
        for i in range(local):
            d_gate[i, rows, :] = nn(inputs[...], wg[i]).astype(BF16)

    def back_products(i):
        def one(r, _):
            hid[i, rows_at(r, t), :] = nt(g_row(r)[...], wd[i]).astype(BF16)
            return 0

        lax.fori_loop(0, n, one, 0)

    def work(owner, which, fresh):
        rows = rows_at(owner, t)
        inputs = x_row(owner)
        columns = jnp.concatenate([coef[owner], jnp.zeros((LANES - dims.experts, t), F32)], axis=0).T
        for i in which:
            share = jnp.sum(jnp.where(lane == at.e * local + i, columns, 0.0), axis=1, keepdims=True)
            pre_gate = nn(inputs[...], wg[i]) if fresh else d_gate[i, rows, :].astype(F32)
            pre_up = nn(inputs[...], wu[i])
            back = hid[i, rows, :].astype(F32)
            sig = 0.5 * jnp.tanh(0.5 * pre_gate) + 0.5
            silu = pre_gate * sig
            hidden = silu * pre_up
            own = jnp.sum(hidden * back, axis=1, keepdims=True)
            grads[owner, i : i + 1, :] = jnp.broadcast_to(own, (t, LANES)).T[:1, :]
            back = share * back
            d_up[i, rows, :] = (back * silu).astype(BF16)
            d_gate[i, rows, :] = (back * pre_up * (sig + silu * (1.0 - sig))).astype(BF16)
            hid[i, rows, :] = (share * hidden).astype(BF16)

    def layer_row(owner, slot):
        rows = rows_at(owner, t)
        stage[slot, :t, :] = sum(nn(hid[i, rows, :], wd[i]) for i in range(local)).astype(BF16)
        local_start(stage.at[slot, pl.ds(0, t)], y_all.at[owner], y_sems.at[slot])

    def y_wait(slot):
        pltpu.make_async_copy(stage.at[slot, pl.ds(0, t)], y_all.at[0], y_sems.at[slot]).wait()

    def side_row(away, k):
        return at_pos((at.p + n + (2 * k - 1) * away) % n, n)

    def both(away, do):
        def one(k, _):
            do(side_row(away, k), k)
            return 0

        lax.fori_loop(0, 2, one, 0)

    def near(which):
        def one(k, _):
            work(at_pos((at.p + n + k - 1) % n, n), which, False)
            return 0

        lax.fori_loop(0, 3, one, 0)

    steps = dims.steps
    load_gate.wait()
    gate_products(at.e)
    if not big:
        load_g.wait()
    load_down.wait()
    for i in range(local - 1):
        back_products(i)
    x_ring.part(1, 0)
    back_products(local - 1)
    x_ring.part(1, 1)
    c_ring.start(1)
    both(1, lambda owner, k: gate_products(owner))
    arrive()
    for s in range(2, steps):
        x_ring.part(s, 0)
        if s == 2:
            near((0,))
        x_ring.part(s, 1)
        c_ring.start(s)
        if s == 2 and local > 1:
            near(range(1, local))
        both(s, lambda owner, k: work(owner, range(local), True))
    layer_row(at.e, 0)
    y_wait(0)
    for away in range(1, steps):
        both(away, layer_row)
        for slot in (0, 1):
            y_wait(slot)
    c_ring.recv_last()
    x_ring.recv_last()
    last = side_row(steps, 1)
    work(last, range(local), True)
    layer_row(last, 0)
    y_wait(0)

    small = Sent()
    for k, peer in enumerate(others):
        small.start(k, remote(grads.at[peer], gate_grad.at[at.e], grad_sems, k, "exp", peer))
    own_small = local_start(grads.at[at.e], gate_grad.at[at.e], local_sems.at[5])

    sources = (hid, d_gate, d_up)
    jobs = [(kind, i) for kind in range(3) for i in range(local)]
    crossing = dims.crossing
    flights, kept = {}, {}

    def spare(k):
        return wd.at[k // 4, pl.ds(k % 4 * ff4, ff4)]

    downs.done()
    pl.semaphore_signal(free_sem, inc=1, device_id={"hid": at.sib}, device_id_type=MESH)
    pl.semaphore_wait(free_sem, 1)


    def job(k):
        kind, i = jobs[k]
        slot = k % 2
        if k >= 2:
            for copy in flights[k - 2]:
                copy.wait_send()
            for copy in kept[k - 2]:
                copy.wait()
        left = sources[kind]
        for f in range(ff // 256):
            units = slice(f * 256, (f + 1) * 256)
            if big:
                def add(r, total, units=units):
                    right = g_row(r) if kind == 0 else x_row(r)
                    return total + tn(left[i, rows_at(r, t), units], right[...])

                value = lax.fori_loop(0, n, add, jnp.zeros((256, d), F32))
            else:
                right = g_near.reshape(n * t, d) if kind == 0 else xs
                value = tn(left[i, :, units], right[...])
            stage[slot, units, :] = value.astype(BF16)
        flights[k], kept[k] = [], []
        if k < crossing:
            far_room = ((at.diag, at.far), (spare(2 * k + 1), spare(2 * k)))
        else:
            far_room = ((at.diag, at.far), (sib_far.at[k - crossing], own_far.at[k - crossing]))
        for which, ((there, here), (sib_spot, own_spot)) in enumerate(
            (((at.sib, at.h), (sib_out.at[k], own_out.at[k])), far_room)
        ):
            copy = remote(stage.at[slot, rows_at(there, ff4)], sib_spot, job_sems, 2 * k + which, "hid", at.sib)
            copy.start()
            flights[k].append(copy)
            kept[k].append(
                local_start(stage.at[slot, rows_at(here, ff4)], own_spot, keep_sems.at[2 * slot + which])
            )

    fars = Sent()

    def cross(k):
        flights[k][1].wait_recv()
        if k >= done_jobs - 2:
            kept[k].pop().wait()
        one, two = spare(2 * k), spare(2 * k + 1)
        one[...] = (one[...].astype(F32) + two[...].astype(F32)).astype(BF16)
        fars.start(k, remote(one, far_out.at[k], far_sems, k, "hid", at.far))

    def input_grad(owner):
        rows = rows_at(owner, t)
        return sum(nt(d_gate[i, rows, :], wg[i]) + nt(d_up[i, rows, :], wu[i]) for i in range(local))

    sums = RingSum(at, send, recv, t, sum_sems)
    done_jobs = 0

    def jobs_until(count):
        nonlocal done_jobs
        while done_jobs < count:
            job(done_jobs)
            done_jobs += 1
            if 2 <= done_jobs <= crossing + 1:
                cross(done_jobs - 2)

    sums.put(0, lambda side, owner: input_grad(owner))
    sums.go(0)
    for s in range(1, steps):
        jobs_until(len(jobs) * (2 * s - 1) // (2 * steps - 1))
        sums.put(s, lambda side, owner: input_grad(owner))
        sums.part(s, 0)
        jobs_until(min(len(jobs), done_jobs + 1))
        sums.part(s, 1)
    jobs_until(len(jobs))
    if crossing >= len(jobs):
        cross(len(jobs) - 1)
    dx[...] = input_grad(at.e)
    sums.arrive_last()
    for rows in split_parts(t):
        dx[rows, :] = dx[rows, :] + sums.total(rows)

    for k in range(len(others)):
        small.recv(k)
    own_small.wait()
    for k in range(len(jobs)):
        flights[k][0].wait_recv()
        if k >= crossing:
            flights[k][1].wait_recv()
    for k in range(len(jobs) - 2, len(jobs)):
        for copy in flights[k]:
            copy.wait_send()
        for copy in kept[k]:
            copy.wait()
    for k in range(crossing):
        fars.recv(k)
    for group in (x_ring, c_ring, downs, small, sums, fars):
        group.done()


def back_kernel(
    dims, big,
    dx, gate_grad, gates, kept, resid, normed_two, g_all, x, ws_in, qkv_in, mixed_in, normed_in, cosine_in, sine_in, probs_in,
    y_all, own_in, sib_in,
    layer, in_grad, small_one, small_two, att_grad, far_rest,
    ws, qkv, mixed, normed, cosine, sine, probs, x_own, g_own, resid_grad, rows_all, mixed_grad, d_query, d_key, d_value,
    d_qkv, w_grad, part, came, mid, came_far, y_rows, y_send, y_recv, w_send, w_recv, out_rows, in_rows, sum_a,
    cut_send, cut_recv, rest,
    row_sems, y_sems, w_sems, hid_sems, in_sems, layer_sems, small_sems, cut_sems, far_sems, local_sems, load_sems,
):
    at = Place(dims.n)
    n, t, d, kv, shard = dims.n, dims.quarter, dims.d, dims.kc, dims.shard
    q4 = d // 4
    others = tuple((at.e + k) % n for k in range(1, n))
    pairs = [
        (ws_in, ws), (g_all.at[at.e], g_own), (own_in, rest.at[0]), (sib_in, rest.at[1]), (qkv_in, qkv),
        (mixed_in, mixed), (normed_in, normed), (cosine_in, cosine), (sine_in, sine), (x.at[rows_at(at.h, t)], x_own),
    ]
    if not big:
        pairs.append((y_all, y_rows))
    loads = [local_start(src, dst, load_sems.at[k]) for k, (src, dst) in enumerate(pairs)]
    for j in range(4):
        span = pl.ds(0, (j + 1) * t)
        loads.append(local_start(probs_in.at[j, :, span], probs.at[j, :, span], load_sems.at[11 + j]))
    greet(others, (at.sib, at.far, at.diag))
    loads[0].wait()
    loads[1].wait()

    slab = ws[:, dims.slab_at :]
    gains = gain_rows(slab, dims.experts)
    spread_shape = (n * 8, LANES)
    sub, lane = iota(spread_shape, 0), iota(spread_shape, 1)
    spread = (
        (sub // 8 == lane // dims.local) & (sub % 8 == lane % dims.local) & (lane < dims.experts)
    ).astype(F32)
    gg = tn_exact(gate_grad[...], spread) * kept[...]
    gate = gates[...]
    logit_grad = (gate * (gg - jnp.sum(gate * gg, axis=1, keepdims=True))).astype(BF16)
    gain_two = jnp.zeros((1, d), F32)
    rows = Sent()
    for c, half in enumerate(split_parts(t)):
        lg = logit_grad[half.start : half.start + half.size, :]
        normed_grad = dx[half, :] + nt(lg, slab)
        inputs = resid[half, :]
        scale = rms(inputs)
        gain_two = gain_two + jnp.sum(normed_grad * inputs * scale, axis=0, keepdims=True)
        weighted = normed_grad * gains[1:2, :]
        value = (
            g_own[half, :].astype(F32) + scale * weighted
            - inputs * (scale * scale * scale) * jnp.mean(weighted * inputs, axis=-1, keepdims=True)
        )
        resid_grad[half, :] = value
        here = pl.ds(pl.multiple_of(at.h * t + half.start, 16), half.size)
        rows_all[here, :] = value.astype(BF16)
        rows.start(("far", c), remote(rows_all.at[here], rows_all.at[here], row_sems, c, "hid", at.far))
        rows.start(("sib", c), remote(rows_all.at[here], rows_all.at[here], row_sems, 2 + c, "hid", at.sib))

    for load in loads[2:]:
        load.wait()
    router_rows = dims.experts
    small_rows = router_rows + 8
    router_part = tn(logit_grad, normed_two[...])
    for owner in range(n):
        cols = slice(owner * shard, (owner + 1) * shard)
        cut_send[owner, :router_rows] = router_part[:router_rows, cols]
        cut_send[owner, router_rows:small_rows] = jnp.broadcast_to(gain_two[:, cols], (8, shard))

    def add_rest(k, _):
        rest[0, k] = (rest[0, k].astype(F32) + rest[1, k].astype(F32)).astype(BF16)
        return 0

    lax.fori_loop(0, dims.jobs - dims.crossing, add_rest, 0)

    y_sum = RingSum(at, y_send, y_recv, t, y_sems)

    def y_row(owner):
        if not big:
            return y_rows.at[owner]
        local_start(y_all.at[owner], y_rows.at[0], local_sems.at[5]).wait()
        return y_rows.at[0]

    def y_step(s):
        y_sum.put(s, lambda side, owner: y_row(owner)[...].astype(F32))
        y_sum.go(s)

    y_step(0)
    wo = ws.at[:, pl.ds(dims.attn_cols, dims.qc)]

    def project(quarter):
        block = rows_at(quarter, t)
        mixed_grad[block, :] = nn(rows_all[block, :], wo[...]).astype(BF16)

    project(at.h)
    rows.recv(("sib", 0))
    rows.recv(("sib", 1))
    project(at.sib)
    for c in (0, 1):
        rows.recv(("far", c))
        here = pl.ds(pl.multiple_of(at.far * t + c * (t // 2), 16), t // 2)
        rows.start(("on", c), remote(rows_all.at[here], rows_all.at[here], row_sems, 4 + c, "hid", at.sib))
    project(at.far)
    fars = Sent()
    count = dims.jobs - dims.crossing

    def send_rest(k):
        fars.start(k, remote(rest.at[0, k], far_rest.at[k], far_sems, k, "hid", at.far))

    for k in range(count // 2):
        send_rest(k)
    rows.recv(("on", 0))
    rows.recv(("on", 1))
    project(at.diag)
    y_step(1)

    d_key[...] = jnp.zeros_like(d_key)
    d_value[...] = jnp.zeros_like(d_value)
    cuts = Sent()
    y_at = 2
    for j in range(4):
        block = pl.ds(j * t, t)
        keys = (j + 1) * t
        for head in range(dims.heads):
            key_at = head // dims.group * HEAD_DIM
            spot = slice(key_at, key_at + HEAD_DIM)
            query = qkv[block, head * HEAD_DIM : (head + 1) * HEAD_DIM]
            key = qkv[:keys, dims.qc + key_at : dims.qc + key_at + HEAD_DIM]
            value = qkv[:keys, dims.qc + kv + key_at : dims.qc + kv + key_at + HEAD_DIM]
            out_grad = mixed_grad[block, head * HEAD_DIM : (head + 1) * HEAD_DIM]
            share = probs[j, head, :keys, :]
            exact = share.astype(F32)
            prob_grad = nt(value, out_grad)
            inner = jnp.sum(exact * prob_grad, axis=0, keepdims=True)
            score_grad = (exact * (prob_grad - inner)).astype(BF16)
            d_query[block, head * HEAD_DIM : (head + 1) * HEAD_DIM] = tn(score_grad, key) * HEAD_DIM**-0.5
            d_key[:keys, spot] += nn(score_grad, query)
            d_value[:keys, spot] += nn(share, out_grad)
    early = pl.ds(0, small_rows)
    for k, peer in enumerate(others):
        cuts.start(k, remote(cut_send.at[peer, early], cut_recv.at[at.e, early], cut_sems, k, "exp", peer))
    own_cut = local_start(cut_send.at[at.e, early], cut_recv.at[at.e, early], local_sems.at[0])

    repeat = (dims.qc + kv) // LANES
    sums = Sent()
    for k, quarter in enumerate((at.diag, at.far, at.sib, at.h)):
        block = rows_at(quarter, t)
        raw = jnp.concatenate([d_query[block, :], d_key[block, :]], axis=1)
        turned = raw * jnp.tile(cosine[block, :], (1, repeat)) - swap_halves(raw) * jnp.tile(
            sine[block, :], (1, repeat)
        )
        d_qkv[block, : dims.qc + kv] = turned.astype(BF16)
        d_qkv[block, dims.qc + kv :] = d_value[block, :].astype(BF16)
        part[quarter] = nt(d_qkv[block, :], ws[:, : dims.attn_cols]).astype(BF16)
        if k == 0:
            sums.start(0, remote(part.at[at.diag], came.at[1], hid_sems, 0, "hid", at.sib))
        if k == 1:
            sums.recv(0)
            for c, half in enumerate(split_parts(t)):
                mid[half, :] = (part[at.far, half].astype(F32) + came[1, half].astype(F32)).astype(BF16)
                sums.start(2 + c, remote(mid.at[half], came_far.at[half], hid_sems, 2 + c, "hid", at.far))
        if k == 2:
            sums.start(1, remote(part.at[at.sib], came.at[0], hid_sems, 1, "hid", at.sib))

    def weight_cols(c, _):
        cols = rows_at(c, 256)
        w_grad[cols, : dims.attn_cols] = tn(normed[:, cols], d_qkv[...])
        w_grad[cols, dims.attn_cols :] = tn(rows_all[:, cols], mixed[...])
        return 0

    lax.fori_loop(0, d // 256, weight_cols, 0)
    w_sum = RingSum(at, w_send, w_recv, shard, w_sems)

    def w_step(s):
        w_sum.put(s, lambda side, owner: w_grad[rows_at(owner, shard), :])
        w_sum.go(s)

    w_step(0)
    if y_at < dims.steps:
        y_step(y_at)
        y_at += 1
    sums.recv(1)
    gain_one = jnp.zeros((1, d), F32)
    ins = Sent()
    own_rows = []
    for c, half in enumerate(split_parts(t)):
        sums.recv(2 + c)
        grad = part[at.h, half].astype(F32) + came[0, half].astype(F32) + came_far[half].astype(F32)
        inputs = x_own[half, :].astype(F32)
        scale = rms(inputs)
        gain_one = gain_one + jnp.sum(grad * inputs * scale, axis=0, keepdims=True)
        weighted = grad * gains[0:1, :]
        in_rows[half, :] = (
            resid_grad[half, :] + scale * weighted
            - inputs * (scale * scale * scale) * jnp.mean(weighted * inputs, axis=-1, keepdims=True)
        ).astype(BF16)
        spot = in_grad.at[pl.ds(pl.multiple_of(at.h * t + half.start, 16), half.size)]
        ins.start(("far", c), remote(in_rows.at[half], spot, in_sems, c, "hid", at.far))
        ins.start(("sib", c), remote(in_rows.at[half], spot, in_sems, 2 + c, "hid", at.sib))
        own_rows.append(local_start(in_rows.at[half], spot, local_sems.at[1 + c]))
    for owner in range(n):
        cols = slice(owner * shard, (owner + 1) * shard)
        cut_send[owner, small_rows:] = jnp.broadcast_to(gain_one[:, cols], (8, shard))
    late = pl.ds(small_rows, 8)
    for k, peer in enumerate(others):
        cuts.start(
            n + k, remote(cut_send.at[peer, late], cut_recv.at[at.e, late], cut_sems, n - 1 + k, "exp", peer)
        )
    own_cut_two = local_start(cut_send.at[at.e, late], cut_recv.at[at.e, late], local_sems.at[4])
    for k in range(count // 2, count):
        send_rest(k)
    w_at = 1
    if w_at < dims.steps:
        w_step(w_at)
        w_at += 1
    for k in range(n - 1):
        cuts.recv(k)
        cuts.recv(n + k)
    own_cut.wait()
    own_cut_two.wait()
    total = cut_recv[0]
    for k in range(1, n):
        total = total + cut_recv[k]
    sum_a[0] = total
    smalls = Sent()
    smalls.start(0, remote(sum_a.at[0], sum_a.at[1], small_sems, 0, "hid", at.sib))
    for c in (0, 1):
        ins.recv(("far", c))
        far_rows = in_grad.at[pl.ds(pl.multiple_of(at.far * t + c * (t // 2), 16), t // 2)]
        ins.start(("on", c), remote(far_rows, far_rows, in_sems, 4 + c, "hid", at.sib))
    smalls.recv(0)
    sum_a[2] = sum_a[0] + sum_a[1]
    smalls.start(1, remote(sum_a.at[2], sum_a.at[3], small_sems, 1, "hid", at.far))
    while y_at < dims.steps:
        y_step(y_at)
        y_at += 1
    while w_at < dims.steps:
        w_step(w_at)
        w_at += 1
    y_sum.arrive_last()
    y_own = y_row(at.e)
    for half in split_parts(t):
        out_rows[half, :] = (resid[half, :] + y_own[half].astype(F32) + y_sum.total(half)).astype(BF16)
    layers = Sent()
    for k, peer in enumerate((at.far, at.diag, at.sib)):
        layers.start(
            k, remote(out_rows.at[:, rows_at(peer, q4)], layer.at[rows_at(at.h, t)], layer_sems, k, "hid", peer)
        )
    own_layer = local_start(out_rows.at[:, rows_at(at.h, q4)], layer.at[rows_at(at.h, t)], local_sems.at[3])
    w_sum.arrive_last()
    for rows_part in split_parts(shard):
        here = pl.ds(pl.multiple_of(at.e * shard + rows_part.start, 16), rows_part.size)
        att_grad[rows_part, :] = w_grad[here, :] + w_sum.total(rows_part)
    smalls.recv(1)
    total = sum_a[2] + sum_a[3]
    small_one[...] = total[:small_rows]
    small_two[...] = total[small_rows:]

    for k in range(count):
        fars.recv(k)
    for k in range(3):
        layers.recv(k)
    for c in (0, 1):
        ins.recv(("sib", c))
        ins.recv(("on", c))
        own_rows[c].wait()
    own_layer.wait()
    for group in (rows, smalls, y_sum, fars, cuts, sums, w_sum, ins, layers):
        group.done()


def out_kernel(
    dims,
    layer_in, in_rows, small_one, small_two, att, own_d, own_g, own_u, sib_d, sib_g, sib_u, far_d, far_g, far_g_rest, far_u,
    layer, in_grad, gain_one, gain_two, wq, wk, wv, wo, router, gate, up, down,
):
    layer[...] = layer_in[...]
    in_grad[...] = in_rows[...].astype(F32)

    def three(own, sib, far):
        return own[0].astype(F32) + sib[0].astype(F32) + far.astype(F32)

    first = pl.program_id(0) < dims.crossing - dims.local
    down[0] = three(own_d, sib_d, far_d[0])
    gate[0] = three(own_g, sib_g, jnp.where(first, far_g[0], far_g_rest[0])).T
    up[0] = three(own_u, sib_u, far_u[0]).T

    @pl.when(pl.program_id(0) == 0)
    def _():
        gain_one[...] = small_two[:1, :]
        gain_two[...] = small_one[dims.experts : dims.experts + 1, :]
        router[...] = small_one[: dims.experts, :]
        qc, kc = dims.qc, dims.kc
        wq[...] = att[:, :qc]
        wk[...] = att[:, qc : qc + kc]
        wv[...] = att[:, qc + kc : qc + 2 * kc]
        wo[...] = att[:, dims.attn_cols :]


def per_device(
    tokens,
    segment_ids,
    routes,
    norm1_gain,
    norm2_gain,
    query_weight,
    key_matrix,
    value_matrix,
    out_weight,
    router_weight,
    gate_weight,
    up_weight,
    down_weight,
    out_grad,
):
    n = lax.axis_size("exp")
    assert lax.axis_size("hid") == 4
    token_count, d = tokens.shape
    local, _, part_ff = gate_weight.shape
    experts = router_weight.shape[1]
    dims = Dims(
        n, token_count, d, experts, local, 4 * part_ff, routes.shape[1], query_weight.shape[1], key_matrix.shape[1]
    )
    t, ff, steps, shard = dims.quarter, dims.ff, dims.steps, dims.shard
    qc, kc = dims.qc, dims.kc

    vmem = pl.BlockSpec(memory_space=pltpu.VMEM)
    anywhere = pl.BlockSpec(memory_space=pl.ANY)
    shape = jax.ShapeDtypeStruct
    dma = pltpu.SemaphoreType.DMA

    (
        ws_all, wg_all, wd_all, wu_cast, g_all, probs, normed, qkv, mixed, cosine, sine, resid, normed_two, coef, gates, kept,
    ) = pl.pallas_call(
        functools.partial(front_kernel, dims),
        out_shape=[
            shape((d, dims.ws_cols), BF16),
            shape((local, d, ff), BF16),
            shape((local, ff, d), BF16),
            shape((local, d, part_ff), BF16),
            shape((n, t, d), BF16),
            shape((4, dims.heads, token_count, t), BF16),
            shape((token_count, d), BF16),
            shape((token_count, dims.attn_cols), BF16),
            shape((token_count, qc), BF16),
            shape((token_count, LANES), F32),
            shape((token_count, LANES), F32),
            shape((t, d), F32),
            shape((t, d), BF16),
            shape((experts, t), F32),
            shape((t, LANES), F32),
            shape((t, LANES), F32),
        ],
        in_specs=[vmem] * 10 + [anywhere] * 4,
        out_specs=[anywhere] * 6 + [vmem] * 10,
        scratch_shapes=[
            pltpu.VMEM((d, dims.ws_cols), BF16),
            pltpu.VMEM((2, local, d, part_ff), F32),
            pltpu.VMEM((2, local, d, part_ff), BF16),
            pltpu.VMEM((local, part_ff, d), F32),
            pltpu.VMEM((local, part_ff, d), BF16),
            pltpu.VMEM((8, token_count), jnp.int32),
            pltpu.VMEM((4, dims.heads, token_count, t), BF16),
            pltpu.VMEM((4, t, d), BF16),
            pltpu.VMEM((2, t, d), BF16),
            pltpu.VMEM((t, d), BF16),
            pltpu.VMEM((t, d), BF16),
            dma((2, 4 * steps)),
            dma((2, 4 * steps)),
            dma((2, 4)),
            dma((2, 3)),
            dma((2, 3 * dims.early)),
            dma((8,)),
            dma((4,)),
            dma((dims.early,)),
        ],
        compiler_params=pltpu.CompilerParams(
            collective_id=0, has_side_effects=True, vmem_limit_bytes=VMEM_LIMIT
        ),
    )(
        tokens, segment_ids, routes.T, query_weight, key_matrix, value_matrix, out_weight, router_weight.T,
        norm1_gain[None, :], norm2_gain[None, :], out_grad, gate_weight, up_weight, down_weight,
    )

    big = n * t * d * 2 > 6 * 2**20
    jobs, crossing = dims.jobs, dims.crossing
    (dx, y_all, gate_grad, own, sib, own_rest, sib_rest, far, _) = pl.pallas_call(
        functools.partial(moe_kernel, dims, big),
        out_shape=[
            shape((t, d), F32),
            shape((n, t, d), BF16),
            shape((n, 8, t), F32),
            shape((jobs, part_ff, d), BF16),
            shape((jobs, part_ff, d), BF16),
            shape((jobs - crossing, part_ff, d), BF16),
            shape((jobs - crossing, part_ff, d), BF16),
            shape((crossing, part_ff, d), BF16),
            shape((n * t if big else 16, d), BF16),
        ],
        in_specs=[vmem, vmem] + [anywhere] * 4,
        out_specs=[vmem] + [anywhere] * 8,
        scratch_shapes=[
            pltpu.VMEM((16 if big else n * t, d), BF16),
            pltpu.VMEM((1, 16, d) if big else (n, t, d), BF16),
            pltpu.VMEM((n, experts, t), F32),
            pltpu.VMEM((local, d, ff), BF16),
            pltpu.VMEM((local, d, ff), BF16),
            pltpu.VMEM((local, ff, d), BF16),
            pltpu.VMEM((local, n * t, ff), BF16),
            pltpu.VMEM((local, n * t, ff), BF16),
            pltpu.VMEM((local, n * t, ff), BF16),
            pltpu.VMEM((2, 2, t, d), BF16),
            pltpu.VMEM((2, steps, t, d), BF16),
            pltpu.VMEM((n, 8, t), F32),
            pltpu.VMEM((2, max(ff, t), d), BF16),
            pltpu.VMEM((t, d) if big else (16, LANES), BF16),
            pltpu.VMEM((t, d) if big else (16, LANES), BF16),
            dma((2, 4 * steps)),
            dma((2, 4 * steps)),
            dma((2, 4 * steps)),
            dma((2, n - 1)),
            dma((2, 3 * local)),
            dma((2, 2 * jobs)),
            dma((2, crossing)),
            dma((6,)),
            dma((4,)),
            dma((2,)),
            dma((local,)),
            pltpu.SemaphoreType.REGULAR,
        ],
        compiler_params=pltpu.CompilerParams(
            collective_id=1, has_side_effects=True, vmem_limit_bytes=VMEM_LIMIT
        ),
    )(normed_two, coef, g_all, wg_all, wd_all, wu_cast)

    small_rows = experts + 8
    att = dims.attn_cols + qc
    (layer, in_rows, small_one, small_two, att_grad, far_rest) = pl.pallas_call(
        functools.partial(back_kernel, dims, big),
        out_shape=[
            shape((token_count, d // 4), BF16),
            shape((token_count, d), BF16),
            shape((small_rows, shard), F32),
            shape((8, shard), F32),
            shape((shard, att), F32),
            shape((jobs - crossing, part_ff, d), BF16),
        ],
        in_specs=[vmem] * 6 + [anywhere] * 12,
        out_specs=[anywhere] * 2 + [vmem] * 3 + [anywhere],
        scratch_shapes=[
            pltpu.VMEM((d, dims.ws_cols), BF16),
            pltpu.VMEM((token_count, dims.attn_cols), BF16),
            pltpu.VMEM((token_count, qc), BF16),
            pltpu.VMEM((token_count, d), BF16),
            pltpu.VMEM((token_count, LANES), F32),
            pltpu.VMEM((token_count, LANES), F32),
            pltpu.VMEM((4, dims.heads, token_count, t), BF16),
            pltpu.VMEM((t, d), BF16),
            pltpu.VMEM((t, d), BF16),
            pltpu.VMEM((t, d), F32),
            pltpu.VMEM((token_count, d), BF16),
            pltpu.VMEM((token_count, qc), BF16),
            pltpu.VMEM((token_count, qc), F32),
            pltpu.VMEM((token_count, kc), F32),
            pltpu.VMEM((token_count, kc), F32),
            pltpu.VMEM((token_count, dims.attn_cols), BF16),
            pltpu.VMEM((d, att), F32),
            pltpu.VMEM((4, t, d), BF16),
            pltpu.VMEM((2, t, d), BF16),
            pltpu.VMEM((t, d), BF16),
            pltpu.VMEM((t, d), BF16),
            pltpu.VMEM((1 if big else n, t, d), BF16),
            pltpu.VMEM((2, 2, t, d), BF16),
            pltpu.VMEM((2, steps, t, d), BF16),
            pltpu.VMEM((2, 2, shard, att), BF16),
            pltpu.VMEM((2, steps, shard, att), BF16),
            pltpu.VMEM((t, d), BF16),
            pltpu.VMEM((t, d), BF16),
            pltpu.VMEM((4, small_rows + 8, shard), F32),
            pltpu.VMEM((n, small_rows + 8, shard), F32),
            pltpu.VMEM((n, small_rows + 8, shard), F32),
            pltpu.VMEM((2, jobs - crossing, part_ff, d), BF16),
            dma((2, 6)),
            dma((2, 4 * steps)),
            dma((2, 4 * steps)),
            dma((2, 4)),
            dma((2, 6)),
            dma((2, 3)),
            dma((2, 2)),
            dma((2, 2 * (n - 1))),
            dma((2, jobs - crossing)),
            dma((6,)),
            dma((15,)),
        ],
        compiler_params=pltpu.CompilerParams(
            collective_id=2, has_side_effects=True, vmem_limit_bytes=VMEM_LIMIT
        ),
    )(
        dx, gate_grad.reshape(n * 8, t), gates, kept, resid, normed_two, g_all, tokens, ws_all, qkv, mixed, normed, cosine, sine,
        probs, y_all, own_rest, sib_rest,
    )

    rows = token_count // local

    def whole(shape_):
        return pl.BlockSpec(shape_, lambda i: (0,) * len(shape_))

    def matrix(index):
        return pl.BlockSpec((1, part_ff, d), lambda i: (index(i), 0, 0))

    (
        layer, in_grad, gain_one, gain_two, wq, wk, wv, wo, router, gate, up, down,
    ) = pl.pallas_call(
        functools.partial(out_kernel, dims),
        grid=(local,),
        out_shape=[
            shape((token_count, d // 4), BF16),
            shape((token_count, d), F32),
            shape((1, shard), F32),
            shape((1, shard), F32),
            shape((shard, qc), F32),
            shape((shard, kc), F32),
            shape((shard, kc), F32),
            shape((shard, qc), F32),
            shape((experts, shard), F32),
            shape((local, d, part_ff), F32),
            shape((local, d, part_ff), F32),
            shape((local, part_ff, d), F32),
        ],
        in_specs=[
            pl.BlockSpec((rows, d // 4), lambda i: (i, 0)),
            pl.BlockSpec((rows, d), lambda i: (i, 0)),
            whole((small_rows, shard)),
            whole((8, shard)),
            whole((shard, att)),
            matrix(lambda i: i),
            matrix(lambda i: local + i),
            matrix(lambda i: 2 * local + i),
            matrix(lambda i: i),
            matrix(lambda i: local + i),
            matrix(lambda i: 2 * local + i),
            matrix(lambda i: i),
            matrix(lambda i: jnp.minimum(local + i, crossing - 1)),
            matrix(lambda i: jnp.maximum(local + i - crossing, 0)),
            matrix(lambda i: 2 * local + i - crossing),
        ],
        out_specs=[
            pl.BlockSpec((rows, d // 4), lambda i: (i, 0)),
            pl.BlockSpec((rows, d), lambda i: (i, 0)),
            whole((1, shard)),
            whole((1, shard)),
            whole((shard, qc)),
            whole((shard, kc)),
            whole((shard, kc)),
            whole((shard, qc)),
            whole((experts, shard)),
            pl.BlockSpec((1, d, part_ff), lambda i: (i, 0, 0)),
            pl.BlockSpec((1, d, part_ff), lambda i: (i, 0, 0)),
            pl.BlockSpec((1, part_ff, d), lambda i: (i, 0, 0)),
        ],
        compiler_params=pltpu.CompilerParams(vmem_limit_bytes=VMEM_LIMIT),
    )(layer, in_rows, small_one, small_two, att_grad, own, own, own, sib, sib, sib, far, far, far_rest, far_rest)

    return (layer, in_grad, gain_one[0], gain_two[0], wq, wk, wv, wo, router.T, gate, up, down)


def solution(mesh):
    in_specs = (
        P("exp", None),
        P("exp", None),
        P("exp", None),
        P("exp"),
        P("exp"),
        P("exp", "hid"),
        P("exp", "hid"),
        P("exp", "hid"),
        P("exp", "hid"),
        P("exp", None),
        P("exp", None, "hid"),
        P("exp", None, "hid"),
        P("exp", "hid", None),
        P("exp", "hid"),
    )
    out_specs = (
        P("exp", "hid"),
        P("exp", None),
        P("exp"),
        P("exp"),
        P("exp", "hid"),
        P("exp", "hid"),
        P("exp", "hid"),
        P("exp", "hid"),
        P("exp", None),
        P("exp", None, "hid"),
        P("exp", None, "hid"),
        P("exp", "hid", None),
    )
    return jax.shard_map(
        per_device, mesh=mesh, in_specs=in_specs, out_specs=out_specs, check_vma=False
    )
```
